32 devices in a mesh: dom: 4 (over y, core), event: 8 (over z, x).
Axes of the slice: x: 2, y: 2, z: 4, core: 2. Of those that a mesh axis runs over, the one named last changes fastest.
Arguments:
- adjoint_state: float32 [8, 9, 64, 3072], P('event', None, None, 'dom'), may hold values from -6 to 6
- forward_velocity: float32 [8, 3, 3, 64, 3072], P('event', None, None, None, 'dom'), may hold values from -6 to 6
- density: float32 [64, 3072], P(None, 'dom'), may hold values from 1 to 3
- lame_lambda: float32 [64, 3072], P(None, 'dom'), may hold values from 0.5 to 2
- shear_modulus: float32 [64, 3072], P(None, 'dom'), may hold values from 0.5 to 2
- neighbour: int32 [6, 3072], P(None, 'dom'), may hold values from -1 to 1647, as said below
- send_list: int32 [2, 1760], P(None, 'dom'), may hold values from -1 to 4607, as said below
Outputs:
- adjoint_velocity: float32 [8, 3, 64, 3072], P('event', None, None, 'dom')
- kernels: float32 [3, 4, 49152], P(None, 'dom', 'event')
The draws below stay inside these ranges and needn't reach their ends.
Inputs may be any that keep to these rules, and one draw needn't show every extreme that they name: `neighbour`: codes 0 to 767 name a slot of the same block, and then that slot's face f xor 1 names this face back; a code 768 + j names position j of row 1 of block b - 1 in send_list, a code 768 + 440 + j position j of row 0 of block b + 1, and such a position holds the partner face; -1 marks outer faces and every face of an unused slot. Every used slot has at least one face with a code other than -1; the used slots of a block come first. In every draw some block uses all 768 slots. `send_list`: positions b * 440 to (b + 1) * 440 - 1 belong to block b: row 0 lists the faces of b whose partner lies in block b - 1, row 1 those whose partner lies in block b + 1, each as f * 768 + s, used positions first and -1 after them. In every draw some block fills all 440 positions of row 0 and some block all 440 of row 1.
All inputs are finite; a program needn't handle non-finite values.
Results may differ from the reference program's by a relative error of at most 0.0001.
Values sent between devices are 32-bit elements; how exact they have to be, the bound alone decides.
No kernel may reach another device: no remote copies, remote signals or barrier semaphores. Data moves between devices by JAX's collectives and lax.ppermute only.
A program may use at most 128 MiB of HBM per device.

```python
import math
import jax
import jax.numpy as jnp
import numpy as np
from jax import lax

GY = 12
GZ = 8
SLAB = 6
SHIFT = 1
NODES = 64
STEPS = 3
E_DEV = 768
E_TOTAL = 3072
CAP = 440
EVENTS = 8
N_DOM = 4


def build_mesh(key):
    columns = GY * GZ
    extent = N_DOM * SLAB
    slot_count = E_DEV
    key_shift, key_chosen, key_pattern, key_order, key_phase = jax.random.split(key, 5)
    drawn_shift = jax.random.randint(key_shift, (N_DOM + 1, columns), -SHIFT, SHIFT + 1).astype(jnp.int32)
    block_ids = jnp.arange(N_DOM + 1, dtype=jnp.int32)[:, None]
    column_ids = jnp.arange(columns, dtype=jnp.int32)
    phase = jax.random.randint(key_phase, (), 0, 2).astype(jnp.int32) * 2 - 1
    checker = ((column_ids // GZ + column_ids % GZ) % 2 * 2 - 1) * phase
    chosen = jax.random.randint(key_chosen, (), 1, N_DOM - 1).astype(jnp.int32)
    patterned = jax.random.randint(key_pattern, (), 1, N_DOM - 2).astype(jnp.int32)
    patterned = jnp.where(patterned >= chosen, patterned + 2, patterned)
    cuts = block_ids * SLAB + drawn_shift
    cuts = jnp.where(block_ids == chosen, block_ids * SLAB - SHIFT, cuts)
    cuts = jnp.where(block_ids == chosen + 1, block_ids * SLAB + SHIFT, cuts)
    cuts = jnp.where(block_ids == patterned, block_ids * SLAB + SHIFT * checker[None, :], cuts)
    cuts = jnp.where(block_ids == 0, 0, cuts)
    cuts = jnp.where(block_ids == N_DOM, extent, cuts).astype(jnp.int32)
    thickness = cuts[1:] - cuts[:-1]
    column_order = jax.random.permutation(key_order, columns).astype(jnp.int32)
    ordered = thickness[:, column_order]
    ordered_starts = jnp.cumsum(ordered, axis=1) - ordered
    starts = jnp.zeros_like(thickness).at[:, column_order].set(ordered_starts)
    layer_ids = jnp.arange(extent, dtype=jnp.int32)[:, None]
    owner = jnp.sum((cuts[1:N_DOM][None, :, :] <= layer_ids[:, None, :]).astype(jnp.int32), axis=1)
    owner_cut = cuts[owner, column_ids[None, :]]
    slot_index = starts[owner, column_ids[None, :]] + layer_ids - owner_cut
    steps_x = jnp.array([-1, 1, 0, 0, 0, 0], jnp.int32)[:, None, None]
    steps_y = jnp.array([0, 0, -1, 1, 0, 0], jnp.int32)[:, None, None]
    steps_z = jnp.array([0, 0, 0, 0, -1, 1], jnp.int32)[:, None, None]
    near_x = layer_ids[None] + steps_x
    near_y = (column_ids // GZ)[None, None, :] + steps_y
    near_z = (column_ids % GZ)[None, None, :] + steps_z
    inside = (near_x >= 0) & (near_x < extent) & (near_y >= 0) & (near_y < GY) & (near_z >= 0) & (near_z < GZ)
    clip_x = jnp.clip(near_x, 0, extent - 1)
    near_column = jnp.clip(near_y, 0, GY - 1) * GZ + jnp.clip(near_z, 0, GZ - 1)
    full_shape = (6, extent, columns)
    near_owner = jnp.broadcast_to(owner[clip_x, near_column], full_shape)
    near_slot = jnp.broadcast_to(slot_index[clip_x, near_column], full_shape)
    inside = jnp.broadcast_to(inside, full_shape)
    own_owner = jnp.broadcast_to(owner[None], full_shape)
    own_slot = jnp.broadcast_to(slot_index[None], full_shape)
    face_ids = jnp.broadcast_to(jnp.arange(6, dtype=jnp.int32)[:, None, None], full_shape)
    to_lower = (inside & (near_owner == own_owner - 1)).astype(jnp.int32)
    to_upper = (inside & (near_owner == own_owner + 1)).astype(jnp.int32)
    face_key = face_ids * slot_count + own_slot
    lower_mark = jnp.zeros((N_DOM, 6 * slot_count), jnp.int32).at[own_owner, face_key].add(to_lower)
    upper_mark = jnp.zeros((N_DOM, 6 * slot_count), jnp.int32).at[own_owner, face_key].add(to_upper)
    lower_rank = jnp.cumsum(lower_mark, axis=1) - lower_mark
    upper_rank = jnp.cumsum(upper_mark, axis=1) - upper_mark
    mark_blocks = jnp.broadcast_to(jnp.arange(N_DOM, dtype=jnp.int32)[:, None], (N_DOM, 6 * slot_count))
    key_values = jnp.broadcast_to(jnp.arange(6 * slot_count, dtype=jnp.int32)[None, :], (N_DOM, 6 * slot_count))
    lower_target = jnp.where(lower_mark > 0, lower_rank, CAP)
    upper_target = jnp.where(upper_mark > 0, upper_rank, CAP)
    lower_list = jnp.full((N_DOM, CAP + 1), -1, jnp.int32).at[mark_blocks, lower_target].set(jnp.where(lower_mark > 0, key_values, -1))[:, :CAP]
    upper_list = jnp.full((N_DOM, CAP + 1), -1, jnp.int32).at[mark_blocks, upper_target].set(jnp.where(upper_mark > 0, key_values, -1))[:, :CAP]
    send_list = jnp.stack([lower_list.reshape(-1), upper_list.reshape(-1)])
    swapped_key = (face_ids ^ 1) * slot_count + near_slot
    code_lower = slot_count + upper_rank[near_owner, swapped_key]
    code_upper = slot_count + CAP + lower_rank[near_owner, swapped_key]
    code = jnp.where(near_owner == own_owner, near_slot, jnp.where(near_owner == own_owner - 1, code_lower, code_upper))
    code = jnp.where(inside, code, -1).astype(jnp.int32)
    neighbour = jnp.full((6, N_DOM * slot_count), -1, jnp.int32).at[face_ids, own_owner * slot_count + own_slot].set(code)
    return (neighbour, send_list)


def draw_neighbour(key, part):
    return build_mesh(jax.random.fold_in(key, 11))[0]


def draw_send_list(key, part):
    return build_mesh(jax.random.fold_in(key, 11))[1]


def shard_levels(rng, shape, cuts, smallest, largest):
    def one(dim, blocks):
        heights = jax.random.uniform(jax.random.fold_in(jax.random.fold_in(rng, 6), dim), (blocks,), jnp.float32, smallest / len(cuts), largest / len(cuts))
        return jnp.repeat(jnp.exp(heights), shape[dim] // blocks).reshape((-1,) + (1,) * (len(shape) - dim - 1))

    loudness = one(*cuts[0])
    for cut in cuts[1:]:
        loudness = loudness * one(*cut)
    return loudness


def scatter_about(rng, shape, scale, most, shards=(), kind=jnp.bfloat16):
    factor_of = shard_levels(rng, shape, shards, -0.22, 0.18) if shards else 1.0
    drawn = jax.random.normal(rng, shape, jnp.float32) * scale * factor_of
    return jnp.minimum(jnp.maximum(drawn, -most), most).astype(kind)


def setup_inputs(seed: int = 0) -> dict:
    arg_keys = jax.random.split(jax.random.key(seed), 8)
    adjoint_state = scatter_about(arg_keys[0], (EVENTS, 9, NODES, E_TOTAL), 1.0, 6.0, ((0, 8), (3, 4)), jnp.float32)
    forward_velocity = scatter_about(arg_keys[1], (EVENTS, STEPS, 3, NODES, E_TOTAL), 1.0, 6.0, ((0, 8), (4, 4)), jnp.float32)
    density = jnp.clip(jnp.exp(math.log(3.0) - 1.0986123 * jax.random.uniform(arg_keys[2], (NODES, E_TOTAL), jnp.float32) ** shard_levels(arg_keys[2], (NODES, E_TOTAL), ((1, 4),), -0.2, 0.2)), 1.0, 3.0)
    lame_lambda = jnp.clip(jnp.exp(math.log(2.0) - 1.3862944 * jax.random.uniform(arg_keys[3], (NODES, E_TOTAL), jnp.float32) ** shard_levels(arg_keys[3], (NODES, E_TOTAL), ((1, 4),), -0.2, 0.2)), 0.5, 2.0)
    shear_modulus = jnp.clip(jnp.exp(math.log(2.0) - 1.3862944 * jax.random.uniform(arg_keys[4], (NODES, E_TOTAL), jnp.float32) ** shard_levels(arg_keys[4], (NODES, E_TOTAL), ((1, 4),), -0.2, 0.2)), 0.5, 2.0)
    neighbour = draw_neighbour(jax.random.fold_in(arg_keys[7], 71), 0)
    send_list = draw_send_list(jax.random.fold_in(arg_keys[7], 71), 0)
    return dict(adjoint_state=adjoint_state, forward_velocity=forward_velocity, density=density, lame_lambda=lame_lambda, shear_modulus=shear_modulus, neighbour=neighbour, send_list=send_list)


time_step = 0.02
lift_weight = 6.0
component_pairs = ((0, 0), (1, 1), (2, 2), (0, 1), (0, 2), (1, 2))
symmetric_index = ((0, 3, 4), (3, 1, 5), (4, 5, 2))

def lobatto_diff():
    points = [-1.0, -1.0 / math.sqrt(5.0), 1.0 / math.sqrt(5.0), 1.0]
    weights = [1.0 / math.prod([points[target] - points[other] for other in range(4) if other != target]) for target in range(4)]
    offdiag = [[0.0 if target == source else weights[source] / weights[target] / (points[target] - points[source]) for source in range(4)] for target in range(4)]
    return np.array([[-sum(offdiag[target]) if target == source else offdiag[target][source] for source in range(4)] for target in range(4)], dtype=np.float32)

def face_table():
    entries = []
    for face_node in range(16):
        first_index = face_node // 4
        second_index = face_node % 4
        layout = []
        for face_id in range(6):
            coordinates = [first_index, second_index]
            coordinates.insert(face_id // 2, 3 * (face_id % 2))
            layout.append(16 * coordinates[0] + 4 * coordinates[1] + coordinates[2])
        entries.append(layout)
    return np.array(entries, dtype=np.int32)

def normal_table():
    return np.array([[face_id % 2 * 2 - 1.0 if face_id // 2 == direction else 0.0 for face_id in range(6)] for direction in range(3)], dtype=np.float32)

def lift_table():
    nodes_of = face_table()
    return np.array([[lift_weight if nodes_of[column // 6, column % 6] == node_id else 0.0 for column in range(96)] for node_id in range(64)], dtype=np.float32)

def normal_parts():
    normals = jnp.asarray(normal_table())
    return normals[:, None, :, None]

def lift_apply(face_terms):
    matrix = jnp.asarray(lift_table())
    components = face_terms.shape[0]
    return jnp.einsum('nm,cme->cne', matrix, face_terms.reshape(components, 96, face_terms.shape[-1]), precision=lax.Precision.HIGHEST)

def stress_faces(velocity_jump, lame_face, shear_face):
    shaped = normal_parts()
    along = velocity_jump[0] * shaped[0] + velocity_jump[1] * shaped[1] + velocity_jump[2] * shaped[2]
    pieces = []
    for first, second in component_pairs:
        shear_part = shear_face * (velocity_jump[first] * shaped[second] + velocity_jump[second] * shaped[first])
        if first == second:
            pieces.append(0.5 * (lame_face * along + shear_part))
        else:
            pieces.append(0.5 * shear_part)
    return jnp.stack(pieces)

def traction_of(traces):
    shaped = normal_parts()
    return jnp.stack([traces[symmetric_index[component][0]] * shaped[0] + traces[symmetric_index[component][1]] * shaped[1] + traces[symmetric_index[component][2]] * shaped[2] for component in range(3)])

def stress_rate(gradient, lame_first, shear_mod):
    trace_sum = gradient[0, 0] + gradient[1, 1] + gradient[2, 2]
    pieces = []
    for first, second in component_pairs:
        shear_part = shear_mod * (gradient[first, second] + gradient[second, first])
        if first == second:
            pieces.append(lame_first * trace_sum + shear_part)
        else:
            pieces.append(shear_part)
    return jnp.stack(pieces)

def divergence(stress_grad):
    return jnp.stack([stress_grad[symmetric_index[component][0], 0] + stress_grad[symmetric_index[component][1], 1] + stress_grad[symmetric_index[component][2], 2] for component in range(3)])

def kernel_terms(forward, velocity, stress, forward_grad):
    rho_term = -time_step * (forward[0] * velocity[0] + forward[1] * velocity[1] + forward[2] * velocity[2])
    trace_rate = forward_grad[0, 0] + forward_grad[1, 1] + forward_grad[2, 2]
    lame_term = -time_step * trace_rate * (stress[0] + stress[1] + stress[2])
    contraction = 0.0
    for first in range(3):
        for second in range(3):
            contraction = contraction + 0.5 * (forward_grad[first, second] + forward_grad[second, first]) * stress[symmetric_index[first][second]]
    shear_term = -time_step * 2.0 * contraction
    return jnp.stack([rho_term, lame_term, shear_term])

def volume_grad(nodal_field):
    components = nodal_field.shape[0]
    width = nodal_field.shape[-1]
    cube = nodal_field.reshape(components, 4, 4, 4, width)
    matrix = jnp.asarray(lobatto_diff())
    along_x = jnp.einsum('ai,cijke->cajke', matrix, cube, precision=lax.Precision.HIGHEST)
    along_y = jnp.einsum('aj,cijke->ciake', matrix, cube, precision=lax.Precision.HIGHEST)
    along_z = jnp.einsum('ak,cijke->cijae', matrix, cube, precision=lax.Precision.HIGHEST)
    return jnp.stack([along_x, along_y, along_z], 1).reshape(components, 3, 64, width)

def plus_values(traces, partner):
    trace_cols = traces.reshape(traces.shape[0] * 16, -1)
    return jnp.take(trace_cols, partner, axis=1).reshape(traces.shape)

def run_event(event_state, forward, partner, outer_sign, valid_mask, lame_first, shear_mod, density):
    nodes_of = face_table()
    lame_face = lame_first[nodes_of]
    shear_face = shear_mod[nodes_of]
    impedance = jnp.sqrt(density[nodes_of] * (lame_face + 2.0 * shear_face))
    velocity = event_state[0:3] * valid_mask
    stress = event_state[3:9] * valid_mask
    summed = jnp.zeros((3,) + density.shape, jnp.float32)
    for step in range(STEPS):
        vel_traces = velocity[:, nodes_of]
        velocity_jump = plus_values(vel_traces, partner) - vel_traces
        vel_grad = volume_grad(velocity)
        stress = stress + time_step * (stress_rate(vel_grad, lame_first, shear_mod) + lift_apply(stress_faces(velocity_jump, lame_face, shear_face)))
        str_traces = stress[:, nodes_of]
        plus_stress = plus_values(str_traces, partner) * outer_sign
        traction_jump = traction_of(plus_stress) - traction_of(str_traces)
        vel_faces = 0.5 * traction_jump + 0.5 * impedance * velocity_jump
        velocity = velocity + time_step / density * (divergence(volume_grad(stress)) + lift_apply(vel_faces))
        summed = summed + kernel_terms(forward[step], velocity, stress, volume_grad(forward[step]))
    return (velocity, summed)

def reference(adjoint_state, forward_velocity, density, lame_lambda, shear_modulus, neighbour, send_list):
    all_slots = density.shape[1]
    slot_count = all_slots // N_DOM
    capacity = send_list.shape[1] // N_DOM
    face_ids = lax.broadcasted_iota(jnp.int32, neighbour.shape, 0)
    global_ids = lax.broadcasted_iota(jnp.int32, neighbour.shape, 1)
    block_ids = global_ids // slot_count
    own_key = face_ids * all_slots + global_ids
    same_key = (face_ids ^ 1) * all_slots + block_ids * slot_count + neighbour
    lower_block = jnp.clip(block_ids - 1, 0, N_DOM - 1)
    upper_block = jnp.clip(block_ids + 1, 0, N_DOM - 1)
    lower_entry = send_list[1, lower_block * capacity + jnp.clip(neighbour - slot_count, 0, capacity - 1)]
    upper_entry = send_list[0, upper_block * capacity + jnp.clip(neighbour - slot_count - capacity, 0, capacity - 1)]
    lower_key = lower_entry // slot_count * all_slots + lower_block * slot_count + lower_entry % slot_count
    upper_key = upper_entry // slot_count * all_slots + upper_block * slot_count + upper_entry % slot_count
    partner = jnp.where(neighbour < 0, own_key, jnp.where(neighbour < slot_count, same_key, jnp.where(neighbour < slot_count + capacity, lower_key, upper_key))).reshape(-1)
    outer_sign = jnp.where(neighbour < 0, -1.0, 1.0).astype(jnp.float32)[None, None]
    valid_mask = jnp.any(neighbour >= 0, axis=0).astype(jnp.float32)

    def one_event(kernel_total, inputs):
        event_state, forward = inputs
        velocity, summed = run_event(event_state, forward, partner, outer_sign, valid_mask, lame_lambda, shear_modulus, density)
        return (kernel_total + summed, velocity)
    kernel_total, velocities = lax.scan(one_event, jnp.zeros((3, 64, all_slots), jnp.float32), (adjoint_state, forward_velocity))
    kernels = kernel_total.reshape(3, 64, N_DOM, slot_count).transpose(0, 2, 1, 3).reshape(3, N_DOM, 64 * slot_count)
    return (velocities, kernels)
```

```python
import functools
import math

import jax
import jax.numpy as jnp
import numpy as np
from jax import lax
from jax.experimental import pallas as pl
from jax.experimental.pallas import tpu as pltpu
from jax.sharding import PartitionSpec as P

time_step = 0.02
lift_half = 3.0
symmetric_index = ((0, 3, 4), (3, 1, 5), (4, 5, 2))
f32 = jnp.float32
bf16 = jnp.bfloat16
CHUNK = 256
HALO = 512
VMEM_LIMIT = 40 * 2**20


def lobatto_diff():
    points = [-1.0, -1.0 / math.sqrt(5.0), 1.0 / math.sqrt(5.0), 1.0]
    weights = [
        1.0 / math.prod([points[t] - points[o] for o in range(4) if o != t]) for t in range(4)
    ]
    offdiag = [
        [
            0.0 if t == s else weights[s] / weights[t] / (points[t] - points[s])
            for s in range(4)
        ]
        for t in range(4)
    ]
    return np.array(
        [[-sum(offdiag[t]) if t == s else offdiag[t][s] for s in range(4)] for t in range(4)],
        dtype=np.float64,
    )


def kron3(first, second, third):
    return np.kron(np.kron(first, second), third)


def deriv_parts(inner):
    matrix = lobatto_diff()
    if inner:
        matrix = matrix + np.diag([lift_half, 0.0, 0.0, -lift_half])
    matrix = matrix.astype(np.float32)
    eye = np.eye(4, dtype=np.float32)
    stack = [kron3(matrix, eye, eye), kron3(eye, matrix, eye), kron3(eye, eye, matrix)]
    high = [np.asarray(m.astype(bf16)) for m in stack]
    low = [np.asarray((m - h.astype(np.float32)).astype(bf16)) for m, h in zip(stack, high)]
    return [h.astype(np.float32) for h in high], [l.astype(np.float32) for l in low]


def face_rows(face):
    rows = np.zeros((16, 64), np.float32)
    for q in range(16):
        at = [q // 4, q % 4]
        at.insert(face // 2, 3 * (face % 2))
        rows[q, 16 * at[0] + 4 * at[1] + at[2]] = 1.0
    return rows


def tables():
    high, low = deriv_parts(True)
    plain_high, plain_low = deriv_parts(False)
    zero = np.zeros((64, 64), np.float32)
    picks = [face_rows(f) for f in range(6)]
    holders = np.diag(sum(p.sum(axis=0) for p in picks))
    vel = np.concatenate(
        [np.concatenate([high[j], high[j], low[j]], axis=1) for j in range(3)]
        + [np.concatenate([-lift_half * holders, -lift_half * holders, zero], axis=1)],
        axis=0,
    )
    fwd = np.concatenate(
        [np.concatenate([plain_high[j], plain_high[j], plain_low[j]], axis=1) for j in range(3)],
        axis=0,
    )
    div = np.concatenate([m for j in range(3) for m in (high[j], high[j], low[j])], axis=1)
    side = np.concatenate(picks[2:4], axis=0)
    ends = np.concatenate(picks[4:6], axis=0)
    none = np.zeros((32, 64), np.float32)
    yz = np.concatenate([side, ends], axis=0)
    pick_vel = np.concatenate(
        [np.concatenate([yz, zero], axis=1), np.concatenate([zero, yz], axis=1)], axis=0
    )
    pick_str = np.concatenate(
        [
            np.concatenate([side, none, none, none], axis=1),
            np.concatenate([none, none, ends, none], axis=1),
            np.concatenate([none, side, none, none], axis=1),
            np.concatenate([none, none, none, ends], axis=1),
        ],
        axis=0,
    )
    signs = np.where(np.arange(64) // 16 % 2 == 1, 1.0, -1.0).astype(np.float32)
    put = lift_half * yz.T
    normal = put * signs[None]
    in_y = (np.arange(64) < 32).astype(np.float32)[None]
    gy, gz = normal * in_y, normal * (1.0 - in_y)
    lift_vel = np.concatenate([np.concatenate([m, m], axis=1) for m in (gy, gz, put)], axis=0)
    lift_str = np.concatenate([normal, normal], axis=1)
    return {
        name: np.asarray(value).astype(bf16)
        for name, value in dict(
            vel=vel, fwd=fwd, div=div, pick_vel=pick_vel, pick_str=pick_str,
            lift_vel=lift_vel, lift_str=lift_str,
        ).items()
    }


def split(value):
    high = value.astype(bf16)
    return high, (value - high.astype(f32)).astype(bf16)


def mm(left, right):
    return jnp.dot(left, right, preferred_element_type=f32)


def onehot(row, depth):
    ids = lax.broadcasted_iota(jnp.int32, (depth, row.shape[-1]), 0)
    return jnp.where(ids == row, 1.0, 0.0).astype(bf16)


def chunks(width):
    return [slice(c, c + CHUNK) for c in range(0, width, CHUNK)]


def side_faces(plus, comp):
    return [plus[f][16 * comp:16 * comp + 16] for f in range(6)]


def pad_x(first, last):
    return jnp.concatenate([first, jnp.zeros((32,) + first.shape[1:], f32), last], axis=0)


def halo_faces(lhs, keys, width):
    blocks = 2 * HALO // CHUNK
    first = width // CHUNK
    out = []
    for f in range(6):
        key = keys[f:f + 1]
        got = mm(lhs, onehot(key & (CHUNK - 1), CHUNK))
        which = key >> 8
        total = jnp.zeros((48, CHUNK), f32)
        for a in range(blocks):
            both = got[48 * a:48 * a + 48] + got[48 * (blocks + a):48 * (blocks + a) + 48]
            total = jnp.where(which == first + a, both, total)
        out.append(total)
    return out


def halo_lhs(recv_one, recv_two):
    parts = [recv_one[:, s] for s in chunks(HALO)] + [recv_two[:, s] for s in chunks(HALO)]
    high, low = split(jnp.concatenate(parts, axis=0))
    return jnp.concatenate([high, low], axis=0)


def local_faces(traces, keys, lanes, own_sign):
    width = traces.shape[1]
    blocks = width // CHUNK
    out = []
    for f in range(6):
        key = keys[f:f + 1]
        other = 48 * (f ^ 1)
        lhs = jnp.concatenate(
            [traces[p + other:p + other + 48, s] for p in (0, 288) for s in chunks(width)], axis=0
        )
        got = mm(lhs, onehot(key & (CHUNK - 1), CHUNK))
        which = key >> 8
        own = traces[48 * f:48 * f + 48, lanes].astype(f32)
        own = own + traces[288 + 48 * f:288 + 48 * f + 48, lanes].astype(f32)
        total = jnp.where(which < 0, own_sign * own, 0.0)
        for a in range(blocks):
            both = got[48 * a:48 * a + 48] + got[48 * (blocks + a):48 * (blocks + a) + 48]
            total = jnp.where(which == a, both, total)
        out.append(total)
    return out


def put_traces(traces, lanes, comp, faces_x, picked):
    base = 16 * comp
    for f in range(2):
        for p in range(2):
            traces[288 * p + 48 * f + base:288 * p + 48 * f + base + 16, lanes] = faces_x[f][p]
    picked = picked.astype(bf16)
    for p in range(2):
        for f in range(4):
            at = 288 * p + 48 * (f + 2) + base
            traces[at:at + 16, lanes] = picked[64 * p + 16 * f:64 * p + 16 * f + 16]


def vel_traces(traces, lanes, velocity, pick):
    for i in range(3):
        high, low = split(velocity[i])
        picked = mm(pick, jnp.concatenate([high, low], axis=0))
        put_traces(traces, lanes, i, ((high[0:16], low[0:16]), (high[48:64], low[48:64])), picked)


def str_traces(traces, lanes, stress, pick):
    pieces = [split(s) for s in stress]
    for i in range(3):
        along_x, along_y, along_z = (pieces[m] for m in symmetric_index[i])
        picked = mm(pick, jnp.concatenate(along_y + along_z, axis=0))
        faces_x = (
            (along_x[0][0:16], along_x[1][0:16]),
            (along_x[0][48:64], along_x[1][48:64]),
        )
        put_traces(traces, lanes, i, faces_x, picked)


def pack(traces, slots, faces, send_one, send_two):
    for row, send in enumerate((send_one, send_two)):
        for s in chunks(HALO):
            slot = slots[row:row + 1, s]
            face = faces[row:row + 1, s]
            got = mm(traces[...], onehot(slot, traces.shape[1]))
            total = jnp.zeros((48, CHUNK), f32)
            for f in range(6):
                both = got[48 * f:48 * f + 48] + got[288 + 48 * f:288 + 48 * f + 48]
                total = jnp.where(face == f, both, total)
            send[:, s] = total


def rate_of(grad, lame, shear):
    trace = lame * (grad[0][0] + grad[1][1] + grad[2][2])
    return [
        trace + 2.0 * shear * grad[0][0],
        trace + 2.0 * shear * grad[1][1],
        trace + 2.0 * shear * grad[2][2],
        shear * (grad[0][1] + grad[1][0]),
        shear * (grad[0][2] + grad[2][0]),
        shear * (grad[1][2] + grad[2][1]),
    ]


def lift_velocity(plus, table):
    grad, jump = [], []
    for i in range(3):
        low_x, high_x, *rest = side_faces(plus, i)
        high, low = split(jnp.concatenate(rest, axis=0))
        put = mm(table, jnp.concatenate([high, low], axis=0))
        grad.append(
            (pad_x(-lift_half * low_x, lift_half * high_x), put[0:64], put[64:128])
        )
        jump.append(put[128:192] + pad_x(lift_half * low_x, lift_half * high_x))
    return grad, jump


def lift_stress(plus, table):
    out = []
    for i in range(3):
        low_x, high_x, *rest = side_faces(plus, i)
        high, low = split(jnp.concatenate(rest, axis=0))
        put = mm(table, jnp.concatenate([high, low], axis=0))
        out.append(put + pad_x(-lift_half * low_x, lift_half * high_x))
    return out


def start_kernel(
    odd, state, neighbour, send_list, pick,
    velocity, stress, keys, slots, faces, traces, send_one, send_two,
):
    width = neighbour.shape[1]
    cap = send_list.shape[1]
    is_odd = odd[0] == 1
    code = neighbour[...]
    low_base = jnp.where(is_odd, width, width + HALO)
    high_base = jnp.where(is_odd, width + HALO, width)
    keys[...] = jnp.where(
        code < width,
        code,
        jnp.where(code < width + cap, code - width + low_base, code - width - cap + high_base),
    )
    valid = jnp.where(jnp.max(code, axis=0, keepdims=True) >= 0, 1.0, 0.0)
    entries = send_list[...]
    entries = jnp.concatenate([entries, jnp.full((2, HALO - cap), -1, jnp.int32)], axis=1)
    entries = jnp.where(
        is_odd, entries, jnp.concatenate([entries[1:2], entries[0:1]], axis=0)
    )
    face = jnp.zeros_like(entries)
    for f in range(1, 6):
        face = face + jnp.where(entries >= f * width, 1, 0)
    faces[...] = face
    slots[...] = entries - face * width
    for lanes in chunks(width):
        mask = valid[:, lanes]
        now = [state[i, :, lanes] * mask for i in range(9)]
        for i in range(3):
            velocity[i, :, lanes] = now[i]
        for i in range(6):
            stress[i, :, lanes] = now[3 + i]
        vel_traces(traces, lanes, now[0:3], pick[...])
    pack(traces, slots[...], faces[...], send_one, send_two)


def vel_local_kernel(
    step, velocity, stress, traces, keys, lame, shear, vel, lift, *rest,
):
    if len(rest) == 2:
        forward = total = total_out = None
        stress_out, jump_out = rest
    else:
        forward, total, stress_out, jump_out, total_out = rest
    width = velocity.shape[2]
    for lanes in chunks(width):
        plus = local_faces(traces, keys[:, lanes], lanes, 1.0)
        grad, jump = lift_velocity(plus, lift[...])
        whole = []
        for i in range(3):
            high, low = split(velocity[i, :, lanes])
            got = mm(vel[...], jnp.concatenate([high, low, high], axis=0))
            whole.append([got[64 * j:64 * j + 64] + grad[i][j] for j in range(3)])
            jump_out[i, :, lanes] = got[192:256] + jump[i]
        rate = rate_of(whole, lame[:, lanes], shear[:, lanes])
        for m in range(6):
            stress_out[m, :, lanes] = stress[m, :, lanes] + time_step * rate[m]
        if total is not None:
            total_out[:, lanes] = total[:, lanes] + rho_term(forward, step, velocity, lanes)


def rho_term(forward, step, velocity, lanes):
    acc = forward[step, 0, :, lanes] * velocity[0, :, lanes]
    acc = acc + forward[step, 1, :, lanes] * velocity[1, :, lanes]
    acc = acc + forward[step, 2, :, lanes] * velocity[2, :, lanes]
    return -time_step * acc


def vel_halo_kernel(
    stress, jump, recv_one, recv_two, keys, slots, faces, lame, shear, lift, pick,
    stress_out, jump_out, traces, send_one, send_two,
):
    width = stress.shape[2]
    lhs = halo_lhs(recv_one, recv_two)
    for lanes in chunks(width):
        plus = halo_faces(lhs, keys[:, lanes], width)
        grad, more = lift_velocity(plus, lift[...])
        rate = rate_of(grad, lame[:, lanes], shear[:, lanes])
        now = [stress[m, :, lanes] + time_step * rate[m] for m in range(6)]
        for m in range(6):
            stress_out[m, :, lanes] = now[m]
        for i in range(3):
            jump_out[i, :, lanes] = jump[i, :, lanes] + more[i]
        str_traces(traces, lanes, now, pick[...])
    pack(traces, slots[...], faces[...], send_one, send_two)


def str_local_kernel(
    step, velocity, stress, jump, traces, keys, density, lame, shear, forward, div, lift, fwd, *rest,
):
    if len(rest) == 2:
        total = None
        velocity_out, total_out = rest
    else:
        total, velocity_out, total_out = rest
    width = velocity.shape[2]
    for lanes in chunks(width):
        plus = local_faces(traces, keys[:, lanes], lanes, -1.0)
        lifted = lift_stress(plus, lift[...])
        now = [stress[m, :, lanes] for m in range(6)]
        pieces = [split(s) for s in now]
        rho = density[:, lanes]
        impedance = jnp.sqrt(rho * (lame[:, lanes] + 2.0 * shear[:, lanes]))
        scale = time_step / rho
        for i in range(3):
            rows = []
            for m in symmetric_index[i]:
                rows += [pieces[m][0], pieces[m][1], pieces[m][0]]
            got = mm(div[...], jnp.concatenate(rows, axis=0))
            velocity_out[i, :, lanes] = velocity[i, :, lanes] + scale * (
                got + lifted[i] + impedance * jump[i, :, lanes]
            )
        grad = []
        for i in range(3):
            high, low = split(forward[step, i, :, lanes])
            got = mm(fwd[...], jnp.concatenate([high, low, high], axis=0))
            grad.append([got[64 * j:64 * j + 64] for j in range(3)])
        diag = (grad[0][0], grad[1][1], grad[2][2])
        lame_term = -time_step * (diag[0] + diag[1] + diag[2]) * (now[0] + now[1] + now[2])
        shear_term = (-2.0 * time_step) * (
            diag[0] * now[0]
            + diag[1] * now[1]
            + diag[2] * now[2]
            + (grad[0][1] + grad[1][0]) * now[3]
            + (grad[0][2] + grad[2][0]) * now[4]
            + (grad[1][2] + grad[2][1]) * now[5]
        )
        for m, term in enumerate((lame_term, shear_term)):
            if total is not None:
                term = total[m, :, lanes] + term
            total_out[m, :, lanes] = term


def str_halo_kernel(
    velocity, recv_one, recv_two, keys, slots, faces, density, lift, pick,
    velocity_out, traces, send_one, send_two,
):
    halo_velocity(velocity, recv_one, recv_two, keys, density, lift, velocity_out, traces, pick)
    pack(traces, slots[...], faces[...], send_one, send_two)


def last_kernel(
    step, velocity, recv_one, recv_two, keys, density, lift, forward, total, velocity_out, total_out
):
    halo_velocity(velocity, recv_one, recv_two, keys, density, lift, velocity_out, None, None)
    for lanes in chunks(velocity.shape[2]):
        total_out[:, lanes] = total[:, lanes] + rho_term(forward, step, velocity_out, lanes)


def halo_velocity(
    velocity, recv_one, recv_two, keys, density, lift, velocity_out, traces, pick
):
    width = velocity.shape[2]
    lhs = halo_lhs(recv_one, recv_two)
    for lanes in chunks(width):
        plus = halo_faces(lhs, keys[:, lanes], width)
        lifted = lift_stress(plus, lift[...])
        scale = time_step / density[:, lanes]
        now = [velocity[i, :, lanes] + scale * lifted[i] for i in range(3)]
        for i in range(3):
            velocity_out[i, :, lanes] = now[i]
        if traces is not None:
            vel_traces(traces, lanes, now, pick[...])


def call(name, kernel, args, outs, specs=None, cost=0):
    whole = pl.BlockSpec(memory_space=pltpu.VMEM)
    specs = specs or {}
    return pl.pallas_call(
        kernel,
        name=name,
        in_specs=[specs.get(k, whole) for k in range(len(args))],
        out_specs=[whole] * len(outs),
        out_shape=[jax.ShapeDtypeStruct(s, d) for s, d in outs],
        compiler_params=pltpu.CompilerParams(vmem_limit_bytes=VMEM_LIMIT),
        cost_estimate=pl.CostEstimate(flops=cost, bytes_accessed=6_000_000, transcendentals=0),
    )(*args)


def swap(sent, axis):
    count = lax.axis_size(axis)
    got = []
    for first, value in enumerate(sent):
        pairs = []
        for low in range(first, count - 1, 2):
            pairs += [(low, low + 1), (low + 1, low)]
        got.append(lax.ppermute(value, axis, pairs))
    return got


def local(
    adjoint_state, forward_velocity, density, lame_lambda, shear_modulus, neighbour, send_list
):
    width = density.shape[1]
    steps = forward_velocity.shape[1]
    table = {k: jnp.asarray(v) for k, v in tables().items()}
    state = adjoint_state[0]
    forward = forward_velocity[0]
    odd = (lax.axis_index("dom") % 2).astype(jnp.int32).reshape(1)

    field = ((64, width), f32)
    vector = ((3, 64, width), f32)
    tensor = ((6, 64, width), f32)
    two = ((2, 64, width), f32)
    trace = ((576, width), bf16)
    sends = [((48, HALO), f32)] * 2
    ints = [((6, width), jnp.int32), ((2, HALO), jnp.int32), ((2, HALO), jnp.int32)]

    velocity, stress, keys, slots, faces, traces, *sent = call(
        "start", start_kernel, (odd, state, neighbour, send_list, table["pick_vel"]),
        [vector, tensor] + ints + [trace] + sends,
        specs={0: pl.BlockSpec(memory_space=pltpu.SMEM)},
    )
    rho_total = jnp.zeros(*field)
    other_total = None
    for n in range(steps):
        recv = swap(sent, "dom")
        args = [velocity, stress, traces, keys, lame_lambda, shear_modulus,
                table["vel"], table["lift_vel"]]
        outs = [tensor, vector]
        if n:
            args += [forward, rho_total]
            outs += [field]
        stress, jump, *more = call(
            "vel_local", functools.partial(vel_local_kernel, n - 1), args, outs, cost=4_000_000_000
        )
        if more:
            rho_total = more[0]
        stress, jump, traces, *sent = call(
            "vel_halo", vel_halo_kernel,
            (stress, jump, *recv, keys, slots, faces, lame_lambda, shear_modulus,
             table["lift_vel"], table["pick_str"]),
            [tensor, vector, trace] + sends,
        )
        recv = swap(sent, "dom")
        args = [velocity, stress, jump, traces, keys, density, lame_lambda, shear_modulus,
                forward, table["div"], table["lift_str"], table["fwd"]]
        if n:
            args += [other_total]
        velocity, other_total = call(
            "str_local", functools.partial(str_local_kernel, n), args, [vector, two],
            cost=4_000_000_000,
        )
        if n < steps - 1:
            velocity, traces, *sent = call(
                "str_halo", str_halo_kernel,
                (velocity, *recv, keys, slots, faces, density, table["lift_str"],
                 table["pick_vel"]),
                [vector, trace] + sends,
            )
        else:
            velocity, rho_total = call(
                "last", functools.partial(last_kernel, n),
                (velocity, *recv, keys, density, table["lift_str"], forward, rho_total),
                [vector, field],
            )

    def reduced(value):
        count = lax.axis_size("event")
        if 64 % count == 0:
            part = lax.psum_scatter(value, "event", scatter_dimension=1, tiled=True)
        else:
            flat = value.reshape(value.shape[0], -1)
            part = lax.psum_scatter(flat, "event", scatter_dimension=1, tiled=True)
        return part.reshape(value.shape[0], 1, -1)

    kernels = jnp.concatenate([reduced(rho_total[None]), reduced(other_total)], axis=0)
    return velocity[None], kernels


def solution(mesh):
    placed = (
        P("event", None, None, "dom"),
        P("event", None, None, None, "dom"),
        P(None, "dom"),
        P(None, "dom"),
        P(None, "dom"),
        P(None, "dom"),
        P(None, "dom"),
    )
    return jax.shard_map(
        local,
        mesh=mesh,
        in_specs=placed,
        out_specs=(P("event", None, None, "dom"), P(None, "dom", "event")),
        check_vma=False,
    )
```

```python
import functools
import math

import jax
import jax.numpy as jnp
import numpy as np
from jax import lax
from jax.experimental import pallas as pl
from jax.experimental.pallas import tpu as pltpu
from jax.sharding import PartitionSpec as P

time_step = 0.02
lift_half = 3.0
symmetric_index = ((0, 3, 4), (3, 1, 5), (4, 5, 2))
f32 = jnp.float32
bf16 = jnp.bfloat16
CHUNK = 256
HALO = 512
VMEM_LIMIT = 40 * 2**20


def lobatto_diff():
    points = [-1.0, -1.0 / math.sqrt(5.0), 1.0 / math.sqrt(5.0), 1.0]
    weights = [
        1.0 / math.prod([points[t] - points[o] for o in range(4) if o != t]) for t in range(4)
    ]
    offdiag = [
        [
            0.0 if t == s else weights[s] / weights[t] / (points[t] - points[s])
            for s in range(4)
        ]
        for t in range(4)
    ]
    return np.array(
        [[-sum(offdiag[t]) if t == s else offdiag[t][s] for s in range(4)] for t in range(4)],
        dtype=np.float64,
    )


def kron3(first, second, third):
    return np.kron(np.kron(first, second), third)


def deriv_parts(inner):
    matrix = lobatto_diff()
    if inner:
        matrix = matrix + np.diag([lift_half, 0.0, 0.0, -lift_half])
    matrix = matrix.astype(np.float32)
    eye = np.eye(4, dtype=np.float32)
    stack = [kron3(matrix, eye, eye), kron3(eye, matrix, eye), kron3(eye, eye, matrix)]
    high = [np.asarray(m.astype(bf16)) for m in stack]
    low = [np.asarray((m - h.astype(np.float32)).astype(bf16)) for m, h in zip(stack, high)]
    return [h.astype(np.float32) for h in high], [l.astype(np.float32) for l in low]


def face_rows(face):
    rows = np.zeros((16, 64), np.float32)
    for q in range(16):
        at = [q // 4, q % 4]
        at.insert(face // 2, 3 * (face % 2))
        rows[q, 16 * at[0] + 4 * at[1] + at[2]] = 1.0
    return rows


def tables():
    high, low = deriv_parts(True)
    plain_high, plain_low = deriv_parts(False)
    zero = np.zeros((64, 64), np.float32)
    picks = [face_rows(f) for f in range(6)]
    holders = np.diag(sum(p.sum(axis=0) for p in picks))
    vel = np.concatenate(
        [np.concatenate([high[j], high[j], low[j]], axis=1) for j in range(3)]
        + [np.concatenate([-lift_half * holders, -lift_half * holders, zero], axis=1)],
        axis=0,
    )
    fwd = np.concatenate(
        [np.concatenate([plain_high[j], plain_high[j], plain_low[j]], axis=1) for j in range(3)],
        axis=0,
    )
    div = np.concatenate([m for j in range(3) for m in (high[j], high[j], low[j])], axis=1)
    side = np.concatenate(picks[2:4], axis=0)
    ends = np.concatenate(picks[4:6], axis=0)
    none = np.zeros((32, 64), np.float32)
    yz = np.concatenate([side, ends], axis=0)
    pick_vel = np.concatenate(
        [np.concatenate([yz, zero], axis=1), np.concatenate([zero, yz], axis=1)], axis=0
    )
    pick_str = np.concatenate(
        [
            np.concatenate([side, none, none, none], axis=1),
            np.concatenate([none, none, ends, none], axis=1),
            np.concatenate([none, side, none, none], axis=1),
            np.concatenate([none, none, none, ends], axis=1),
        ],
        axis=0,
    )
    signs = np.where(np.arange(64) // 16 % 2 == 1, 1.0, -1.0).astype(np.float32)
    put = lift_half * yz.T
    normal = put * signs[None]
    in_y = (np.arange(64) < 32).astype(np.float32)[None]
    gy, gz = normal * in_y, normal * (1.0 - in_y)
    lift_vel = np.concatenate([np.concatenate([m, m], axis=1) for m in (gy, gz, put)], axis=0)
    lift_str = np.concatenate([normal, normal], axis=1)
    return {
        name: np.asarray(value).astype(bf16)
        for name, value in dict(
            vel=vel, fwd=fwd, div=div, pick_vel=pick_vel, pick_str=pick_str,
            lift_vel=lift_vel, lift_str=lift_str,
        ).items()
    }


def split(value):
    high = value.astype(bf16)
    return high, (value - high.astype(f32)).astype(bf16)


def mm(left, right):
    return jnp.dot(left, right, preferred_element_type=f32)


def onehot(row, depth):
    ids = lax.broadcasted_iota(jnp.int32, (depth, row.shape[-1]), 0)
    return jnp.where(ids == row, 1.0, 0.0).astype(bf16)


def chunks(width):
    return [slice(c, c + CHUNK) for c in range(0, width, CHUNK)]


def side_faces(plus, comp):
    return [plus[f][16 * comp:16 * comp + 16] for f in range(6)]


def pad_x(first, last):
    return jnp.concatenate([first, jnp.zeros((32,) + first.shape[1:], f32), last], axis=0)


def halo_faces(lhs, keys, width):
    blocks = 2 * HALO // CHUNK
    first = width // CHUNK
    out = []
    for f in range(6):
        key = keys[f:f + 1]
        got = mm(lhs, onehot(key & (CHUNK - 1), CHUNK))
        which = key >> 8
        total = jnp.zeros((48, CHUNK), f32)
        for a in range(blocks):
            both = got[48 * a:48 * a + 48] + got[48 * (blocks + a):48 * (blocks + a) + 48]
            total = jnp.where(which == first + a, both, total)
        out.append(total)
    return out


def halo_lhs(recv_one, recv_two):
    parts = [recv_one[:, s] for s in chunks(HALO)] + [recv_two[:, s] for s in chunks(HALO)]
    high, low = split(jnp.concatenate(parts, axis=0))
    return jnp.concatenate([high, low], axis=0)


def local_faces(traces, keys, lanes, own_sign):
    width = traces.shape[1]
    blocks = width // CHUNK
    out = []
    for f in range(6):
        key = keys[f:f + 1]
        other = 48 * (f ^ 1)
        lhs = jnp.concatenate(
            [traces[p + other:p + other + 48, s] for p in (0, 288) for s in chunks(width)], axis=0
        )
        got = mm(lhs, onehot(key & (CHUNK - 1), CHUNK))
        which = key >> 8
        own = traces[48 * f:48 * f + 48, lanes].astype(f32)
        own = own + traces[288 + 48 * f:288 + 48 * f + 48, lanes].astype(f32)
        total = jnp.where(which < 0, own_sign * own, 0.0)
        for a in range(blocks):
            both = got[48 * a:48 * a + 48] + got[48 * (blocks + a):48 * (blocks + a) + 48]
            total = jnp.where(which == a, both, total)
        out.append(total)
    return out


def put_traces(traces, lanes, comp, faces_x, picked):
    base = 16 * comp
    for f in range(2):
        for p in range(2):
            traces[288 * p + 48 * f + base:288 * p + 48 * f + base + 16, lanes] = faces_x[f][p]
    picked = picked.astype(bf16)
    for p in range(2):
        for f in range(4):
            at = 288 * p + 48 * (f + 2) + base
            traces[at:at + 16, lanes] = picked[64 * p + 16 * f:64 * p + 16 * f + 16]


def vel_traces(traces, lanes, velocity, pick):
    for i in range(3):
        high, low = split(velocity[i])
        picked = mm(pick, jnp.concatenate([high, low], axis=0))
        put_traces(traces, lanes, i, ((high[0:16], low[0:16]), (high[48:64], low[48:64])), picked)


def str_traces(traces, lanes, stress, pick):
    pieces = [split(s) for s in stress]
    for i in range(3):
        along_x, along_y, along_z = (pieces[m] for m in symmetric_index[i])
        picked = mm(pick, jnp.concatenate(along_y + along_z, axis=0))
        faces_x = (
            (along_x[0][0:16], along_x[1][0:16]),
            (along_x[0][48:64], along_x[1][48:64]),
        )
        put_traces(traces, lanes, i, faces_x, picked)


def pack(traces, slots, faces, send_one, send_two):
    for row, send in enumerate((send_one, send_two)):
        for s in chunks(HALO):
            slot = slots[row:row + 1, s]
            face = faces[row:row + 1, s]
            got = mm(traces[...], onehot(slot, traces.shape[1]))
            total = jnp.zeros((48, CHUNK), f32)
            for f in range(6):
                both = got[48 * f:48 * f + 48] + got[288 + 48 * f:288 + 48 * f + 48]
                total = jnp.where(face == f, both, total)
            send[:, s] = total


def pack_gather(traces, values, slots, faces, send_one, send_two):
    width = traces.shape[1]
    for at in range(0, 288, 16):
        values[at:at + 16] = (
            traces[at:at + 16].astype(f32) + traces[288 + at:288 + at + 16].astype(f32)
        )
    for row, send in enumerate((send_one, send_two)):
        for t in range(HALO // 128):
            s = slice(128 * t, 128 * t + 128)
            slot = jnp.broadcast_to(slots[row:row + 1, s], (8, 128))
            face = jnp.broadcast_to(faces[row:row + 1, s], (8, 128))
            lane = slot & 127
            key = jnp.where(slot < 0, -1, face * width + slot) >> 7
            total = [jnp.zeros((8, 128), f32)] * 6
            for f in range(6):
                for a in range(width // 128):
                    here = key == f * (width // 128) + a
                    for r in range(6):
                        at = 48 * f + 8 * r
                        src = values[at:at + 8, 128 * a:128 * a + 128]
                        got = jnp.take_along_axis(src, lane, axis=1)
                        total[r] = jnp.where(here, got, total[r])
            for r in range(6):
                send[8 * r:8 * r + 8, s] = total[r]


def rate_of(grad, lame, shear):
    trace = lame * (grad[0][0] + grad[1][1] + grad[2][2])
    return [
        trace + 2.0 * shear * grad[0][0],
        trace + 2.0 * shear * grad[1][1],
        trace + 2.0 * shear * grad[2][2],
        shear * (grad[0][1] + grad[1][0]),
        shear * (grad[0][2] + grad[2][0]),
        shear * (grad[1][2] + grad[2][1]),
    ]


def lift_velocity(plus, table):
    grad, jump = [], []
    for i in range(3):
        low_x, high_x, *rest = side_faces(plus, i)
        high, low = split(jnp.concatenate(rest, axis=0))
        put = mm(table, jnp.concatenate([high, low], axis=0))
        grad.append(
            (pad_x(-lift_half * low_x, lift_half * high_x), put[0:64], put[64:128])
        )
        jump.append(put[128:192] + pad_x(lift_half * low_x, lift_half * high_x))
    return grad, jump


def lift_stress(plus, table):
    out = []
    for i in range(3):
        low_x, high_x, *rest = side_faces(plus, i)
        high, low = split(jnp.concatenate(rest, axis=0))
        put = mm(table, jnp.concatenate([high, low], axis=0))
        out.append(put + pad_x(-lift_half * low_x, lift_half * high_x))
    return out


def start_kernel(
    odd, state_hbm, neighbour_hbm, send_list_hbm, pick_hbm,
    velocity, stress, keys, slots, faces, traces, send_one, send_two,
    state, neighbour, send_list, pick, sems,
):
    copies = [
        pltpu.make_async_copy(source, target, sems.at[k])
        for k, (source, target) in enumerate((
            (neighbour_hbm, neighbour), (send_list_hbm, send_list), (pick_hbm, pick),
            (state_hbm.at[0:3], state.at[0:3]), (state_hbm.at[3:9], state.at[3:9]),
        ))
    ]
    for copy in copies:
        copy.start()
    for copy in copies[0:2]:
        copy.wait()
    width = neighbour.shape[1]
    cap = send_list.shape[1]
    is_odd = odd[0] == 1
    code = neighbour[...]
    low_base = jnp.where(is_odd, width, width + HALO)
    high_base = jnp.where(is_odd, width + HALO, width)
    keys[...] = jnp.where(
        code < width,
        code,
        jnp.where(code < width + cap, code - width + low_base, code - width - cap + high_base),
    )
    valid = jnp.where(jnp.max(code, axis=0, keepdims=True) >= 0, 1.0, 0.0)
    entries = send_list[...]
    entries = jnp.concatenate([entries, jnp.full((2, HALO - cap), -1, jnp.int32)], axis=1)
    entries = jnp.where(
        is_odd, entries, jnp.concatenate([entries[1:2], entries[0:1]], axis=0)
    )
    face = jnp.zeros_like(entries)
    for f in range(1, 6):
        face = face + jnp.where(entries >= f * width, 1, 0)
    faces[...] = face
    slots[...] = entries - face * width
    for copy in copies[2:4]:
        copy.wait()
    for lanes in chunks(width):
        mask = valid[:, lanes]
        now = [state[i, :, lanes] * mask for i in range(3)]
        for i in range(3):
            velocity[i, :, lanes] = now[i]
        vel_traces(traces, lanes, now[0:3], pick[...])
    pack(traces, slots[...], faces[...], send_one, send_two)
    copies[4].wait()
    for lanes in chunks(width):
        for i in range(6):
            stress[i, :, lanes] = state[3 + i, :, lanes] * valid[:, lanes]


def vel_local_kernel(
    step, velocity, stress, traces, keys, lame, shear, vel, lift, *rest,
):
    if len(rest) == 2:
        forward = total = total_out = None
        stress_out, jump_out = rest
    else:
        forward, total, stress_out, jump_out, total_out = rest
    width = velocity.shape[2]
    for lanes in chunks(width):
        plus = local_faces(traces, keys[:, lanes], lanes, 1.0)
        grad, jump = lift_velocity(plus, lift[...])
        whole = []
        for i in range(3):
            high, low = split(velocity[i, :, lanes])
            got = mm(vel[...], jnp.concatenate([high, low, high], axis=0))
            whole.append([got[64 * j:64 * j + 64] + grad[i][j] for j in range(3)])
            jump_out[i, :, lanes] = got[192:256] + jump[i]
        rate = rate_of(whole, lame[:, lanes], shear[:, lanes])
        for m in range(6):
            stress_out[m, :, lanes] = stress[m, :, lanes] + time_step * rate[m]
        if total is not None:
            total_out[:, lanes] = total[:, lanes] + rho_term(forward, step, velocity, lanes)


def rho_term(forward, step, velocity, lanes):
    acc = forward[step, 0, :, lanes] * velocity[0, :, lanes]
    acc = acc + forward[step, 1, :, lanes] * velocity[1, :, lanes]
    acc = acc + forward[step, 2, :, lanes] * velocity[2, :, lanes]
    return -time_step * acc


def vel_halo_kernel(
    stress, jump, recv_one, recv_two, keys, slots, faces, lame, shear, lift, pick,
    stress_out, jump_out, traces, send_one, send_two,
):
    width = stress.shape[2]
    lhs = halo_lhs(recv_one, recv_two)
    for lanes in chunks(width):
        plus = halo_faces(lhs, keys[:, lanes], width)
        grad, more = lift_velocity(plus, lift[...])
        rate = rate_of(grad, lame[:, lanes], shear[:, lanes])
        now = [stress[m, :, lanes] + time_step * rate[m] for m in range(6)]
        for m in range(6):
            stress_out[m, :, lanes] = now[m]
        for i in range(3):
            jump_out[i, :, lanes] = jump[i, :, lanes] + more[i]
        str_traces(traces, lanes, now, pick[...])
    pack(traces, slots[...], faces[...], send_one, send_two)


def str_local_kernel(
    step, velocity, stress, jump, traces, keys, density, lame, shear, forward, div, lift, fwd, *rest,
):
    if len(rest) == 2:
        total = None
        velocity_out, total_out = rest
    else:
        total, velocity_out, total_out = rest
    width = velocity.shape[2]
    for lanes in chunks(width):
        plus = local_faces(traces, keys[:, lanes], lanes, -1.0)
        lifted = lift_stress(plus, lift[...])
        now = [stress[m, :, lanes] for m in range(6)]
        pieces = [split(s) for s in now]
        rho = density[:, lanes]
        impedance = jnp.sqrt(rho * (lame[:, lanes] + 2.0 * shear[:, lanes]))
        scale = time_step / rho
        for i in range(3):
            rows = []
            for m in symmetric_index[i]:
                rows += [pieces[m][0], pieces[m][1], pieces[m][0]]
            got = mm(div[...], jnp.concatenate(rows, axis=0))
            velocity_out[i, :, lanes] = velocity[i, :, lanes] + scale * (
                got + lifted[i] + impedance * jump[i, :, lanes]
            )
        grad = []
        for i in range(3):
            high, low = split(forward[step, i, :, lanes])
            got = mm(fwd[...], jnp.concatenate([high, low, high], axis=0))
            grad.append([got[64 * j:64 * j + 64] for j in range(3)])
        diag = (grad[0][0], grad[1][1], grad[2][2])
        lame_term = -time_step * (diag[0] + diag[1] + diag[2]) * (now[0] + now[1] + now[2])
        shear_term = (-2.0 * time_step) * (
            diag[0] * now[0]
            + diag[1] * now[1]
            + diag[2] * now[2]
            + (grad[0][1] + grad[1][0]) * now[3]
            + (grad[0][2] + grad[2][0]) * now[4]
            + (grad[1][2] + grad[2][1]) * now[5]
        )
        for m, term in enumerate((lame_term, shear_term)):
            if total is not None:
                term = total[m, :, lanes] + term
            total_out[m, :, lanes] = term


def str_halo_kernel(
    velocity, recv_one, recv_two, keys, slots, faces, density, lift, pick,
    velocity_out, traces, send_one, send_two, values,
):
    halo_velocity(velocity, recv_one, recv_two, keys, density, lift, velocity_out, traces, pick)
    pack_gather(traces, values, slots, faces, send_one, send_two)


def last_kernel(
    step, velocity, recv_one, recv_two, keys, density, lift, forward, total, velocity_out, total_out
):
    halo_velocity(velocity, recv_one, recv_two, keys, density, lift, velocity_out, None, None)
    for lanes in chunks(velocity.shape[2]):
        total_out[:, lanes] = total[:, lanes] + rho_term(forward, step, velocity_out, lanes)


def event_sum_kernel(other, rho, out):
    width = rho.shape[3]
    for m, (terms, at) in enumerate(((rho, 0), (other, 0), (other, 1))):
        total = terms[at, 0]
        for e in range(1, terms.shape[1]):
            total = total + terms[at, e]
        for k in range(total.shape[0]):
            out[m, :, k * width:(k + 1) * width] = total[k:k + 1]


def halo_velocity(
    velocity, recv_one, recv_two, keys, density, lift, velocity_out, traces, pick
):
    width = velocity.shape[2]
    lhs = halo_lhs(recv_one, recv_two)
    for lanes in chunks(width):
        plus = halo_faces(lhs, keys[:, lanes], width)
        lifted = lift_stress(plus, lift[...])
        scale = time_step / density[:, lanes]
        now = [velocity[i, :, lanes] + scale * lifted[i] for i in range(3)]
        for i in range(3):
            velocity_out[i, :, lanes] = now[i]
        if traces is not None:
            vel_traces(traces, lanes, now, pick[...])


def call(name, kernel, args, outs, specs=None, cost=0, scratch=()):
    whole = pl.BlockSpec(memory_space=pltpu.VMEM)
    specs = specs or {}
    return pl.pallas_call(
        kernel,
        name=name,
        in_specs=[specs.get(k, whole) for k in range(len(args))],
        out_specs=[whole] * len(outs),
        out_shape=[jax.ShapeDtypeStruct(s, d) for s, d in outs],
        scratch_shapes=list(scratch),
        compiler_params=pltpu.CompilerParams(vmem_limit_bytes=VMEM_LIMIT),
        cost_estimate=pl.CostEstimate(flops=cost, bytes_accessed=6_000_000, transcendentals=0),
    )(*args)


def swap(sent, axis):
    count = lax.axis_size(axis)
    got = []
    for first, value in enumerate(sent):
        pairs = []
        for low in range(first, count - 1, 2):
            pairs += [(low, low + 1), (low + 1, low)]
        got.append(lax.ppermute(value, axis, pairs))
    return got


def local(
    adjoint_state, forward_velocity, density, lame_lambda, shear_modulus, neighbour, send_list
):
    width = density.shape[1]
    steps = forward_velocity.shape[1]
    table = {k: jnp.asarray(v) for k, v in tables().items()}
    state = adjoint_state[0]
    forward = forward_velocity[0]
    odd = (lax.axis_index("dom") % 2).astype(jnp.int32).reshape(1)

    field = ((64, width), f32)
    vector = ((3, 64, width), f32)
    tensor = ((6, 64, width), f32)
    two = ((2, 64, width), f32)
    trace = ((576, width), bf16)
    sends = [((48, HALO), f32)] * 2
    ints = [((6, width), jnp.int32), ((2, HALO), jnp.int32), ((2, HALO), jnp.int32)]

    velocity, stress, keys, slots, faces, traces, *sent = call(
        "start", start_kernel, (odd, state, neighbour, send_list, table["pick_vel"]),
        [vector, tensor] + ints + [trace] + sends,
        specs={0: pl.BlockSpec(memory_space=pltpu.SMEM)}
        | {k: pl.BlockSpec(memory_space=pltpu.HBM) for k in range(1, 5)},
        scratch=[
            pltpu.VMEM(state.shape, f32), pltpu.VMEM(neighbour.shape, jnp.int32),
            pltpu.VMEM(send_list.shape, jnp.int32), pltpu.VMEM((128, 128), bf16),
            pltpu.SemaphoreType.DMA((5,)),
        ],
    )
    rho_total = jnp.zeros(*field)
    other_total = None
    for n in range(steps):
        recv = swap(sent, "dom")
        args = [velocity, stress, traces, keys, lame_lambda, shear_modulus,
                table["vel"], table["lift_vel"]]
        outs = [tensor, vector]
        if n:
            args += [forward, rho_total]
            outs += [field]
        stress, jump, *more = call(
            "vel_local", functools.partial(vel_local_kernel, n - 1), args, outs, cost=4_000_000_000
        )
        if more:
            rho_total = more[0]
        stress, jump, traces, *sent = call(
            "vel_halo", vel_halo_kernel,
            (stress, jump, *recv, keys, slots, faces, lame_lambda, shear_modulus,
             table["lift_vel"], table["pick_str"]),
            [tensor, vector, trace] + sends,
        )
        recv = swap(sent, "dom")
        args = [velocity, stress, jump, traces, keys, density, lame_lambda, shear_modulus,
                forward, table["div"], table["lift_str"], table["fwd"]]
        if n:
            args += [other_total]
        velocity, other_total = call(
            "str_local", functools.partial(str_local_kernel, n), args, [vector, two],
            cost=4_000_000_000,
        )
        if n < steps - 1:
            velocity, traces, *sent = call(
                "str_halo", str_halo_kernel,
                (velocity, *recv, keys, slots, faces, density, table["lift_str"],
                 table["pick_vel"]),
                [vector, trace] + sends, scratch=[pltpu.VMEM((288, width), f32)],
            )
        else:
            velocity, rho_total = call(
                "last", functools.partial(last_kernel, n),
                (velocity, *recv, keys, density, table["lift_str"], forward, rho_total),
                [vector, field],
            )

    count = lax.axis_size("event")
    if 64 % (8 * count) == 0:
        parts = []
        for value in (other_total, rho_total[None]):
            shares = value.reshape(-1, count, 64 // count, width)
            parts.append(lax.all_to_all(shares, "event", 1, 1))
        kernels, = call(
            "event_sum", event_sum_kernel, parts, [((3, 1, 64 // count * width), f32)]
        )
    else:
        flat = jnp.concatenate([rho_total[None], other_total], axis=0).reshape(3, -1)
        part = lax.psum_scatter(flat, "event", scatter_dimension=1, tiled=True)
        kernels = part.reshape(3, 1, -1)
    return velocity[None], kernels


def solution(mesh):
    placed = (
        P("event", None, None, "dom"),
        P("event", None, None, None, "dom"),
        P(None, "dom"),
        P(None, "dom"),
        P(None, "dom"),
        P(None, "dom"),
        P(None, "dom"),
    )
    return jax.shard_map(
        local,
        mesh=mesh,
        in_specs=placed,
        out_specs=(P("event", None, None, "dom"), P(None, "dom", "event")),
        check_vma=False,
    )
```

```python
import functools
import math

import jax
import jax.numpy as jnp
import numpy as np
from jax import lax
from jax.experimental import pallas as pl
from jax.experimental.pallas import tpu as pltpu
from jax.sharding import PartitionSpec as P

time_step = 0.02
lift_half = 3.0
symmetric_index = ((0, 3, 4), (3, 1, 5), (4, 5, 2))
f32 = jnp.float32
bf16 = jnp.bfloat16
CHUNK = 256
HALO = 512
VMEM_LIMIT = 40 * 2**20


def lobatto_diff():
    points = [-1.0, -1.0 / math.sqrt(5.0), 1.0 / math.sqrt(5.0), 1.0]
    weights = [
        1.0 / math.prod([points[t] - points[o] for o in range(4) if o != t]) for t in range(4)
    ]
    offdiag = [
        [
            0.0 if t == s else weights[s] / weights[t] / (points[t] - points[s])
            for s in range(4)
        ]
        for t in range(4)
    ]
    return np.array(
        [[-sum(offdiag[t]) if t == s else offdiag[t][s] for s in range(4)] for t in range(4)],
        dtype=np.float64,
    )


def kron3(first, second, third):
    return np.kron(np.kron(first, second), third)


def deriv_parts(inner):
    matrix = lobatto_diff()
    if inner:
        matrix = matrix + np.diag([lift_half, 0.0, 0.0, -lift_half])
    matrix = matrix.astype(np.float32)
    eye = np.eye(4, dtype=np.float32)
    stack = [kron3(matrix, eye, eye), kron3(eye, matrix, eye), kron3(eye, eye, matrix)]
    high = [np.asarray(m.astype(bf16)) for m in stack]
    low = [np.asarray((m - h.astype(np.float32)).astype(bf16)) for m, h in zip(stack, high)]
    return [h.astype(np.float32) for h in high], [l.astype(np.float32) for l in low]


def face_rows(face):
    rows = np.zeros((16, 64), np.float32)
    for q in range(16):
        at = [q // 4, q % 4]
        at.insert(face // 2, 3 * (face % 2))
        rows[q, 16 * at[0] + 4 * at[1] + at[2]] = 1.0
    return rows


def tables():
    high, low = deriv_parts(True)
    plain_high, plain_low = deriv_parts(False)
    zero = np.zeros((64, 64), np.float32)
    picks = [face_rows(f) for f in range(6)]
    holders = np.diag(sum(p.sum(axis=0) for p in picks))
    vel = np.concatenate(
        [np.concatenate([high[j], high[j], low[j]], axis=1) for j in range(3)]
        + [np.concatenate([-lift_half * holders, -lift_half * holders, zero], axis=1)],
        axis=0,
    )
    fwd = np.concatenate(
        [np.concatenate([plain_high[j], plain_high[j], plain_low[j]], axis=1) for j in range(3)],
        axis=0,
    )
    div = np.concatenate([m for j in range(3) for m in (high[j], high[j], low[j])], axis=1)
    side = np.concatenate(picks[2:4], axis=0)
    ends = np.concatenate(picks[4:6], axis=0)
    none = np.zeros((32, 64), np.float32)
    yz = np.concatenate([side, ends], axis=0)
    pick_vel = np.concatenate(
        [np.concatenate([yz, zero], axis=1), np.concatenate([zero, yz], axis=1)], axis=0
    )
    pick_str = np.concatenate(
        [
            np.concatenate([side, none, none, none], axis=1),
            np.concatenate([none, none, ends, none], axis=1),
            np.concatenate([none, side, none, none], axis=1),
            np.concatenate([none, none, none, ends], axis=1),
        ],
        axis=0,
    )
    signs = np.where(np.arange(64) // 16 % 2 == 1, 1.0, -1.0).astype(np.float32)
    put = lift_half * yz.T
    normal = put * signs[None]
    in_y = (np.arange(64) < 32).astype(np.float32)[None]
    gy, gz = normal * in_y, normal * (1.0 - in_y)
    lift_vel = np.concatenate([np.concatenate([m, m], axis=1) for m in (gy, gz, put)], axis=0)
    lift_str = np.concatenate([normal, normal], axis=1)
    return {
        name: np.asarray(value).astype(bf16)
        for name, value in dict(
            vel=vel, fwd=fwd, div=div, pick_vel=pick_vel, pick_str=pick_str,
            lift_vel=lift_vel, lift_str=lift_str,
        ).items()
    }


def split(value):
    high = value.astype(bf16)
    return high, (value - high.astype(f32)).astype(bf16)


def mm(left, right):
    return jnp.dot(left, right, preferred_element_type=f32)


def onehot(row, depth):
    ids = lax.broadcasted_iota(jnp.int32, (depth, row.shape[-1]), 0)
    return jnp.where(ids == row, 1.0, 0.0).astype(bf16)


def chunks(width):
    return [slice(c, c + CHUNK) for c in range(0, width, CHUNK)]


def side_faces(plus, comp):
    return [plus[f][16 * comp:16 * comp + 16] for f in range(6)]


def pad_x(first, last):
    return jnp.concatenate([first, jnp.zeros((32,) + first.shape[1:], f32), last], axis=0)


def halo_faces(lhs, keys, hots, lanes, width):
    blocks = 2 * HALO // CHUNK
    first = width // CHUNK
    out = []
    for f in range(6):
        key = keys[f:f + 1]
        got = mm(lhs, hots[f, :, lanes])
        which = key >> 8
        total = jnp.zeros((48, CHUNK), f32)
        for a in range(blocks):
            both = got[48 * a:48 * a + 48] + got[48 * (blocks + a):48 * (blocks + a) + 48]
            total = jnp.where(which == first + a, both, total)
        out.append(total)
    return out


def halo_lhs(recv_one, recv_two):
    parts = [recv_one[:, s] for s in chunks(HALO)] + [recv_two[:, s] for s in chunks(HALO)]
    high, low = split(jnp.concatenate(parts, axis=0))
    return jnp.concatenate([high, low], axis=0)


def local_faces(traces, keys, hots, lanes, own_sign):
    width = traces.shape[1]
    blocks = width // CHUNK
    out = []
    for f in range(6):
        key = keys[f:f + 1]
        other = 48 * (f ^ 1)
        lhs = jnp.concatenate(
            [traces[p + other:p + other + 48, s] for p in (0, 288) for s in chunks(width)], axis=0
        )
        got = mm(lhs, hots[f, :, lanes])
        which = key >> 8
        own = traces[48 * f:48 * f + 48, lanes].astype(f32)
        own = own + traces[288 + 48 * f:288 + 48 * f + 48, lanes].astype(f32)
        total = jnp.where(which < 0, own_sign * own, 0.0)
        for a in range(blocks):
            both = got[48 * a:48 * a + 48] + got[48 * (blocks + a):48 * (blocks + a) + 48]
            total = jnp.where(which == a, both, total)
        out.append(total)
    return out


def put_traces(traces, lanes, comp, faces_x, picked):
    base = 16 * comp
    for f in range(2):
        for p in range(2):
            traces[288 * p + 48 * f + base:288 * p + 48 * f + base + 16, lanes] = faces_x[f][p]
    picked = picked.astype(bf16)
    for p in range(2):
        for f in range(4):
            at = 288 * p + 48 * (f + 2) + base
            traces[at:at + 16, lanes] = picked[64 * p + 16 * f:64 * p + 16 * f + 16]


def vel_traces(traces, lanes, velocity, pick):
    for i in range(3):
        high, low = split(velocity[i])
        picked = mm(pick, jnp.concatenate([high, low], axis=0))
        put_traces(traces, lanes, i, ((high[0:16], low[0:16]), (high[48:64], low[48:64])), picked)


def str_traces(traces, lanes, stress, pick):
    pieces = [split(s) for s in stress]
    for i in range(3):
        along_x, along_y, along_z = (pieces[m] for m in symmetric_index[i])
        picked = mm(pick, jnp.concatenate(along_y + along_z, axis=0))
        faces_x = (
            (along_x[0][0:16], along_x[1][0:16]),
            (along_x[0][48:64], along_x[1][48:64]),
        )
        put_traces(traces, lanes, i, faces_x, picked)


def pack(traces, picks, faces, send_one, send_two):
    for row, send in enumerate((send_one, send_two)):
        for s in chunks(HALO):
            face = faces[row:row + 1, s]
            got = mm(traces[...], picks[row, :, s])
            total = jnp.zeros((48, CHUNK), f32)
            for f in range(6):
                both = got[48 * f:48 * f + 48] + got[288 + 48 * f:288 + 48 * f + 48]
                total = jnp.where(face == f, both, total)
            send[:, s] = total


def rate_of(grad, lame, shear):
    trace = lame * (grad[0][0] + grad[1][1] + grad[2][2])
    return [
        trace + 2.0 * shear * grad[0][0],
        trace + 2.0 * shear * grad[1][1],
        trace + 2.0 * shear * grad[2][2],
        shear * (grad[0][1] + grad[1][0]),
        shear * (grad[0][2] + grad[2][0]),
        shear * (grad[1][2] + grad[2][1]),
    ]


def lift_velocity(plus, table):
    grad, jump = [], []
    for i in range(3):
        low_x, high_x, *rest = side_faces(plus, i)
        high, low = split(jnp.concatenate(rest, axis=0))
        put = mm(table, jnp.concatenate([high, low], axis=0))
        grad.append(
            (pad_x(-lift_half * low_x, lift_half * high_x), put[0:64], put[64:128])
        )
        jump.append(put[128:192] + pad_x(lift_half * low_x, lift_half * high_x))
    return grad, jump


def lift_stress(plus, table):
    out = []
    for i in range(3):
        low_x, high_x, *rest = side_faces(plus, i)
        high, low = split(jnp.concatenate(rest, axis=0))
        put = mm(table, jnp.concatenate([high, low], axis=0))
        out.append(put + pad_x(-lift_half * low_x, lift_half * high_x))
    return out


def start_kernel(
    odd, state_hbm, neighbour_hbm, send_list_hbm, pick_hbm,
    velocity, stress, keys, hots, picks, faces, traces, send_one, send_two,
    state, neighbour, send_list, pick, sems,
):
    copies = [
        pltpu.make_async_copy(source, target, sems.at[k])
        for k, (source, target) in enumerate((
            (neighbour_hbm, neighbour), (send_list_hbm, send_list), (pick_hbm, pick),
            (state_hbm.at[0:3], state.at[0:3]), (state_hbm.at[3:9], state.at[3:9]),
        ))
    ]
    for copy in copies:
        copy.start()
    for copy in copies[0:2]:
        copy.wait()
    width = neighbour.shape[1]
    cap = send_list.shape[1]
    is_odd = odd[0] == 1
    code = neighbour[...]
    low_base = jnp.where(is_odd, width, width + HALO)
    high_base = jnp.where(is_odd, width + HALO, width)
    keys[...] = jnp.where(
        code < width,
        code,
        jnp.where(code < width + cap, code - width + low_base, code - width - cap + high_base),
    )
    valid = jnp.where(jnp.max(code, axis=0, keepdims=True) >= 0, 1.0, 0.0)
    entries = send_list[...]
    entries = jnp.concatenate([entries, jnp.full((2, HALO - cap), -1, jnp.int32)], axis=1)
    entries = jnp.where(
        is_odd, entries, jnp.concatenate([entries[1:2], entries[0:1]], axis=0)
    )
    face = jnp.zeros_like(entries)
    for f in range(1, 6):
        face = face + jnp.where(entries >= f * width, 1, 0)
    faces[...] = face
    slots = entries - face * width
    for row in range(2):
        for s in chunks(HALO):
            picks[row, :, s] = onehot(slots[row:row + 1, s], width)
    for copy in copies[2:4]:
        copy.wait()
    for lanes in chunks(width):
        mask = valid[:, lanes]
        now = [state[i, :, lanes] * mask for i in range(3)]
        for i in range(3):
            velocity[i, :, lanes] = now[i]
        vel_traces(traces, lanes, now[0:3], pick[...])
    pack(traces, picks, faces, send_one, send_two)
    copies[4].wait()
    for lanes in chunks(width):
        for i in range(6):
            stress[i, :, lanes] = state[3 + i, :, lanes] * valid[:, lanes]
        for f in range(6):
            hots[f, :, lanes] = onehot(keys[f:f + 1, lanes] & (CHUNK - 1), CHUNK)


def vel_local_kernel(
    step, velocity, stress, traces, keys, hots, lame, shear, vel, lift, *rest,
):
    if len(rest) == 2:
        forward = total = total_out = None
        stress_out, jump_out = rest
    else:
        forward, total, stress_out, jump_out, total_out = rest
    width = velocity.shape[2]
    for lanes in chunks(width):
        plus = local_faces(traces, keys[:, lanes], hots, lanes, 1.0)
        grad, jump = lift_velocity(plus, lift[...])
        whole = []
        for i in range(3):
            high, low = split(velocity[i, :, lanes])
            got = mm(vel[...], jnp.concatenate([high, low, high], axis=0))
            whole.append([got[64 * j:64 * j + 64] + grad[i][j] for j in range(3)])
            jump_out[i, :, lanes] = got[192:256] + jump[i]
        rate = rate_of(whole, lame[:, lanes], shear[:, lanes])
        for m in range(6):
            stress_out[m, :, lanes] = stress[m, :, lanes] + time_step * rate[m]
        if total is not None:
            total_out[:, lanes] = total[:, lanes] + rho_term(forward, step, velocity, lanes)


def rho_term(forward, step, velocity, lanes):
    acc = forward[step, 0, :, lanes] * velocity[0, :, lanes]
    acc = acc + forward[step, 1, :, lanes] * velocity[1, :, lanes]
    acc = acc + forward[step, 2, :, lanes] * velocity[2, :, lanes]
    return -time_step * acc


def vel_halo_kernel(
    stress, jump, recv_one, recv_two, keys, hots, picks, faces, lame, shear, lift, pick,
    stress_out, jump_out, traces, send_one, send_two,
):
    width = stress.shape[2]
    lhs = halo_lhs(recv_one, recv_two)
    for lanes in chunks(width):
        plus = halo_faces(lhs, keys[:, lanes], hots, lanes, width)
        grad, more = lift_velocity(plus, lift[...])
        rate = rate_of(grad, lame[:, lanes], shear[:, lanes])
        now = [stress[m, :, lanes] + time_step * rate[m] for m in range(6)]
        for m in range(6):
            stress_out[m, :, lanes] = now[m]
        for i in range(3):
            jump_out[i, :, lanes] = jump[i, :, lanes] + more[i]
        str_traces(traces, lanes, now, pick[...])
    pack(traces, picks, faces, send_one, send_two)


def str_local_kernel(
    step, velocity, stress, jump, traces, keys, hots, density, lame, shear, forward, div, lift, fwd, *rest,
):
    if len(rest) == 2:
        total = None
        velocity_out, total_out = rest
    else:
        total, velocity_out, total_out = rest
    width = velocity.shape[2]
    for lanes in chunks(width):
        plus = local_faces(traces, keys[:, lanes], hots, lanes, -1.0)
        lifted = lift_stress(plus, lift[...])
        now = [stress[m, :, lanes] for m in range(6)]
        pieces = [split(s) for s in now]
        rho = density[:, lanes]
        impedance = jnp.sqrt(rho * (lame[:, lanes] + 2.0 * shear[:, lanes]))
        scale = time_step / rho
        for i in range(3):
            rows = []
            for m in symmetric_index[i]:
                rows += [pieces[m][0], pieces[m][1], pieces[m][0]]
            got = mm(div[...], jnp.concatenate(rows, axis=0))
            velocity_out[i, :, lanes] = velocity[i, :, lanes] + scale * (
                got + lifted[i] + impedance * jump[i, :, lanes]
            )
        grad = []
        for i in range(3):
            high, low = split(forward[step, i, :, lanes])
            got = mm(fwd[...], jnp.concatenate([high, low, high], axis=0))
            grad.append([got[64 * j:64 * j + 64] for j in range(3)])
        diag = (grad[0][0], grad[1][1], grad[2][2])
        lame_term = -time_step * (diag[0] + diag[1] + diag[2]) * (now[0] + now[1] + now[2])
        shear_term = (-2.0 * time_step) * (
            diag[0] * now[0]
            + diag[1] * now[1]
            + diag[2] * now[2]
            + (grad[0][1] + grad[1][0]) * now[3]
            + (grad[0][2] + grad[2][0]) * now[4]
            + (grad[1][2] + grad[2][1]) * now[5]
        )
        for m, term in enumerate((lame_term, shear_term)):
            rows = total_out.shape[2]
            for e in range(total_out.shape[0]):
                share = term[rows * e:rows * e + rows]
                if total is not None:
                    share = total[e, m, :, lanes] + share
                total_out[e, m, :, lanes] = share


def str_halo_kernel(
    velocity, recv_one, recv_two, keys, hots, picks, faces, density, lift, pick,
    velocity_out, traces, send_one, send_two,
):
    halo_velocity(velocity, recv_one, recv_two, keys, hots, density, lift, velocity_out, traces, pick)
    pack(traces, picks, faces, send_one, send_two)


def last_kernel(
    step, velocity, recv_one, recv_two, keys, hots, density, lift, forward, total, velocity_out, total_out
):
    halo_velocity(velocity, recv_one, recv_two, keys, hots, density, lift, velocity_out, None, None)
    for lanes in chunks(velocity.shape[2]):
        total_out[:, lanes] = total[:, lanes] + rho_term(forward, step, velocity_out, lanes)


def event_sum_kernel(other, rho, out):
    width = rho.shape[3]
    for m, (terms, at) in enumerate(((rho, 0), (other, 0), (other, 1))):
        total = terms[0, at]
        for e in range(1, terms.shape[0]):
            total = total + terms[e, at]
        for k in range(total.shape[0]):
            out[m, :, k * width:(k + 1) * width] = total[k:k + 1]


def halo_velocity(
    velocity, recv_one, recv_two, keys, hots, density, lift, velocity_out, traces, pick
):
    width = velocity.shape[2]
    lhs = halo_lhs(recv_one, recv_two)
    for lanes in chunks(width):
        plus = halo_faces(lhs, keys[:, lanes], hots, lanes, width)
        lifted = lift_stress(plus, lift[...])
        scale = time_step / density[:, lanes]
        now = [velocity[i, :, lanes] + scale * lifted[i] for i in range(3)]
        for i in range(3):
            velocity_out[i, :, lanes] = now[i]
        if traces is not None:
            vel_traces(traces, lanes, now, pick[...])


def call(name, kernel, args, outs, specs=None, cost=0, scratch=()):
    whole = pl.BlockSpec(memory_space=pltpu.VMEM)
    specs = specs or {}
    return pl.pallas_call(
        kernel,
        name=name,
        in_specs=[specs.get(k, whole) for k in range(len(args))],
        out_specs=[whole] * len(outs),
        out_shape=[jax.ShapeDtypeStruct(s, d) for s, d in outs],
        scratch_shapes=list(scratch),
        compiler_params=pltpu.CompilerParams(vmem_limit_bytes=VMEM_LIMIT),
        cost_estimate=pl.CostEstimate(flops=cost, bytes_accessed=6_000_000, transcendentals=0),
    )(*args)


def swap(sent, axis):
    count = lax.axis_size(axis)
    got = []
    for first, value in enumerate(sent):
        pairs = []
        for low in range(first, count - 1, 2):
            pairs += [(low, low + 1), (low + 1, low)]
        got.append(lax.ppermute(value, axis, pairs))
    return got


def local(
    adjoint_state, forward_velocity, density, lame_lambda, shear_modulus, neighbour, send_list
):
    width = density.shape[1]
    steps = forward_velocity.shape[1]
    table = {k: jnp.asarray(v) for k, v in tables().items()}
    state = adjoint_state[0]
    forward = forward_velocity[0]
    odd = (lax.axis_index("dom") % 2).astype(jnp.int32).reshape(1)

    field = ((64, width), f32)
    vector = ((3, 64, width), f32)
    tensor = ((6, 64, width), f32)
    count = lax.axis_size("event")
    shares = count if 64 % (8 * count) == 0 else 1
    two = ((shares, 2, 64 // shares, width), f32)
    trace = ((576, width), bf16)
    sends = [((48, HALO), f32)] * 2
    ints = [((6, width), jnp.int32), ((6, CHUNK, width), bf16), ((2, width, HALO), bf16),
            ((2, HALO), jnp.int32)]

    velocity, stress, keys, hots, picks, faces, traces, *sent = call(
        "start", start_kernel,
        (odd, *(pltpu.with_memory_space_constraint(x, pltpu.HBM)
                for x in (state, neighbour, send_list, table["pick_vel"]))),
        [vector, tensor] + ints + [trace] + sends,
        specs={0: pl.BlockSpec(memory_space=pltpu.SMEM)}
        | {k: pl.BlockSpec(memory_space=pltpu.HBM) for k in range(1, 5)},
        scratch=[
            pltpu.VMEM(state.shape, f32), pltpu.VMEM(neighbour.shape, jnp.int32),
            pltpu.VMEM(send_list.shape, jnp.int32), pltpu.VMEM((128, 128), bf16),
            pltpu.SemaphoreType.DMA((5,)),
        ],
    )
    rho_total = jnp.zeros(*field)
    other_total = None
    for n in range(steps):
        recv = swap(sent, "dom")
        args = [velocity, stress, traces, keys, hots, lame_lambda, shear_modulus,
                table["vel"], table["lift_vel"]]
        outs = [tensor, vector]
        if n:
            args += [forward, rho_total]
            outs += [field]
        stress, jump, *more = call(
            "vel_local", functools.partial(vel_local_kernel, n - 1), args, outs, cost=4_000_000_000
        )
        if more:
            rho_total = more[0]
        stress, jump, traces, *sent = call(
            "vel_halo", vel_halo_kernel,
            (stress, jump, *recv, keys, hots, picks, faces, lame_lambda, shear_modulus,
             table["lift_vel"], table["pick_str"]),
            [tensor, vector, trace] + sends,
        )
        recv = swap(sent, "dom")
        args = [velocity, stress, jump, traces, keys, hots, density, lame_lambda, shear_modulus,
                forward, table["div"], table["lift_str"], table["fwd"]]
        if n:
            args += [other_total]
        velocity, other_total = call(
            "str_local", functools.partial(str_local_kernel, n), args, [vector, two],
            cost=4_000_000_000,
        )
        if n < steps - 1:
            velocity, traces, *sent = call(
                "str_halo", str_halo_kernel,
                (velocity, *recv, keys, hots, picks, faces, density, table["lift_str"],
                 table["pick_vel"]),
                [vector, trace] + sends,
            )
        else:
            *recv, other_total = lax.optimization_barrier((*recv, other_total))
            velocity, rho_total = call(
                "last", functools.partial(last_kernel, n),
                (velocity, *recv, keys, hots, density, table["lift_str"], forward, rho_total),
                [vector, field],
            )

    if shares == count:
        parts = [
            lax.all_to_all(value, "event", 0, 0, tiled=True)
            for value in (other_total, rho_total.reshape(count, 1, 64 // count, width))
        ]
        kernels, = call(
            "event_sum", event_sum_kernel, parts, [((3, 1, 64 // count * width), f32)]
        )
    else:
        flat = jnp.concatenate([rho_total[None], other_total[0]], axis=0).reshape(3, -1)
        part = lax.psum_scatter(flat, "event", scatter_dimension=1, tiled=True)
        kernels = part.reshape(3, 1, -1)
    return velocity[None], kernels


def solution(mesh):
    placed = (
        P("event", None, None, "dom"),
        P("event", None, None, None, "dom"),
        P(None, "dom"),
        P(None, "dom"),
        P(None, "dom"),
        P(None, "dom"),
        P(None, "dom"),
    )
    return jax.shard_map(
        local,
        mesh=mesh,
        in_specs=placed,
        out_specs=(P("event", None, None, "dom"), P(None, "dom", "event")),
        check_vma=False,
    )
```

```python
import functools
import math

import jax
import jax.numpy as jnp
import numpy as np
from jax import lax
from jax.experimental import pallas as pl
from jax.experimental.pallas import tpu as pltpu
from jax.sharding import PartitionSpec as P

time_step = 0.02
lift_half = 3.0
symmetric_index = ((0, 3, 4), (3, 1, 5), (4, 5, 2))
f32 = jnp.float32
bf16 = jnp.bfloat16
CHUNK = 256
MAIN = 384
TAIL = 64
HALO = 512
VMEM_LIMIT = 40 * 2**20


def lobatto_diff():
    points = [-1.0, -1.0 / math.sqrt(5.0), 1.0 / math.sqrt(5.0), 1.0]
    weights = [
        1.0 / math.prod([points[t] - points[o] for o in range(4) if o != t]) for t in range(4)
    ]
    offdiag = [
        [
            0.0 if t == s else weights[s] / weights[t] / (points[t] - points[s])
            for s in range(4)
        ]
        for t in range(4)
    ]
    return np.array(
        [[-sum(offdiag[t]) if t == s else offdiag[t][s] for s in range(4)] for t in range(4)],
        dtype=np.float64,
    )


def kron3(first, second, third):
    return np.kron(np.kron(first, second), third)


def deriv_parts(inner):
    matrix = lobatto_diff()
    if inner:
        matrix = matrix + np.diag([lift_half, 0.0, 0.0, -lift_half])
    matrix = matrix.astype(np.float32)
    eye = np.eye(4, dtype=np.float32)
    stack = [kron3(matrix, eye, eye), kron3(eye, matrix, eye), kron3(eye, eye, matrix)]
    high = [np.asarray(m.astype(bf16)) for m in stack]
    low = [np.asarray((m - h.astype(np.float32)).astype(bf16)) for m, h in zip(stack, high)]
    return [h.astype(np.float32) for h in high], [l.astype(np.float32) for l in low]


def face_rows(face):
    rows = np.zeros((16, 64), np.float32)
    for q in range(16):
        at = [q // 4, q % 4]
        at.insert(face // 2, 3 * (face % 2))
        rows[q, 16 * at[0] + 4 * at[1] + at[2]] = 1.0
    return rows


def tables():
    high, low = deriv_parts(True)
    plain_high, plain_low = deriv_parts(False)
    zero = np.zeros((64, 64), np.float32)
    picks = [face_rows(f) for f in range(6)]
    holders = np.diag(sum(p.sum(axis=0) for p in picks))
    vel = np.concatenate(
        [np.concatenate([high[j], high[j], low[j]], axis=1) for j in range(3)]
        + [np.concatenate([-lift_half * holders, -lift_half * holders, zero], axis=1)],
        axis=0,
    )
    fwd = np.concatenate(
        [np.concatenate([plain_high[j], plain_high[j], plain_low[j]], axis=1) for j in range(3)],
        axis=0,
    )
    div = np.concatenate([m for j in range(3) for m in (high[j], high[j], low[j])], axis=1)
    side = np.concatenate(picks[2:4], axis=0)
    ends = np.concatenate(picks[4:6], axis=0)
    none = np.zeros((32, 64), np.float32)
    yz = np.concatenate([side, ends], axis=0)
    pick_vel = np.concatenate(
        [np.concatenate([yz, zero], axis=1), np.concatenate([zero, yz], axis=1)], axis=0
    )
    pick_str = np.concatenate(
        [
            np.concatenate([side, none, none, none], axis=1),
            np.concatenate([none, none, ends, none], axis=1),
            np.concatenate([none, side, none, none], axis=1),
            np.concatenate([none, none, none, ends], axis=1),
        ],
        axis=0,
    )
    signs = np.where(np.arange(64) // 16 % 2 == 1, 1.0, -1.0).astype(np.float32)
    put = lift_half * yz.T
    normal = put * signs[None]
    in_y = (np.arange(64) < 32).astype(np.float32)[None]
    gy, gz = normal * in_y, normal * (1.0 - in_y)
    lift_vel = np.concatenate([np.concatenate([m, m], axis=1) for m in (gy, gz, put)], axis=0)
    lift_str = np.concatenate([normal, normal], axis=1)
    return {
        name: np.asarray(value).astype(bf16)
        for name, value in dict(
            vel=vel, fwd=fwd, div=div, pick_vel=pick_vel, pick_str=pick_str,
            lift_vel=lift_vel, lift_str=lift_str,
        ).items()
    }


def split(value):
    high = value.astype(bf16)
    return high, (value - high.astype(f32)).astype(bf16)


def mm(left, right):
    return jnp.dot(left, right, preferred_element_type=f32)


def onehot(row, depth):
    ids = lax.broadcasted_iota(jnp.int32, (depth, row.shape[-1]), 0)
    return jnp.where(ids == row, 1.0, 0.0).astype(bf16)


def chunks(width):
    return [slice(c, c + CHUNK) for c in range(0, width, CHUNK)]


def side_faces(plus, comp):
    return [plus[f][16 * comp:16 * comp + 16] for f in range(6)]


def pad_x(first, last):
    return jnp.concatenate([first, jnp.zeros((32,) + first.shape[1:], f32), last], axis=0)


def gather_tile(source, lane):
    lane = jnp.broadcast_to(lane, (8, 128))
    return jnp.concatenate(
        [jnp.take_along_axis(source[r:r + 8], lane, axis=1) for r in range(0, 48, 8)], axis=0
    )


def halo_faces(lhs, tail, keys, hots, lanes, width):
    blocks = 2 * MAIN // CHUNK
    first = width // CHUNK
    out = []
    for f in range(6):
        key = keys[f:f + 1]
        got = mm(lhs, hots[f, :, lanes])
        which = key >> 8
        late = jnp.concatenate(
            [gather_tile(tail, key[:, t:t + 128] & 127) for t in range(0, CHUNK, 128)], axis=1
        )
        total = jnp.where(which == first + blocks, late, 0.0)
        for a in range(blocks):
            both = got[48 * a:48 * a + 48] + got[48 * (blocks + a):48 * (blocks + a) + 48]
            total = jnp.where(which == first + a, both, total)
        out.append(total)
    return out


def halo_lhs(recv_one, recv_two):
    whole = jnp.concatenate([recv_one[:, 0:MAIN], recv_two[:, 0:MAIN]], axis=1)
    high, low = split(jnp.concatenate([whole[:, s] for s in chunks(2 * MAIN)], axis=0))
    tail = jnp.concatenate(
        [recv_one[:, MAIN:MAIN + TAIL], recv_two[:, MAIN:MAIN + TAIL]], axis=1
    )
    return jnp.concatenate([high, low], axis=0), tail


def local_faces(traces, keys, hots, lanes, own_sign):
    width = traces.shape[1]
    blocks = width // CHUNK
    out = []
    for f in range(6):
        key = keys[f:f + 1]
        other = 48 * (f ^ 1)
        lhs = jnp.concatenate(
            [traces[p + other:p + other + 48, s] for p in (0, 288) for s in chunks(width)], axis=0
        )
        got = mm(lhs, hots[f, :, lanes])
        which = key >> 8
        own = traces[48 * f:48 * f + 48, lanes].astype(f32)
        own = own + traces[288 + 48 * f:288 + 48 * f + 48, lanes].astype(f32)
        total = jnp.where(which < 0, own_sign * own, 0.0)
        for a in range(blocks):
            both = got[48 * a:48 * a + 48] + got[48 * (blocks + a):48 * (blocks + a) + 48]
            total = jnp.where(which == a, both, total)
        out.append(total)
    return out


def put_traces(traces, lanes, comp, faces_x, picked):
    base = 16 * comp
    for f in range(2):
        for p in range(2):
            traces[288 * p + 48 * f + base:288 * p + 48 * f + base + 16, lanes] = faces_x[f][p]
    picked = picked.astype(bf16)
    for p in range(2):
        for f in range(4):
            at = 288 * p + 48 * (f + 2) + base
            traces[at:at + 16, lanes] = picked[64 * p + 16 * f:64 * p + 16 * f + 16]


def vel_traces(traces, lanes, velocity, pick):
    for i in range(3):
        high, low = split(velocity[i])
        picked = mm(pick, jnp.concatenate([high, low], axis=0))
        put_traces(traces, lanes, i, ((high[0:16], low[0:16]), (high[48:64], low[48:64])), picked)


def str_traces(traces, lanes, stress, pick):
    pieces = [split(s) for s in stress]
    for i in range(3):
        along_x, along_y, along_z = (pieces[m] for m in symmetric_index[i])
        picked = mm(pick, jnp.concatenate(along_y + along_z, axis=0))
        faces_x = (
            (along_x[0][0:16], along_x[1][0:16]),
            (along_x[0][48:64], along_x[1][48:64]),
        )
        put_traces(traces, lanes, i, faces_x, picked)


def pack(traces, values, picks, faces, late, send_one, send_two):
    width = traces.shape[1]
    pieces = []
    for s in chunks(2 * MAIN):
        face = faces[:, s]
        got = mm(traces[...], picks[:, s])
        total = jnp.zeros((48, CHUNK), f32)
        for f in range(6):
            both = got[48 * f:48 * f + 48] + got[288 + 48 * f:288 + 48 * f + 48]
            total = jnp.where(face == f, both, total)
        pieces.append(total)
    whole = jnp.concatenate(pieces, axis=1)
    send_one[:, 0:MAIN] = whole[:, 0:MAIN]
    send_two[:, 0:MAIN] = whole[:, MAIN:2 * MAIN]
    for at in range(0, 288, 16):
        values[at:at + 16] = (
            traces[at:at + 16].astype(f32) + traces[288 + at:288 + at + 16].astype(f32)
        )
    key = late[...]
    lane = key & 127
    which = jnp.broadcast_to(key >> 7, (48, 128))
    total = jnp.zeros((48, 128), f32)
    for f in range(6):
        for a in range(width // 128):
            got = gather_tile(values[48 * f:48 * f + 48, 128 * a:128 * a + 128], lane)
            total = jnp.where(which == f * (width // 128) + a, got, total)
    none = jnp.zeros((48, HALO - MAIN - TAIL), f32)
    send_one[:, MAIN:HALO] = jnp.concatenate([total[:, 0:TAIL], none], axis=1)
    send_two[:, MAIN:HALO] = jnp.concatenate([total[:, TAIL:2 * TAIL], none], axis=1)


def rate_of(grad, lame, shear):
    trace = lame * (grad[0][0] + grad[1][1] + grad[2][2])
    return [
        trace + 2.0 * shear * grad[0][0],
        trace + 2.0 * shear * grad[1][1],
        trace + 2.0 * shear * grad[2][2],
        shear * (grad[0][1] + grad[1][0]),
        shear * (grad[0][2] + grad[2][0]),
        shear * (grad[1][2] + grad[2][1]),
    ]


def lift_velocity(plus, table):
    grad, jump = [], []
    for i in range(3):
        low_x, high_x, *rest = side_faces(plus, i)
        high, low = split(jnp.concatenate(rest, axis=0))
        put = mm(table, jnp.concatenate([high, low], axis=0))
        grad.append(
            (pad_x(-lift_half * low_x, lift_half * high_x), put[0:64], put[64:128])
        )
        jump.append(put[128:192] + pad_x(lift_half * low_x, lift_half * high_x))
    return grad, jump


def lift_stress(plus, table):
    out = []
    for i in range(3):
        low_x, high_x, *rest = side_faces(plus, i)
        high, low = split(jnp.concatenate(rest, axis=0))
        put = mm(table, jnp.concatenate([high, low], axis=0))
        out.append(put + pad_x(-lift_half * low_x, lift_half * high_x))
    return out


def start_kernel(
    even, state_hbm, neighbour_hbm, send_list_hbm, pick_hbm,
    velocity, stress, keys, picks, faces, late, traces, send_one, send_two,
    state, neighbour, send_list, pick, values, sems,
):
    copies = [
        pltpu.make_async_copy(source, target, sems.at[k])
        for k, (source, target) in enumerate((
            (neighbour_hbm, neighbour), (send_list_hbm, send_list), (pick_hbm, pick),
            (state_hbm.at[0:3], state.at[0:3]), (state_hbm.at[3:9], state.at[3:9]),
        ))
    ]
    for copy in copies:
        copy.start()
    for copy in copies[0:2]:
        copy.wait()
    width = neighbour.shape[1]
    cap = send_list.shape[1]
    is_even = even[0] == 1
    code = neighbour[...]
    low = code < width + cap
    at = code - width - jnp.where(low, 0, cap)
    second = jnp.where(low == is_even, 0, 1)
    place = jnp.where(
        at < MAIN, at + MAIN * second, at - MAIN + 2 * MAIN + TAIL * second
    )
    keys[...] = jnp.where(code < width, code, width + place)
    valid = jnp.where(jnp.max(code, axis=0, keepdims=True) >= 0, 1.0, 0.0)
    entries = send_list[...]
    entries = jnp.concatenate(
        [entries, jnp.full((2, MAIN + TAIL - cap), -1, jnp.int32)], axis=1
    )
    one, two = entries[0:1], entries[1:2]
    one, two = jnp.where(is_even, one, two), jnp.where(is_even, two, one)
    late[...] = jnp.concatenate([one[:, MAIN:], two[:, MAIN:]], axis=1)
    main = jnp.concatenate([one[:, 0:MAIN], two[:, 0:MAIN]], axis=1)
    face = jnp.zeros_like(main)
    for f in range(1, 6):
        face = face + jnp.where(main >= f * width, 1, 0)
    faces[...] = face
    slots = main - face * width
    for s in chunks(2 * MAIN):
        picks[:, s] = onehot(slots[:, s], width)
    for copy in copies[2:4]:
        copy.wait()
    for lanes in chunks(width):
        mask = valid[:, lanes]
        now = [state[i, :, lanes] * mask for i in range(3)]
        for i in range(3):
            velocity[i, :, lanes] = now[i]
        vel_traces(traces, lanes, now[0:3], pick[...])
    pack(traces, values, picks, faces, late, send_one, send_two)
    copies[4].wait()
    for lanes in chunks(width):
        for i in range(6):
            stress[i, :, lanes] = state[3 + i, :, lanes] * valid[:, lanes]


def vel_local_kernel(
    step, velocity, stress, traces, keys, lame, shear, vel, lift, *rest,
):
    total = None
    if step < 0:
        stress_out, jump_out, hots = rest
    elif step == 0:
        hots, forward, stress_out, jump_out, total_out = rest
    else:
        hots, forward, total, stress_out, jump_out, total_out = rest
    width = velocity.shape[2]
    for lanes in chunks(width):
        if step < 0:
            for f in range(6):
                hots[f, :, lanes] = onehot(keys[f:f + 1, lanes] & (CHUNK - 1), CHUNK)
        plus = local_faces(traces, keys[:, lanes], hots, lanes, 1.0)
        grad, jump = lift_velocity(plus, lift[...])
        whole = []
        for i in range(3):
            high, low = split(velocity[i, :, lanes])
            got = mm(vel[...], jnp.concatenate([high, low, high], axis=0))
            whole.append([got[64 * j:64 * j + 64] + grad[i][j] for j in range(3)])
            jump_out[i, :, lanes] = got[192:256] + jump[i]
        rate = rate_of(whole, lame[:, lanes], shear[:, lanes])
        for m in range(6):
            stress_out[m, :, lanes] = stress[m, :, lanes] + time_step * rate[m]
        if step >= 0:
            term = rho_term(forward, step, velocity, lanes)
            total_out[:, lanes] = term if total is None else total[:, lanes] + term


def rho_term(forward, step, velocity, lanes):
    acc = forward[step, 0, :, lanes] * velocity[0, :, lanes]
    acc = acc + forward[step, 1, :, lanes] * velocity[1, :, lanes]
    acc = acc + forward[step, 2, :, lanes] * velocity[2, :, lanes]
    return -time_step * acc


def vel_halo_kernel(
    stress, jump, recv_one, recv_two, keys, hots, picks, faces, late, lame, shear, lift, pick,
    stress_out, jump_out, traces, send_one, send_two, values,
):
    width = stress.shape[2]
    lhs, tail = halo_lhs(recv_one, recv_two)
    for lanes in chunks(width):
        plus = halo_faces(lhs, tail, keys[:, lanes], hots, lanes, width)
        grad, more = lift_velocity(plus, lift[...])
        rate = rate_of(grad, lame[:, lanes], shear[:, lanes])
        now = [stress[m, :, lanes] + time_step * rate[m] for m in range(6)]
        for m in range(6):
            stress_out[m, :, lanes] = now[m]
        for i in range(3):
            jump_out[i, :, lanes] = jump[i, :, lanes] + more[i]
        str_traces(traces, lanes, now, pick[...])
    pack(traces, values, picks, faces, late, send_one, send_two)


def str_local_kernel(
    step, velocity, stress, jump, traces, keys, hots, density, lame, shear, forward, div, lift, fwd, *rest,
):
    if len(rest) == 2:
        total = None
        velocity_out, total_out = rest
    else:
        total, velocity_out, total_out = rest
    width = velocity.shape[2]
    for lanes in chunks(width):
        plus = local_faces(traces, keys[:, lanes], hots, lanes, -1.0)
        lifted = lift_stress(plus, lift[...])
        now = [stress[m, :, lanes] for m in range(6)]
        pieces = [split(s) for s in now]
        rho = density[:, lanes]
        impedance = jnp.sqrt(rho * (lame[:, lanes] + 2.0 * shear[:, lanes]))
        scale = time_step / rho
        for i in range(3):
            rows = []
            for m in symmetric_index[i]:
                rows += [pieces[m][0], pieces[m][1], pieces[m][0]]
            got = mm(div[...], jnp.concatenate(rows, axis=0))
            velocity_out[i, :, lanes] = velocity[i, :, lanes] + scale * (
                got + lifted[i] + impedance * jump[i, :, lanes]
            )
        grad = []
        for i in range(3):
            high, low = split(forward[step, i, :, lanes])
            got = mm(fwd[...], jnp.concatenate([high, low, high], axis=0))
            grad.append([got[64 * j:64 * j + 64] for j in range(3)])
        diag = (grad[0][0], grad[1][1], grad[2][2])
        lame_term = -time_step * (diag[0] + diag[1] + diag[2]) * (now[0] + now[1] + now[2])
        shear_term = (-2.0 * time_step) * (
            diag[0] * now[0]
            + diag[1] * now[1]
            + diag[2] * now[2]
            + (grad[0][1] + grad[1][0]) * now[3]
            + (grad[0][2] + grad[2][0]) * now[4]
            + (grad[1][2] + grad[2][1]) * now[5]
        )
        for m, term in enumerate((lame_term, shear_term)):
            rows = total_out.shape[2]
            for e in range(total_out.shape[0]):
                share = term[rows * e:rows * e + rows]
                if total is not None:
                    share = total[e, m, :, lanes] + share
                total_out[e, m, :, lanes] = share


def str_halo_kernel(
    velocity, recv_one, recv_two, keys, hots, picks, faces, late, density, lift, pick,
    velocity_out, traces, send_one, send_two, values,
):
    halo_velocity(velocity, recv_one, recv_two, keys, hots, density, lift, velocity_out, traces, pick)
    pack(traces, values, picks, faces, late, send_one, send_two)


def last_kernel(
    step, velocity, recv_one, recv_two, keys, hots, density, lift, forward, other, *rest
):
    *total, velocity_out, total_out = rest
    total = total[0] if total else None
    halo_velocity(velocity, recv_one, recv_two, keys, hots, density, lift, velocity_out, None, None)
    for lanes in chunks(velocity.shape[2]):
        term = rho_term(forward, step, velocity_out, lanes)
        if total is not None:
            term = total[:, lanes] + term
        rows = total_out.shape[2]
        for e in range(total_out.shape[0]):
            total_out[e, 0, :, lanes] = term[rows * e:rows * e + rows]
            for m in range(2):
                total_out[e, m + 1, :, lanes] = other[e, m, :, lanes]


def event_sum_kernel(parts, out):
    width = parts.shape[3]
    for m in range(3):
        total = parts[0, m]
        for e in range(1, parts.shape[0]):
            total = total + parts[e, m]
        for k in range(total.shape[0]):
            out[m, :, k * width:(k + 1) * width] = total[k:k + 1]


def halo_velocity(
    velocity, recv_one, recv_two, keys, hots, density, lift, velocity_out, traces, pick
):
    width = velocity.shape[2]
    lhs, tail = halo_lhs(recv_one, recv_two)
    for lanes in chunks(width):
        plus = halo_faces(lhs, tail, keys[:, lanes], hots, lanes, width)
        lifted = lift_stress(plus, lift[...])
        scale = time_step / density[:, lanes]
        now = [velocity[i, :, lanes] + scale * lifted[i] for i in range(3)]
        for i in range(3):
            velocity_out[i, :, lanes] = now[i]
        if traces is not None:
            vel_traces(traces, lanes, now, pick[...])


def call(name, kernel, args, outs, specs=None, cost=0, scratch=()):
    whole = pl.BlockSpec(memory_space=pltpu.VMEM)
    specs = specs or {}
    return pl.pallas_call(
        kernel,
        name=name,
        in_specs=[specs.get(k, whole) for k in range(len(args))],
        out_specs=[whole] * len(outs),
        out_shape=[jax.ShapeDtypeStruct(s, d) for s, d in outs],
        scratch_shapes=list(scratch),
        compiler_params=pltpu.CompilerParams(vmem_limit_bytes=VMEM_LIMIT),
        cost_estimate=pl.CostEstimate(flops=cost, bytes_accessed=6_000_000, transcendentals=0),
    )(*args)


def swap(sent, axis):
    count = lax.axis_size(axis)
    got = []
    for first, value in enumerate(sent):
        pairs = []
        for low in range(1 - first, count - 1, 2):
            pairs += [(low, low + 1), (low + 1, low)]
        got.append(lax.ppermute(value, axis, pairs))
    return got


def local(
    adjoint_state, forward_velocity, density, lame_lambda, shear_modulus, neighbour, send_list
):
    width = density.shape[1]
    steps = forward_velocity.shape[1]
    table = {k: jnp.asarray(v) for k, v in tables().items()}
    state = adjoint_state[0]
    forward = forward_velocity[0]
    even = (1 - lax.axis_index("dom") % 2).astype(jnp.int32).reshape(1)

    values = pltpu.VMEM((288, width), f32)
    field = ((64, width), f32)
    vector = ((3, 64, width), f32)
    tensor = ((6, 64, width), f32)
    count = lax.axis_size("event")
    shares = count if 64 % (8 * count) == 0 else 1
    two = ((shares, 2, 64 // shares, width), f32)
    three = ((shares, 3, 64 // shares, width), f32)
    trace = ((576, width), bf16)
    hot = ((6, CHUNK, width), bf16)
    sends = [((48, HALO), f32)] * 2
    lists = [((6, width), jnp.int32), ((width, 2 * MAIN), bf16),
             ((1, 2 * MAIN), jnp.int32), ((1, 2 * TAIL), jnp.int32)]

    velocity, stress, keys, picks, faces, late, traces, *sent = call(
        "start", start_kernel,
        (even, *(pltpu.with_memory_space_constraint(x, pltpu.HBM)
                for x in (state, neighbour, send_list, table["pick_vel"]))),
        [vector, tensor] + lists + [trace] + sends,
        specs={0: pl.BlockSpec(memory_space=pltpu.SMEM)}
        | {k: pl.BlockSpec(memory_space=pltpu.HBM) for k in range(1, 5)},
        scratch=[
            pltpu.VMEM(state.shape, f32), pltpu.VMEM(neighbour.shape, jnp.int32),
            pltpu.VMEM(send_list.shape, jnp.int32), pltpu.VMEM((128, 128), bf16),
            values,
            pltpu.SemaphoreType.DMA((5,)),
        ],
    )
    rho_total = other_total = hots = None
    for n in range(steps):
        recv = swap(sent, "dom")
        args = [velocity, stress, traces, keys, lame_lambda, shear_modulus,
                table["vel"], table["lift_vel"]]
        outs = [tensor, vector]
        if n:
            args += [hots, forward] + ([rho_total] if n > 1 else [])
            outs += [field]
        else:
            outs += [hot]
        stress, jump, more = call(
            "vel_local", functools.partial(vel_local_kernel, n - 1), args, outs, cost=4_000_000_000
        )
        if n:
            rho_total = more
        else:
            hots = more
        stress, jump, traces, *sent = call(
            "vel_halo", vel_halo_kernel,
            (stress, jump, *recv, keys, hots, picks, faces, late, lame_lambda, shear_modulus,
             table["lift_vel"], table["pick_str"]),
            [tensor, vector, trace] + sends, scratch=[values],
        )
        recv = swap(sent, "dom")
        args = [velocity, stress, jump, traces, keys, hots, density, lame_lambda, shear_modulus,
                forward, table["div"], table["lift_str"], table["fwd"]]
        if n:
            args += [other_total]
        velocity, other_total = call(
            "str_local", functools.partial(str_local_kernel, n), args, [vector, two],
            cost=4_000_000_000,
        )
        if n < steps - 1:
            velocity, traces, *sent = call(
                "str_halo", str_halo_kernel,
                (velocity, *recv, keys, hots, picks, faces, late, density, table["lift_str"],
                 table["pick_vel"]),
                [vector, trace] + sends, scratch=[values],
            )
        else:
            velocity, kernel_total = call(
                "last", functools.partial(last_kernel, n),
                (velocity, *recv, keys, hots, density, table["lift_str"], forward, other_total)
                + ((rho_total,) if n else ()),
                [vector, three],
            )

    if shares == count:
        parts = lax.all_to_all(kernel_total, "event", 0, 0, tiled=True)
        kernels, = call(
            "event_sum", event_sum_kernel, (parts,), [((3, 1, 64 // count * width), f32)]
        )
    else:
        flat = kernel_total.reshape(3, -1)
        part = lax.psum_scatter(flat, "event", scatter_dimension=1, tiled=True)
        kernels = part.reshape(3, 1, -1)
    return velocity[None], kernels


def solution(mesh):
    placed = (
        P("event", None, None, "dom"),
        P("event", None, None, None, "dom"),
        P(None, "dom"),
        P(None, "dom"),
        P(None, "dom"),
        P(None, "dom"),
        P(None, "dom"),
    )
    return jax.shard_map(
        local,
        mesh=mesh,
        in_specs=placed,
        out_specs=(P("event", None, None, "dom"), P(None, "dom", "event")),
        check_vma=False,
    )
```

```python
import functools
import math

import jax
import jax.numpy as jnp
import numpy as np
from jax import lax
from jax.experimental import pallas as pl
from jax.experimental.pallas import tpu as pltpu
from jax.sharding import PartitionSpec as P

time_step = 0.02
lift_half = 3.0
symmetric_index = ((0, 3, 4), (3, 1, 5), (4, 5, 2))
f32 = jnp.float32
bf16 = jnp.bfloat16
CHUNK = 256
MAIN = 384
TAIL = 64
HALO = 512
VMEM_LIMIT = 40 * 2**20


def lobatto_diff():
    points = [-1.0, -1.0 / math.sqrt(5.0), 1.0 / math.sqrt(5.0), 1.0]
    weights = [
        1.0 / math.prod([points[t] - points[o] for o in range(4) if o != t]) for t in range(4)
    ]
    offdiag = [
        [
            0.0 if t == s else weights[s] / weights[t] / (points[t] - points[s])
            for s in range(4)
        ]
        for t in range(4)
    ]
    return np.array(
        [[-sum(offdiag[t]) if t == s else offdiag[t][s] for s in range(4)] for t in range(4)],
        dtype=np.float64,
    )


def kron3(first, second, third):
    return np.kron(np.kron(first, second), third)


def deriv_parts(inner):
    matrix = lobatto_diff()
    if inner:
        matrix = matrix + np.diag([lift_half, 0.0, 0.0, -lift_half])
    matrix = matrix.astype(np.float32)
    eye = np.eye(4, dtype=np.float32)
    stack = [kron3(matrix, eye, eye), kron3(eye, matrix, eye), kron3(eye, eye, matrix)]
    high = [np.asarray(m.astype(bf16)) for m in stack]
    low = [np.asarray((m - h.astype(np.float32)).astype(bf16)) for m, h in zip(stack, high)]
    return [h.astype(np.float32) for h in high], [l.astype(np.float32) for l in low]


def face_rows(face):
    rows = np.zeros((16, 64), np.float32)
    for q in range(16):
        at = [q // 4, q % 4]
        at.insert(face // 2, 3 * (face % 2))
        rows[q, 16 * at[0] + 4 * at[1] + at[2]] = 1.0
    return rows


def tables():
    high, low = deriv_parts(True)
    plain_high, plain_low = deriv_parts(False)
    zero = np.zeros((64, 64), np.float32)
    picks = [face_rows(f) for f in range(6)]
    holders = np.diag(sum(p.sum(axis=0) for p in picks))
    vel = np.concatenate(
        [np.concatenate([high[j], high[j], low[j]], axis=1) for j in range(3)]
        + [np.concatenate([-lift_half * holders, -lift_half * holders, zero], axis=1)],
        axis=0,
    )
    fwd = np.concatenate(
        [np.concatenate([plain_high[j], plain_high[j], plain_low[j]], axis=1) for j in range(3)],
        axis=0,
    )
    div = np.concatenate([m for j in range(3) for m in (high[j], high[j], low[j])], axis=1)
    side = np.concatenate(picks[2:4], axis=0)
    ends = np.concatenate(picks[4:6], axis=0)
    none = np.zeros((32, 64), np.float32)
    yz = np.concatenate([side, ends], axis=0)
    pick_vel = np.concatenate(
        [np.concatenate([yz, zero], axis=1), np.concatenate([zero, yz], axis=1)], axis=0
    )
    pick_str = np.concatenate(
        [
            np.concatenate([side, none, none, none], axis=1),
            np.concatenate([none, none, ends, none], axis=1),
            np.concatenate([none, side, none, none], axis=1),
            np.concatenate([none, none, none, ends], axis=1),
        ],
        axis=0,
    )
    signs = np.where(np.arange(64) // 16 % 2 == 1, 1.0, -1.0).astype(np.float32)
    put = lift_half * yz.T
    normal = put * signs[None]
    in_y = (np.arange(64) < 32).astype(np.float32)[None]
    gy, gz = normal * in_y, normal * (1.0 - in_y)
    lift_vel = np.concatenate([np.concatenate([m, m], axis=1) for m in (gy, gz, put)], axis=0)
    lift_str = np.concatenate([normal, normal], axis=1)
    return {
        name: np.asarray(value).astype(bf16)
        for name, value in dict(
            vel=vel, fwd=fwd, div=div, pick_vel=pick_vel, pick_str=pick_str,
            lift_vel=lift_vel, lift_str=lift_str,
        ).items()
    }


def split(value):
    high = value.astype(bf16)
    return high, (value - high.astype(f32)).astype(bf16)


def mm(left, right):
    return jnp.dot(left, right, preferred_element_type=f32)


def onehot(row, depth):
    ids = lax.broadcasted_iota(jnp.int32, (depth, row.shape[-1]), 0)
    return jnp.where(ids == row, 1.0, 0.0).astype(bf16)


def chunks(width):
    return [slice(c, c + CHUNK) for c in range(0, width, CHUNK)]


def each_chunk(width, body):
    def step(c, carry):
        body(pl.ds(pl.multiple_of(c * CHUNK, CHUNK), CHUNK))
        return carry

    lax.fori_loop(0, width // CHUNK, step, 0)


def side_faces(plus, comp):
    return [plus[f][16 * comp:16 * comp + 16] for f in range(6)]


def pad_x(first, last):
    return jnp.concatenate([first, jnp.zeros((32,) + first.shape[1:], f32), last], axis=0)


def gather_tile(source, lane):
    lane = jnp.broadcast_to(lane, (8, 128))
    return jnp.concatenate(
        [jnp.take_along_axis(source[r:r + 8], lane, axis=1) for r in range(0, 48, 8)], axis=0
    )


def halo_faces(lhs, tail, keys, hots, lanes, width):
    blocks = 2 * MAIN // CHUNK
    first = width // CHUNK
    out = []
    for f in range(6):
        key = keys[f:f + 1]
        got = mm(lhs, hots[f, :, lanes])
        which = key >> 8
        late = jnp.concatenate(
            [gather_tile(tail, key[:, t:t + 128] & 127) for t in range(0, CHUNK, 128)], axis=1
        )
        total = jnp.where(which == first + blocks, late, 0.0)
        for a in range(blocks):
            both = got[48 * a:48 * a + 48] + got[48 * (blocks + a):48 * (blocks + a) + 48]
            total = jnp.where(which == first + a, both, total)
        out.append(total)
    return out


def halo_lhs(recv_one, recv_two):
    whole = jnp.concatenate([recv_one[:, 0:MAIN], recv_two[:, 0:MAIN]], axis=1)
    high, low = split(jnp.concatenate([whole[:, s] for s in chunks(2 * MAIN)], axis=0))
    tail = jnp.concatenate(
        [recv_one[:, MAIN:MAIN + TAIL], recv_two[:, MAIN:MAIN + TAIL]], axis=1
    )
    return jnp.concatenate([high, low], axis=0), tail


def local_faces(traces, keys, hots, lanes, own_sign):
    width = traces.shape[1]
    blocks = width // CHUNK
    out = []
    for f in range(6):
        key = keys[f:f + 1]
        other = 48 * (f ^ 1)
        lhs = jnp.concatenate(
            [traces[p + other:p + other + 48, s] for p in (0, 288) for s in chunks(width)], axis=0
        )
        got = mm(lhs, hots[f, :, lanes])
        which = key >> 8
        own = traces[48 * f:48 * f + 48, lanes].astype(f32)
        own = own + traces[288 + 48 * f:288 + 48 * f + 48, lanes].astype(f32)
        total = jnp.where(which < 0, own_sign * own, 0.0)
        for a in range(blocks):
            both = got[48 * a:48 * a + 48] + got[48 * (blocks + a):48 * (blocks + a) + 48]
            total = jnp.where(which == a, both, total)
        out.append(total)
    return out


def put_traces(traces, lanes, comp, faces_x, picked):
    base = 16 * comp
    for f in range(2):
        for p in range(2):
            traces[288 * p + 48 * f + base:288 * p + 48 * f + base + 16, lanes] = faces_x[f][p]
    picked = picked.astype(bf16)
    for p in range(2):
        for f in range(4):
            at = 288 * p + 48 * (f + 2) + base
            traces[at:at + 16, lanes] = picked[64 * p + 16 * f:64 * p + 16 * f + 16]


def vel_traces(traces, lanes, velocity, pick):
    for i in range(3):
        high, low = split(velocity[i])
        picked = mm(pick, jnp.concatenate([high, low], axis=0))
        put_traces(traces, lanes, i, ((high[0:16], low[0:16]), (high[48:64], low[48:64])), picked)


def str_traces(traces, lanes, stress, pick):
    pieces = [split(s) for s in stress]
    for i in range(3):
        along_x, along_y, along_z = (pieces[m] for m in symmetric_index[i])
        picked = mm(pick, jnp.concatenate(along_y + along_z, axis=0))
        faces_x = (
            (along_x[0][0:16], along_x[1][0:16]),
            (along_x[0][48:64], along_x[1][48:64]),
        )
        put_traces(traces, lanes, i, faces_x, picked)


def pack(traces, values, picks, faces, late, send_one, send_two):
    width = traces.shape[1]

    def main(lanes):
        face = faces[:, lanes]
        got = mm(traces[...], picks[:, lanes])
        total = jnp.zeros((48, CHUNK), f32)
        for f in range(6):
            both = got[48 * f:48 * f + 48] + got[288 + 48 * f:288 + 48 * f + 48]
            total = jnp.where(face == f, both, total)
        values[0:48, lanes] = total

    each_chunk(2 * MAIN, main)
    send_one[:, 0:MAIN] = values[0:48, 0:MAIN]
    send_two[:, 0:MAIN] = values[0:48, MAIN:2 * MAIN]
    key = late[...]
    lane = key & 127
    which = jnp.broadcast_to(key >> 7, (48, 128))
    tiles = width // 128

    def last(f, total):
        at = pl.multiple_of(48 * f, 16)
        rows = traces[pl.ds(at, 48)].astype(f32)
        rows = rows + traces[pl.ds(pl.multiple_of(at + 288, 16), 48)].astype(f32)
        for a in range(tiles):
            got = gather_tile(rows[:, 128 * a:128 * a + 128], lane)
            total = jnp.where(which == f * tiles + a, got, total)
        return total

    total = lax.fori_loop(0, 6, last, jnp.zeros((48, 128), f32))
    none = jnp.zeros((48, HALO - MAIN - TAIL), f32)
    send_one[:, MAIN:HALO] = jnp.concatenate([total[:, 0:TAIL], none], axis=1)
    send_two[:, MAIN:HALO] = jnp.concatenate([total[:, TAIL:2 * TAIL], none], axis=1)


def rate_of(grad, lame, shear):
    trace = lame * (grad[0][0] + grad[1][1] + grad[2][2])
    return [
        trace + 2.0 * shear * grad[0][0],
        trace + 2.0 * shear * grad[1][1],
        trace + 2.0 * shear * grad[2][2],
        shear * (grad[0][1] + grad[1][0]),
        shear * (grad[0][2] + grad[2][0]),
        shear * (grad[1][2] + grad[2][1]),
    ]


def lift_velocity(plus, table):
    grad, jump = [], []
    for i in range(3):
        low_x, high_x, *rest = side_faces(plus, i)
        high, low = split(jnp.concatenate(rest, axis=0))
        put = mm(table, jnp.concatenate([high, low], axis=0))
        grad.append(
            (pad_x(-lift_half * low_x, lift_half * high_x), put[0:64], put[64:128])
        )
        jump.append(put[128:192] + pad_x(lift_half * low_x, lift_half * high_x))
    return grad, jump


def lift_stress(plus, table):
    out = []
    for i in range(3):
        low_x, high_x, *rest = side_faces(plus, i)
        high, low = split(jnp.concatenate(rest, axis=0))
        put = mm(table, jnp.concatenate([high, low], axis=0))
        out.append(put + pad_x(-lift_half * low_x, lift_half * high_x))
    return out


def start_kernel(
    even, state_hbm, neighbour_hbm, send_list_hbm, pick_hbm,
    velocity, stress, keys, picks, faces, late, traces, send_one, send_two,
    state, neighbour, send_list, pick, values, sems,
):
    copies = [
        pltpu.make_async_copy(source, target, sems.at[k])
        for k, (source, target) in enumerate((
            (neighbour_hbm, neighbour), (send_list_hbm, send_list), (pick_hbm, pick),
            (state_hbm.at[0:3], state.at[0:3]), (state_hbm.at[3:9], state.at[3:9]),
        ))
    ]
    for copy in copies:
        copy.start()
    for copy in copies[0:2]:
        copy.wait()
    width = neighbour.shape[1]
    cap = send_list.shape[1]
    is_even = even[0] == 1
    code = neighbour[...]
    low = code < width + cap
    at = code - width - jnp.where(low, 0, cap)
    second = jnp.where(low == is_even, 0, 1)
    place = jnp.where(
        at < MAIN, at + MAIN * second, at - MAIN + 2 * MAIN + TAIL * second
    )
    keys[...] = jnp.where(code < width, code, width + place)
    valid = jnp.where(jnp.max(code, axis=0, keepdims=True) >= 0, 1.0, 0.0)
    entries = send_list[...]
    entries = jnp.concatenate(
        [entries, jnp.full((2, MAIN + TAIL - cap), -1, jnp.int32)], axis=1
    )
    one, two = entries[0:1], entries[1:2]
    one, two = jnp.where(is_even, one, two), jnp.where(is_even, two, one)
    late[...] = jnp.concatenate([one[:, MAIN:], two[:, MAIN:]], axis=1)
    main = jnp.concatenate([one[:, 0:MAIN], two[:, 0:MAIN]], axis=1)
    face = jnp.zeros_like(main)
    for f in range(1, 6):
        face = face + jnp.where(main >= f * width, 1, 0)
    faces[...] = face
    slots = main - face * width
    for s in chunks(2 * MAIN):
        picks[:, s] = onehot(slots[:, s], width)
    for copy in copies[2:4]:
        copy.wait()
    for lanes in chunks(width):
        mask = valid[:, lanes]
        now = [state[i, :, lanes] * mask for i in range(3)]
        for i in range(3):
            velocity[i, :, lanes] = now[i]
        vel_traces(traces, lanes, now[0:3], pick[...])
    pack(traces, values, picks, faces, late, send_one, send_two)
    copies[4].wait()
    for lanes in chunks(width):
        for i in range(6):
            stress[i, :, lanes] = state[3 + i, :, lanes] * valid[:, lanes]


def vel_local_kernel(
    step, velocity, stress, traces, keys, lame, shear, vel, lift, *rest,
):
    total = None
    if step < 0:
        stress_out, jump_out, hots = rest
    elif step == 0:
        hots, forward, stress_out, jump_out, total_out = rest
    else:
        hots, forward, total, stress_out, jump_out, total_out = rest
    width = velocity.shape[2]
    def body(lanes):
        if step < 0:
            for f in range(6):
                hots[f, :, lanes] = onehot(keys[f:f + 1, lanes] & (CHUNK - 1), CHUNK)
        plus = local_faces(traces, keys[:, lanes], hots, lanes, 1.0)
        grad, jump = lift_velocity(plus, lift[...])
        whole = []
        for i in range(3):
            high, low = split(velocity[i, :, lanes])
            got = mm(vel[...], jnp.concatenate([high, low, high], axis=0))
            whole.append([got[64 * j:64 * j + 64] + grad[i][j] for j in range(3)])
            jump_out[i, :, lanes] = got[192:256] + jump[i]
        rate = rate_of(whole, lame[:, lanes], shear[:, lanes])
        for m in range(6):
            stress_out[m, :, lanes] = stress[m, :, lanes] + time_step * rate[m]
        if step >= 0:
            term = rho_term(forward, step, velocity, lanes)
            total_out[:, lanes] = term if total is None else total[:, lanes] + term

    each_chunk(width, body)


def rho_term(forward, step, velocity, lanes):
    acc = forward[step, 0, :, lanes] * velocity[0, :, lanes]
    acc = acc + forward[step, 1, :, lanes] * velocity[1, :, lanes]
    acc = acc + forward[step, 2, :, lanes] * velocity[2, :, lanes]
    return -time_step * acc


def vel_halo_kernel(
    stress, jump, recv_one, recv_two, keys, hots, picks, faces, late, lame, shear, lift, pick,
    stress_out, jump_out, traces, send_one, send_two, values,
):
    width = stress.shape[2]
    lhs, tail = halo_lhs(recv_one, recv_two)
    def body(lanes):
        plus = halo_faces(lhs, tail, keys[:, lanes], hots, lanes, width)
        grad, more = lift_velocity(plus, lift[...])
        rate = rate_of(grad, lame[:, lanes], shear[:, lanes])
        now = [stress[m, :, lanes] + time_step * rate[m] for m in range(6)]
        for m in range(6):
            stress_out[m, :, lanes] = now[m]
        for i in range(3):
            jump_out[i, :, lanes] = jump[i, :, lanes] + more[i]
        str_traces(traces, lanes, now, pick[...])

    each_chunk(width, body)
    pack(traces, values, picks, faces, late, send_one, send_two)


def str_local_kernel(
    step, velocity, stress, jump, traces, keys, hots, density, lame, shear, forward, div, lift, fwd, *rest,
):
    if len(rest) == 2:
        total = None
        velocity_out, total_out = rest
    else:
        total, velocity_out, total_out = rest
    width = velocity.shape[2]
    def body(lanes):
        plus = local_faces(traces, keys[:, lanes], hots, lanes, -1.0)
        lifted = lift_stress(plus, lift[...])
        now = [stress[m, :, lanes] for m in range(6)]
        pieces = [split(s) for s in now]
        rho = density[:, lanes]
        impedance = jnp.sqrt(rho * (lame[:, lanes] + 2.0 * shear[:, lanes]))
        scale = time_step / rho
        for i in range(3):
            rows = []
            for m in symmetric_index[i]:
                rows += [pieces[m][0], pieces[m][1], pieces[m][0]]
            got = mm(div[...], jnp.concatenate(rows, axis=0))
            velocity_out[i, :, lanes] = velocity[i, :, lanes] + scale * (
                got + lifted[i] + impedance * jump[i, :, lanes]
            )
        grad = []
        for i in range(3):
            high, low = split(forward[step, i, :, lanes])
            got = mm(fwd[...], jnp.concatenate([high, low, high], axis=0))
            grad.append([got[64 * j:64 * j + 64] for j in range(3)])
        diag = (grad[0][0], grad[1][1], grad[2][2])
        lame_term = -time_step * (diag[0] + diag[1] + diag[2]) * (now[0] + now[1] + now[2])
        shear_term = (-2.0 * time_step) * (
            diag[0] * now[0]
            + diag[1] * now[1]
            + diag[2] * now[2]
            + (grad[0][1] + grad[1][0]) * now[3]
            + (grad[0][2] + grad[2][0]) * now[4]
            + (grad[1][2] + grad[2][1]) * now[5]
        )
        for m, term in enumerate((lame_term, shear_term)):
            rows = total_out.shape[2]
            for e in range(total_out.shape[0]):
                share = term[rows * e:rows * e + rows]
                if total is not None:
                    share = total[e, m, :, lanes] + share
                total_out[e, m, :, lanes] = share

    each_chunk(width, body)


def str_halo_kernel(
    velocity, recv_one, recv_two, keys, hots, picks, faces, late, density, lift, pick,
    velocity_out, traces, send_one, send_two, values,
):
    halo_velocity(velocity, recv_one, recv_two, keys, hots, density, lift, velocity_out, traces, pick)
    pack(traces, values, picks, faces, late, send_one, send_two)


def last_kernel(
    step, velocity, recv_one, recv_two, keys, hots, density, lift, forward, other, *rest
):
    *total, velocity_out, total_out = rest
    total = total[0] if total else None
    halo_velocity(velocity, recv_one, recv_two, keys, hots, density, lift, velocity_out, None, None)
    for lanes in chunks(velocity.shape[2]):
        term = rho_term(forward, step, velocity_out, lanes)
        if total is not None:
            term = total[:, lanes] + term
        rows = total_out.shape[2]
        for e in range(total_out.shape[0]):
            total_out[e, 0, :, lanes] = term[rows * e:rows * e + rows]
            for m in range(2):
                total_out[e, m + 1, :, lanes] = other[e, m, :, lanes]


def event_sum_kernel(parts, out):
    width = parts.shape[3]
    for m in range(3):
        total = parts[0, m]
        for e in range(1, parts.shape[0]):
            total = total + parts[e, m]
        for k in range(total.shape[0]):
            out[m, :, k * width:(k + 1) * width] = total[k:k + 1]


def halo_velocity(
    velocity, recv_one, recv_two, keys, hots, density, lift, velocity_out, traces, pick
):
    width = velocity.shape[2]
    lhs, tail = halo_lhs(recv_one, recv_two)
    def body(lanes):
        plus = halo_faces(lhs, tail, keys[:, lanes], hots, lanes, width)
        lifted = lift_stress(plus, lift[...])
        scale = time_step / density[:, lanes]
        now = [velocity[i, :, lanes] + scale * lifted[i] for i in range(3)]
        for i in range(3):
            velocity_out[i, :, lanes] = now[i]
        if traces is not None:
            vel_traces(traces, lanes, now, pick[...])

    each_chunk(width, body)


def call(name, kernel, args, outs, specs=None, cost=0, scratch=()):
    whole = pl.BlockSpec(memory_space=pltpu.VMEM)
    specs = specs or {}
    return pl.pallas_call(
        kernel,
        name=name,
        in_specs=[specs.get(k, whole) for k in range(len(args))],
        out_specs=[whole] * len(outs),
        out_shape=[jax.ShapeDtypeStruct(s, d) for s, d in outs],
        scratch_shapes=list(scratch),
        compiler_params=pltpu.CompilerParams(vmem_limit_bytes=VMEM_LIMIT),
        cost_estimate=pl.CostEstimate(flops=cost, bytes_accessed=6_000_000, transcendentals=0),
    )(*args)


def swap(sent, axis):
    count = lax.axis_size(axis)
    got = []
    for first, value in enumerate(sent):
        pairs = []
        for low in range(1 - first, count - 1, 2):
            pairs += [(low, low + 1), (low + 1, low)]
        got.append(lax.ppermute(value, axis, pairs))
    return got


def local(
    adjoint_state, forward_velocity, density, lame_lambda, shear_modulus, neighbour, send_list
):
    width = density.shape[1]
    steps = forward_velocity.shape[1]
    table = {k: jnp.asarray(v) for k, v in tables().items()}
    state = adjoint_state[0]
    forward = forward_velocity[0]
    even = (1 - lax.axis_index("dom") % 2).astype(jnp.int32).reshape(1)

    values = pltpu.VMEM((48, 2 * MAIN), f32)
    field = ((64, width), f32)
    vector = ((3, 64, width), f32)
    tensor = ((6, 64, width), f32)
    count = lax.axis_size("event")
    shares = count if 64 % (8 * count) == 0 else 1
    two = ((shares, 2, 64 // shares, width), f32)
    three = ((shares, 3, 64 // shares, width), f32)
    trace = ((576, width), bf16)
    hot = ((6, CHUNK, width), bf16)
    sends = [((48, HALO), f32)] * 2
    lists = [((6, width), jnp.int32), ((width, 2 * MAIN), bf16),
             ((1, 2 * MAIN), jnp.int32), ((1, 2 * TAIL), jnp.int32)]

    velocity, stress, keys, picks, faces, late, traces, *sent = call(
        "start", start_kernel,
        (even, *(pltpu.with_memory_space_constraint(x, pltpu.HBM)
                for x in (state, neighbour, send_list, table["pick_vel"]))),
        [vector, tensor] + lists + [trace] + sends,
        specs={0: pl.BlockSpec(memory_space=pltpu.SMEM)}
        | {k: pl.BlockSpec(memory_space=pltpu.HBM) for k in range(1, 5)},
        scratch=[
            pltpu.VMEM(state.shape, f32), pltpu.VMEM(neighbour.shape, jnp.int32),
            pltpu.VMEM(send_list.shape, jnp.int32), pltpu.VMEM((128, 128), bf16),
            values,
            pltpu.SemaphoreType.DMA((5,)),
        ],
    )
    rho_total = other_total = hots = None
    for n in range(steps):
        recv = swap(sent, "dom")
        args = [velocity, stress, traces, keys, lame_lambda, shear_modulus,
                table["vel"], table["lift_vel"]]
        outs = [tensor, vector]
        if n:
            args += [hots, forward] + ([rho_total] if n > 1 else [])
            outs += [field]
        else:
            outs += [hot]
        stress, jump, more = call(
            "vel_local", functools.partial(vel_local_kernel, n - 1), args, outs, cost=4_000_000_000
        )
        if n:
            rho_total = more
        else:
            hots = more
        stress, jump, traces, *sent = call(
            "vel_halo", vel_halo_kernel,
            (stress, jump, *recv, keys, hots, picks, faces, late, lame_lambda, shear_modulus,
             table["lift_vel"], table["pick_str"]),
            [tensor, vector, trace] + sends, scratch=[values],
        )
        recv = swap(sent, "dom")
        args = [velocity, stress, jump, traces, keys, hots, density, lame_lambda, shear_modulus,
                forward, table["div"], table["lift_str"], table["fwd"]]
        if n:
            args += [other_total]
        velocity, other_total = call(
            "str_local", functools.partial(str_local_kernel, n), args, [vector, two],
            cost=4_000_000_000,
        )
        if n < steps - 1:
            velocity, traces, *sent = call(
                "str_halo", str_halo_kernel,
                (velocity, *recv, keys, hots, picks, faces, late, density, table["lift_str"],
                 table["pick_vel"]),
                [vector, trace] + sends, scratch=[values],
            )
        else:
            velocity, kernel_total = call(
                "last", functools.partial(last_kernel, n),
                (velocity, *recv, keys, hots, density, table["lift_str"], forward, other_total)
                + ((rho_total,) if n else ()),
                [vector, three],
            )

    if shares == count:
        parts = lax.all_to_all(kernel_total, "event", 0, 0, tiled=True)
        kernels, = call(
            "event_sum", event_sum_kernel, (parts,), [((3, 1, 64 // count * width), f32)]
        )
    else:
        flat = kernel_total.reshape(3, -1)
        part = lax.psum_scatter(flat, "event", scatter_dimension=1, tiled=True)
        kernels = part.reshape(3, 1, -1)
    return velocity[None], kernels


def solution(mesh):
    placed = (
        P("event", None, None, "dom"),
        P("event", None, None, None, "dom"),
        P(None, "dom"),
        P(None, "dom"),
        P(None, "dom"),
        P(None, "dom"),
        P(None, "dom"),
    )
    return jax.shard_map(
        local,
        mesh=mesh,
        in_specs=placed,
        out_specs=(P("event", None, None, "dom"), P(None, "dom", "event")),
        check_vma=False,
    )
```

```python
import functools
import math

import jax
import jax.numpy as jnp
import numpy as np
from jax import lax
from jax.experimental import pallas as pl
from jax.experimental.pallas import tpu as pltpu
from jax.sharding import PartitionSpec as P

time_step = 0.02
lift_half = 3.0
symmetric_index = ((0, 3, 4), (3, 1, 5), (4, 5, 2))
f32 = jnp.float32
bf16 = jnp.bfloat16
CHUNK = 256
MAIN = 384
TAIL = 64
HALO = 512
VMEM_LIMIT = 40 * 2**20


def lobatto_diff():
    points = [-1.0, -1.0 / math.sqrt(5.0), 1.0 / math.sqrt(5.0), 1.0]
    weights = [
        1.0 / math.prod([points[t] - points[o] for o in range(4) if o != t]) for t in range(4)
    ]
    offdiag = [
        [
            0.0 if t == s else weights[s] / weights[t] / (points[t] - points[s])
            for s in range(4)
        ]
        for t in range(4)
    ]
    return np.array(
        [[-sum(offdiag[t]) if t == s else offdiag[t][s] for s in range(4)] for t in range(4)],
        dtype=np.float64,
    )


def kron3(first, second, third):
    return np.kron(np.kron(first, second), third)


def deriv_parts(inner):
    matrix = lobatto_diff()
    if inner:
        matrix = matrix + np.diag([lift_half, 0.0, 0.0, -lift_half])
    matrix = matrix.astype(np.float32)
    eye = np.eye(4, dtype=np.float32)
    stack = [kron3(matrix, eye, eye), kron3(eye, matrix, eye), kron3(eye, eye, matrix)]
    high = [np.asarray(m.astype(bf16)) for m in stack]
    low = [np.asarray((m - h.astype(np.float32)).astype(bf16)) for m, h in zip(stack, high)]
    return [h.astype(np.float32) for h in high], [l.astype(np.float32) for l in low]


def tables():
    high, low = deriv_parts(True)
    plain_high, plain_low = deriv_parts(False)

    def rows(upper, lower):
        return np.concatenate(
            [np.concatenate([upper[j], upper[j], lower[j]], axis=1) for j in range(3)], axis=0
        )

    vel = rows(high, low)
    fwd = rows(plain_high, plain_low)
    div = np.concatenate([m for j in range(3) for m in (high[j], high[j], low[j])], axis=1)
    return {
        name: np.asarray(value).astype(bf16) for name, value in dict(vel=vel, fwd=fwd, div=div).items()
    }


def split(value):
    high = value.astype(bf16)
    return high, (value - high.astype(f32)).astype(bf16)


def mm(left, right):
    return jnp.dot(left, right, preferred_element_type=f32)


def onehot(row, depth):
    ids = lax.broadcasted_iota(jnp.int32, (depth, row.shape[-1]), 0)
    return jnp.where(ids == row, 1.0, 0.0).astype(bf16)


def chunks(width):
    return [slice(c, c + CHUNK) for c in range(0, width, CHUNK)]


def top_half(shape):
    return lax.broadcasted_iota(jnp.int32, shape, 0) < 4


def tiles_of(lanes):
    return [(lanes.start // 128 + t, slice(128 * t, 128 * t + 128)) for t in range(CHUNK // 128)]


def z_faces(value, stage, lanes):
    low, high = [], []
    for tile, at in tiles_of(lanes):
        stage[tile] = value[:, at]
        low.append(stage[tile, pl.ds(0, 16, stride=4)])
        high.append(stage[tile, pl.ds(3, 16, stride=4)])
    return jnp.concatenate(low, axis=1), jnp.concatenate(high, axis=1)


def xy_faces(value):
    top = top_half((8, value.shape[1]))

    def rows(at):
        return value[at:at + 8]

    def turned(at):
        return pltpu.roll(value[at:at + 8], 4, 0)

    low_y = [jnp.where(top, rows(at), turned(at + 16)) for at in (0, 32)]
    high_y = [jnp.where(top, turned(at), rows(at + 16)) for at in (8, 40)]
    return [
        value[0:16],
        value[48:64],
        jnp.concatenate(low_y, axis=0),
        jnp.concatenate(high_y, axis=0),
    ]


def spread(faces, comp, scratch, lanes):
    low_x, high_x, low_y, high_y, low_z, high_z = (
        p[16 * comp:16 * comp + 16] for p in faces
    )
    width = low_x.shape[1]
    top = top_half((8, width))
    none = jnp.zeros((8, width), f32)
    along_y = []
    for a in range(4):
        first = low_y[8 * (a // 2):8 * (a // 2) + 8]
        second = high_y[8 * (a // 2):8 * (a // 2) + 8]
        first, second = (
            (pltpu.roll(first, 4, 0), second) if a % 2 else (first, pltpu.roll(second, 4, 0))
        )
        along_y += [jnp.where(top, first, none), jnp.where(top, none, second)]
    along_z = []
    for tile, at in tiles_of(lanes):
        scratch[comp, tile, pl.ds(0, 16, stride=4)] = low_z[:, at]
        scratch[comp, tile, pl.ds(3, 16, stride=4)] = high_z[:, at]
        along_z.append(scratch[comp, tile])
    return (
        jnp.concatenate([low_x, none, none, none, none, high_x], axis=0),
        jnp.concatenate(along_y, axis=0),
        jnp.concatenate(along_z, axis=1),
    )


def signed(fields):
    along_x, along_y, along_z = fields
    width = along_x.shape[1]
    node = lax.broadcasted_iota(jnp.int32, (8, width), 0) & 3
    sign = jnp.where(node == 0, -lift_half, lift_half)
    return (
        jnp.concatenate([-lift_half * along_x[0:16], along_x[16:48], lift_half * along_x[48:64]], axis=0),
        jnp.concatenate(
            [(lift_half if b % 2 else -lift_half) * along_y[8 * b:8 * b + 8] for b in range(8)], axis=0
        ),
        jnp.concatenate([sign * along_z[8 * b:8 * b + 8] for b in range(8)], axis=0),
    )


def holders(width):
    node = lax.broadcasted_iota(jnp.int32, (64, width), 0)
    total = jnp.zeros((64, width), f32)
    for index in (node >> 4, (node >> 2) & 3, node & 3):
        total = total + jnp.where((index == 0) | (index == 3), 1.0, 0.0)
    return total


def gather_tile(source, lane):
    lane = jnp.broadcast_to(lane, (8, 128))
    return jnp.concatenate(
        [jnp.take_along_axis(source[r:r + 8], lane, axis=1) for r in range(0, 48, 8)], axis=0
    )


def halo_faces(lhs, tail, keys, hots, lanes, width):
    blocks = 2 * MAIN // CHUNK
    first = width // CHUNK
    out = []
    for f in range(6):
        key = keys[f:f + 1]
        got = mm(lhs, hots[f, :, lanes])
        which = key >> 8
        late = jnp.concatenate(
            [gather_tile(tail, key[:, t:t + 128] & 127) for t in range(0, CHUNK, 128)], axis=1
        )
        total = jnp.where(which == first + blocks, late, 0.0)
        for a in range(blocks):
            both = got[48 * a:48 * a + 48] + got[48 * (blocks + a):48 * (blocks + a) + 48]
            total = jnp.where(which == first + a, both, total)
        out.append(total)
    return out


def halo_lhs(recv_one, recv_two):
    whole = jnp.concatenate([recv_one[:, 0:MAIN], recv_two[:, 0:MAIN]], axis=1)
    high, low = split(jnp.concatenate([whole[:, s] for s in chunks(2 * MAIN)], axis=0))
    tail = jnp.concatenate(
        [recv_one[:, MAIN:MAIN + TAIL], recv_two[:, MAIN:MAIN + TAIL]], axis=1
    )
    return jnp.concatenate([high, low], axis=0), tail


def local_faces(traces, keys, hots, lanes, own_sign):
    width = traces.shape[1]
    blocks = width // CHUNK
    out = []
    for f in range(6):
        key = keys[f:f + 1]
        other = 48 * (f ^ 1)
        lhs = jnp.concatenate(
            [traces[p + other:p + other + 48, s] for p in (0, 288) for s in chunks(width)], axis=0
        )
        got = mm(lhs, hots[f, :, lanes])
        which = key >> 8
        own = traces[48 * f:48 * f + 48, lanes].astype(f32)
        own = own + traces[288 + 48 * f:288 + 48 * f + 48, lanes].astype(f32)
        total = jnp.where(which < 0, own_sign * own, 0.0)
        for a in range(blocks):
            both = got[48 * a:48 * a + 48] + got[48 * (blocks + a):48 * (blocks + a) + 48]
            total = jnp.where(which == a, both, total)
        out.append(total)
    return out


def put_traces(traces, lanes, comp, face, value):
    at = 48 * face + 16 * comp
    traces[at:at + 16, lanes], traces[288 + at:288 + at + 16, lanes] = split(value)


def vel_traces(traces, lanes, velocity, stage):
    for i in range(3):
        faces = (*xy_faces(velocity[i]), *z_faces(velocity[i], stage.at[i], lanes))
        for f, value in enumerate(faces):
            put_traces(traces, lanes, i, f, value)


def str_traces(traces, lanes, stress, stage):
    faces = [xy_faces(stress[m]) for m in range(6)]
    for i in range(3):
        for f in range(4):
            put_traces(traces, lanes, i, f, faces[symmetric_index[i][f // 2]][f])
        for f, value in enumerate(z_faces(stress[symmetric_index[i][2]], stage.at[i], lanes)):
            put_traces(traces, lanes, i, 4 + f, value)


def pack(traces, values, picks, faces, late, send_one, send_two):
    width = traces.shape[1]
    pieces = []
    for s in chunks(2 * MAIN):
        face = faces[:, s]
        got = mm(traces[...], picks[:, s])
        total = jnp.zeros((48, CHUNK), f32)
        for f in range(6):
            both = got[48 * f:48 * f + 48] + got[288 + 48 * f:288 + 48 * f + 48]
            total = jnp.where(face == f, both, total)
        pieces.append(total)
    whole = jnp.concatenate(pieces, axis=1)
    send_one[:, 0:MAIN] = whole[:, 0:MAIN]
    send_two[:, 0:MAIN] = whole[:, MAIN:2 * MAIN]
    for at in range(0, 288, 16):
        values[at:at + 16] = (
            traces[at:at + 16].astype(f32) + traces[288 + at:288 + at + 16].astype(f32)
        )
    key = late[...]
    lane = key & 127
    which = jnp.broadcast_to(key >> 7, (48, 128))
    total = jnp.zeros((48, 128), f32)
    for f in range(6):
        for a in range(width // 128):
            got = gather_tile(values[48 * f:48 * f + 48, 128 * a:128 * a + 128], lane)
            total = jnp.where(which == f * (width // 128) + a, got, total)
    none = jnp.zeros((48, HALO - MAIN - TAIL), f32)
    send_one[:, MAIN:HALO] = jnp.concatenate([total[:, 0:TAIL], none], axis=1)
    send_two[:, MAIN:HALO] = jnp.concatenate([total[:, TAIL:2 * TAIL], none], axis=1)


def rate_of(grad, lame, shear):
    trace = lame * (grad[0][0] + grad[1][1] + grad[2][2])
    return [
        trace + 2.0 * shear * grad[0][0],
        trace + 2.0 * shear * grad[1][1],
        trace + 2.0 * shear * grad[2][2],
        shear * (grad[0][1] + grad[1][0]),
        shear * (grad[0][2] + grad[2][0]),
        shear * (grad[1][2] + grad[2][1]),
    ]


def lift_velocity(plus, scratch, lanes):
    grad, jump = [], []
    for i in range(3):
        fields = spread(plus, i, scratch, lanes)
        grad.append(signed(fields))
        jump.append(lift_half * (fields[0] + fields[1] + fields[2]))
    return grad, jump


def lift_stress(plus, scratch, lanes):
    out = []
    for i in range(3):
        along_x, along_y, along_z = signed(spread(plus, i, scratch, lanes))
        out.append(along_x + along_y + along_z)
    return out


def start_kernel(
    even, state_hbm, neighbour_hbm, send_list_hbm,
    velocity, stress, keys, picks, faces, late, traces, send_one, send_two,
    state, neighbour, send_list, values, stage, sems,
):
    copies = [
        pltpu.make_async_copy(source, target, sems.at[k])
        for k, (source, target) in enumerate((
            (neighbour_hbm, neighbour), (send_list_hbm, send_list),
            (state_hbm.at[0:3], state.at[0:3]), (state_hbm.at[3:9], state.at[3:9]),
        ))
    ]
    for copy in copies:
        copy.start()
    for copy in copies[0:2]:
        copy.wait()
    width = neighbour.shape[1]
    cap = send_list.shape[1]
    is_even = even[0] == 1
    code = neighbour[...]
    low = code < width + cap
    at = code - width - jnp.where(low, 0, cap)
    second = jnp.where(low == is_even, 0, 1)
    place = jnp.where(
        at < MAIN, at + MAIN * second, at - MAIN + 2 * MAIN + TAIL * second
    )
    keys[...] = jnp.where(code < width, code, width + place)
    valid = jnp.where(jnp.max(code, axis=0, keepdims=True) >= 0, 1.0, 0.0)
    entries = send_list[...]
    entries = jnp.concatenate(
        [entries, jnp.full((2, MAIN + TAIL - cap), -1, jnp.int32)], axis=1
    )
    one, two = entries[0:1], entries[1:2]
    one, two = jnp.where(is_even, one, two), jnp.where(is_even, two, one)
    late[...] = jnp.concatenate([one[:, MAIN:], two[:, MAIN:]], axis=1)
    main = jnp.concatenate([one[:, 0:MAIN], two[:, 0:MAIN]], axis=1)
    face = jnp.zeros_like(main)
    for f in range(1, 6):
        face = face + jnp.where(main >= f * width, 1, 0)
    faces[...] = face
    slots = main - face * width
    for s in chunks(2 * MAIN):
        picks[:, s] = onehot(slots[:, s], width)
    copies[2].wait()
    for lanes in chunks(width):
        mask = valid[:, lanes]
        now = [state[i, :, lanes] * mask for i in range(3)]
        for i in range(3):
            velocity[i, :, lanes] = now[i]
        vel_traces(traces, lanes, now, stage)
    pack(traces, values, picks, faces, late, send_one, send_two)
    copies[3].wait()
    for lanes in chunks(width):
        for i in range(6):
            stress[i, :, lanes] = state[3 + i, :, lanes] * valid[:, lanes]


def vel_local_kernel(
    step, velocity, stress, traces, keys, lame, shear, vel, *rest,
):
    total = None
    *rest, scratch = rest
    scratch[...] = jnp.zeros(scratch.shape, f32)
    if step < 0:
        stress_out, jump_out, hots = rest
    elif step == 0:
        hots, forward, stress_out, jump_out, total_out = rest
    else:
        hots, forward, total, stress_out, jump_out, total_out = rest
    width = velocity.shape[2]
    for lanes in chunks(width):
        if step < 0:
            for f in range(6):
                hots[f, :, lanes] = onehot(keys[f:f + 1, lanes] & (CHUNK - 1), CHUNK)
        plus = local_faces(traces, keys[:, lanes], hots, lanes, 1.0)
        grad, jump = lift_velocity(plus, scratch, lanes)
        own = -lift_half * holders(CHUNK)
        whole = []
        for i in range(3):
            now = velocity[i, :, lanes]
            high, low = split(now)
            got = mm(vel[...], jnp.concatenate([high, low, high], axis=0))
            whole.append([got[64 * j:64 * j + 64] + grad[i][j] for j in range(3)])
            jump_out[i, :, lanes] = own * now + jump[i]
        rate = rate_of(whole, lame[:, lanes], shear[:, lanes])
        for m in range(6):
            stress_out[m, :, lanes] = stress[m, :, lanes] + time_step * rate[m]
        if step >= 0:
            term = rho_term(forward, step, velocity, lanes)
            total_out[:, lanes] = term if total is None else total[:, lanes] + term


def rho_term(forward, step, velocity, lanes):
    acc = forward[step, 0, :, lanes] * velocity[0, :, lanes]
    acc = acc + forward[step, 1, :, lanes] * velocity[1, :, lanes]
    acc = acc + forward[step, 2, :, lanes] * velocity[2, :, lanes]
    return -time_step * acc


def vel_halo_kernel(
    stress, jump, recv_one, recv_two, keys, hots, picks, faces, late, lame, shear,
    stress_out, jump_out, traces, send_one, send_two, values, scratch, stage,
):
    width = stress.shape[2]
    scratch[...] = jnp.zeros(scratch.shape, f32)
    lhs, tail = halo_lhs(recv_one, recv_two)
    for lanes in chunks(width):
        plus = halo_faces(lhs, tail, keys[:, lanes], hots, lanes, width)
        grad, more = lift_velocity(plus, scratch, lanes)
        rate = rate_of(grad, lame[:, lanes], shear[:, lanes])
        now = [stress[m, :, lanes] + time_step * rate[m] for m in range(6)]
        for m in range(6):
            stress_out[m, :, lanes] = now[m]
        for i in range(3):
            jump_out[i, :, lanes] = jump[i, :, lanes] + more[i]
        str_traces(traces, lanes, now, stage)
    pack(traces, values, picks, faces, late, send_one, send_two)


def str_local_kernel(
    step, velocity, stress, jump, traces, keys, hots, density, lame, shear, forward, div, fwd, *rest,
):
    *rest, scratch = rest
    scratch[...] = jnp.zeros(scratch.shape, f32)
    if len(rest) == 2:
        total = None
        velocity_out, total_out = rest
    else:
        total, velocity_out, total_out = rest
    width = velocity.shape[2]
    for lanes in chunks(width):
        plus = local_faces(traces, keys[:, lanes], hots, lanes, -1.0)
        lifted = lift_stress(plus, scratch, lanes)
        now = [stress[m, :, lanes] for m in range(6)]
        pieces = [split(s) for s in now]
        rho = density[:, lanes]
        impedance = jnp.sqrt(rho * (lame[:, lanes] + 2.0 * shear[:, lanes]))
        scale = time_step / rho
        for i in range(3):
            rows = []
            for m in symmetric_index[i]:
                rows += [pieces[m][0], pieces[m][1], pieces[m][0]]
            got = mm(div[...], jnp.concatenate(rows, axis=0))
            velocity_out[i, :, lanes] = velocity[i, :, lanes] + scale * (
                got + lifted[i] + impedance * jump[i, :, lanes]
            )
        grad = []
        for i in range(3):
            high, low = split(forward[step, i, :, lanes])
            got = mm(fwd[...], jnp.concatenate([high, low, high], axis=0))
            grad.append([got[64 * j:64 * j + 64] for j in range(3)])
        diag = (grad[0][0], grad[1][1], grad[2][2])
        lame_term = -time_step * (diag[0] + diag[1] + diag[2]) * (now[0] + now[1] + now[2])
        shear_term = (-2.0 * time_step) * (
            diag[0] * now[0]
            + diag[1] * now[1]
            + diag[2] * now[2]
            + (grad[0][1] + grad[1][0]) * now[3]
            + (grad[0][2] + grad[2][0]) * now[4]
            + (grad[1][2] + grad[2][1]) * now[5]
        )
        for m, term in enumerate((lame_term, shear_term)):
            rows = total_out.shape[2]
            for e in range(total_out.shape[0]):
                share = term[rows * e:rows * e + rows]
                if total is not None:
                    share = total[e, m, :, lanes] + share
                total_out[e, m, :, lanes] = share


def str_halo_kernel(
    velocity, recv_one, recv_two, keys, hots, picks, faces, late, density,
    velocity_out, traces, send_one, send_two, values, scratch, stage,
):
    halo_velocity(velocity, recv_one, recv_two, keys, hots, density, velocity_out, traces, scratch, stage)
    pack(traces, values, picks, faces, late, send_one, send_two)


def last_kernel(
    step, velocity, recv_one, recv_two, keys, hots, density, forward, other, *rest
):
    *total, velocity_out, total_out, scratch = rest
    total = total[0] if total else None
    halo_velocity(velocity, recv_one, recv_two, keys, hots, density, velocity_out, None, scratch, None)
    for lanes in chunks(velocity.shape[2]):
        term = rho_term(forward, step, velocity_out, lanes)
        if total is not None:
            term = total[:, lanes] + term
        rows = total_out.shape[2]
        for e in range(total_out.shape[0]):
            total_out[e, 0, :, lanes] = term[rows * e:rows * e + rows]
            for m in range(2):
                total_out[e, m + 1, :, lanes] = other[e, m, :, lanes]


def event_sum_kernel(parts, out):
    width = parts.shape[3]
    for m in range(3):
        total = parts[0, m]
        for e in range(1, parts.shape[0]):
            total = total + parts[e, m]
        for k in range(total.shape[0]):
            out[m, :, k * width:(k + 1) * width] = total[k:k + 1]


def halo_velocity(
    velocity, recv_one, recv_two, keys, hots, density, velocity_out, traces, scratch, stage
):
    width = velocity.shape[2]
    scratch[...] = jnp.zeros(scratch.shape, f32)
    lhs, tail = halo_lhs(recv_one, recv_two)
    for lanes in chunks(width):
        plus = halo_faces(lhs, tail, keys[:, lanes], hots, lanes, width)
        lifted = lift_stress(plus, scratch, lanes)
        scale = time_step / density[:, lanes]
        now = [velocity[i, :, lanes] + scale * lifted[i] for i in range(3)]
        for i in range(3):
            velocity_out[i, :, lanes] = now[i]
        if traces is not None:
            vel_traces(traces, lanes, now, stage)


def call(name, kernel, args, outs, specs=None, cost=0, scratch=()):
    whole = pl.BlockSpec(memory_space=pltpu.VMEM)
    specs = specs or {}
    return pl.pallas_call(
        kernel,
        name=name,
        in_specs=[specs.get(k, whole) for k in range(len(args))],
        out_specs=[whole] * len(outs),
        out_shape=[jax.ShapeDtypeStruct(s, d) for s, d in outs],
        scratch_shapes=list(scratch),
        compiler_params=pltpu.CompilerParams(vmem_limit_bytes=VMEM_LIMIT),
        cost_estimate=pl.CostEstimate(flops=cost, bytes_accessed=6_000_000, transcendentals=0),
    )(*args)


def swap(sent, axis):
    count = lax.axis_size(axis)
    got = []
    for first, value in enumerate(sent):
        pairs = []
        for low in range(1 - first, count - 1, 2):
            pairs += [(low, low + 1), (low + 1, low)]
        got.append(lax.ppermute(value, axis, pairs))
    return got


def local(
    adjoint_state, forward_velocity, density, lame_lambda, shear_modulus, neighbour, send_list
):
    width = density.shape[1]
    steps = forward_velocity.shape[1]
    table = {k: jnp.asarray(v) for k, v in tables().items()}
    state = adjoint_state[0]
    forward = forward_velocity[0]
    even = (1 - lax.axis_index("dom") % 2).astype(jnp.int32).reshape(1)

    nodal = pltpu.VMEM((3, width // 128, 64, 128), f32)
    values = pltpu.VMEM((288, width), f32)
    field = ((64, width), f32)
    vector = ((3, 64, width), f32)
    tensor = ((6, 64, width), f32)
    count = lax.axis_size("event")
    shares = count if 64 % (8 * count) == 0 else 1
    two = ((shares, 2, 64 // shares, width), f32)
    three = ((shares, 3, 64 // shares, width), f32)
    trace = ((576, width), bf16)
    hot = ((6, CHUNK, width), bf16)
    sends = [((48, HALO), f32)] * 2
    lists = [((6, width), jnp.int32), ((width, 2 * MAIN), bf16),
             ((1, 2 * MAIN), jnp.int32), ((1, 2 * TAIL), jnp.int32)]

    velocity, stress, keys, picks, faces, late, traces, *sent = call(
        "start", start_kernel,
        (even, *(pltpu.with_memory_space_constraint(x, pltpu.HBM)
                for x in (state, neighbour, send_list))),
        [vector, tensor] + lists + [trace] + sends,
        specs={0: pl.BlockSpec(memory_space=pltpu.SMEM)}
        | {k: pl.BlockSpec(memory_space=pltpu.HBM) for k in range(1, 4)},
        scratch=[
            pltpu.VMEM(state.shape, f32), pltpu.VMEM(neighbour.shape, jnp.int32),
            pltpu.VMEM(send_list.shape, jnp.int32), values, nodal, pltpu.SemaphoreType.DMA((4,)),
        ],
    )
    rho_total = other_total = hots = None
    for n in range(steps):
        recv = swap(sent, "dom")
        args = [velocity, stress, traces, keys, lame_lambda, shear_modulus,
                table["vel"]]
        outs = [tensor, vector]
        if n:
            args += [hots, forward] + ([rho_total] if n > 1 else [])
            outs += [field]
        else:
            outs += [hot]
        stress, jump, more = call(
            "vel_local", functools.partial(vel_local_kernel, n - 1), args, outs, cost=4_000_000_000,
            scratch=[nodal],
        )
        if n:
            rho_total = more
        else:
            hots = more
        stress, jump, traces, *sent = call(
            "vel_halo", vel_halo_kernel,
            (stress, jump, *recv, keys, hots, picks, faces, late, lame_lambda, shear_modulus),
            [tensor, vector, trace] + sends, scratch=[values, nodal, nodal],
        )
        recv = swap(sent, "dom")
        args = [velocity, stress, jump, traces, keys, hots, density, lame_lambda, shear_modulus,
                forward, table["div"], table["fwd"]]
        if n:
            args += [other_total]
        velocity, other_total = call(
            "str_local", functools.partial(str_local_kernel, n), args, [vector, two],
            cost=4_000_000_000, scratch=[nodal],
        )
        if n < steps - 1:
            velocity, traces, *sent = call(
                "str_halo", str_halo_kernel,
                (velocity, *recv, keys, hots, picks, faces, late, density),
                [vector, trace] + sends, scratch=[values, nodal, nodal],
            )
        else:
            velocity, kernel_total = call(
                "last", functools.partial(last_kernel, n),
                (velocity, *recv, keys, hots, density, forward, other_total)
                + ((rho_total,) if n else ()),
                [vector, three], scratch=[nodal],
            )

    if shares == count:
        parts = lax.all_to_all(kernel_total, "event", 0, 0, tiled=True)
        kernels, = call(
            "event_sum", event_sum_kernel, (parts,), [((3, 1, 64 // count * width), f32)]
        )
    else:
        flat = kernel_total.reshape(3, -1)
        part = lax.psum_scatter(flat, "event", scatter_dimension=1, tiled=True)
        kernels = part.reshape(3, 1, -1)
    return velocity[None], kernels


def solution(mesh):
    placed = (
        P("event", None, None, "dom"),
        P("event", None, None, None, "dom"),
        P(None, "dom"),
        P(None, "dom"),
        P(None, "dom"),
        P(None, "dom"),
        P(None, "dom"),
    )
    return jax.shard_map(
        local,
        mesh=mesh,
        in_specs=placed,
        out_specs=(P("event", None, None, "dom"), P(None, "dom", "event")),
        check_vma=False,
    )
```

```python
import functools
import math

import jax
import jax.numpy as jnp
import numpy as np
from jax import lax
from jax.experimental import pallas as pl
from jax.experimental.pallas import tpu as pltpu
from jax.sharding import PartitionSpec as P

time_step = 0.02
lift_half = 3.0
symmetric_index = ((0, 3, 4), (3, 1, 5), (4, 5, 2))
f32 = jnp.float32
bf16 = jnp.bfloat16
CHUNK = 256
MAIN = 384
TAIL = 64
SEND_MAIN = 48 * MAIN // 128
SEND_ROWS = SEND_MAIN + 48 * TAIL // 128
VMEM_LIMIT = 40 * 2**20


def lobatto_diff():
    points = [-1.0, -1.0 / math.sqrt(5.0), 1.0 / math.sqrt(5.0), 1.0]
    weights = [
        1.0 / math.prod([points[t] - points[o] for o in range(4) if o != t]) for t in range(4)
    ]
    offdiag = [
        [
            0.0 if t == s else weights[s] / weights[t] / (points[t] - points[s])
            for s in range(4)
        ]
        for t in range(4)
    ]
    return np.array(
        [[-sum(offdiag[t]) if t == s else offdiag[t][s] for s in range(4)] for t in range(4)],
        dtype=np.float64,
    )


def kron3(first, second, third):
    return np.kron(np.kron(first, second), third)


def deriv_parts(inner):
    matrix = lobatto_diff()
    if inner:
        matrix = matrix + np.diag([lift_half, 0.0, 0.0, -lift_half])
    matrix = matrix.astype(np.float32)
    eye = np.eye(4, dtype=np.float32)
    stack = [kron3(matrix, eye, eye), kron3(eye, matrix, eye), kron3(eye, eye, matrix)]
    high = [np.asarray(m.astype(bf16)) for m in stack]
    low = [np.asarray((m - h.astype(np.float32)).astype(bf16)) for m, h in zip(stack, high)]
    return [h.astype(np.float32) for h in high], [l.astype(np.float32) for l in low]


def tables():
    high, low = deriv_parts(True)
    plain_high, plain_low = deriv_parts(False)

    def rows(upper, lower):
        return np.concatenate(
            [np.concatenate([upper[j], upper[j], lower[j]], axis=1) for j in range(3)], axis=0
        )

    vel = rows(high, low)
    fwd = rows(plain_high, plain_low)
    div = np.concatenate([m for j in range(3) for m in (high[j], high[j], low[j])], axis=1)
    return {
        name: np.asarray(value).astype(bf16) for name, value in dict(vel=vel, fwd=fwd, div=div).items()
    }


def split(value):
    high = value.astype(bf16)
    return high, (value - high.astype(f32)).astype(bf16)


def mm(left, right):
    return jnp.dot(left, right, preferred_element_type=f32)


def onehot(row, depth):
    ids = lax.broadcasted_iota(jnp.int32, (depth, row.shape[-1]), 0)
    return jnp.where(ids == row, 1.0, 0.0).astype(bf16)


def chunks(width):
    return [slice(c, c + CHUNK) for c in range(0, width, CHUNK)]


def top_half(shape):
    return lax.broadcasted_iota(jnp.int32, shape, 0) < 4


def tiles_of(lanes):
    return [(lanes.start // 128 + t, slice(128 * t, 128 * t + 128)) for t in range(CHUNK // 128)]


def z_faces(value, stage, lanes):
    low, high = [], []
    for tile, at in tiles_of(lanes):
        stage[tile] = value[:, at]
        low.append(stage[tile, pl.ds(0, 16, stride=4)])
        high.append(stage[tile, pl.ds(3, 16, stride=4)])
    return jnp.concatenate(low, axis=1), jnp.concatenate(high, axis=1)


def xy_faces(value):
    top = top_half((8, value.shape[1]))

    def rows(at):
        return value[at:at + 8]

    def turned(at):
        return pltpu.roll(value[at:at + 8], 4, 0)

    low_y = [jnp.where(top, rows(at), turned(at + 16)) for at in (0, 32)]
    high_y = [jnp.where(top, turned(at), rows(at + 16)) for at in (8, 40)]
    return [
        value[0:16],
        value[48:64],
        jnp.concatenate(low_y, axis=0),
        jnp.concatenate(high_y, axis=0),
    ]


def spread(faces, comp, scratch, lanes):
    low_x, high_x, low_y, high_y, low_z, high_z = (
        p[16 * comp:16 * comp + 16] for p in faces
    )
    width = low_x.shape[1]
    top = top_half((8, width))
    none = jnp.zeros((8, width), f32)
    along_y = []
    for a in range(4):
        first = low_y[8 * (a // 2):8 * (a // 2) + 8]
        second = high_y[8 * (a // 2):8 * (a // 2) + 8]
        first, second = (
            (pltpu.roll(first, 4, 0), second) if a % 2 else (first, pltpu.roll(second, 4, 0))
        )
        along_y += [jnp.where(top, first, none), jnp.where(top, none, second)]
    along_z = []
    for tile, at in tiles_of(lanes):
        scratch[comp, tile, pl.ds(0, 16, stride=4)] = low_z[:, at]
        scratch[comp, tile, pl.ds(3, 16, stride=4)] = high_z[:, at]
        along_z.append(scratch[comp, tile])
    return (
        jnp.concatenate([low_x, none, none, none, none, high_x], axis=0),
        jnp.concatenate(along_y, axis=0),
        jnp.concatenate(along_z, axis=1),
    )


def signed(fields):
    along_x, along_y, along_z = fields
    width = along_x.shape[1]
    node = lax.broadcasted_iota(jnp.int32, (8, width), 0) & 3
    sign = jnp.where(node == 0, -lift_half, lift_half)
    return (
        jnp.concatenate([-lift_half * along_x[0:16], along_x[16:48], lift_half * along_x[48:64]], axis=0),
        jnp.concatenate(
            [(lift_half if b % 2 else -lift_half) * along_y[8 * b:8 * b + 8] for b in range(8)], axis=0
        ),
        jnp.concatenate([sign * along_z[8 * b:8 * b + 8] for b in range(8)], axis=0),
    )


def holders(width):
    node = lax.broadcasted_iota(jnp.int32, (64, width), 0)
    total = jnp.zeros((64, width), f32)
    for index in (node >> 4, (node >> 2) & 3, node & 3):
        total = total + jnp.where((index == 0) | (index == 3), 1.0, 0.0)
    return total


def gather_tile(source, lane):
    lane = jnp.broadcast_to(lane, (8, 128))
    return jnp.concatenate(
        [jnp.take_along_axis(source[r:r + 8], lane, axis=1) for r in range(0, 48, 8)], axis=0
    )


def halo_faces(lhs, tail, keys, hots, lanes, width):
    blocks = 2 * MAIN // CHUNK
    first = width // CHUNK
    out = []
    for f in range(6):
        key = keys[f:f + 1]
        got = mm(lhs, hots[f, :, lanes])
        which = key >> 8
        late = jnp.concatenate(
            [gather_tile(tail, key[:, t:t + 128] & 127) for t in range(0, CHUNK, 128)], axis=1
        )
        total = jnp.where(which == first + blocks, late, 0.0)
        for a in range(blocks):
            both = got[48 * a:48 * a + 48] + got[48 * (blocks + a):48 * (blocks + a) + 48]
            total = jnp.where(which == first + a, both, total)
        out.append(total)
    return out


def halo_lhs(recv_one, recv_two):
    tiles = [
        recv[48 * t:48 * t + 48] for recv in (recv_one, recv_two) for t in range(MAIN // 128)
    ]
    blocks = [jnp.concatenate(tiles[t:t + 2], axis=1) for t in range(0, len(tiles), 2)]
    high, low = split(jnp.concatenate(blocks, axis=0))
    one, two = recv_one[SEND_MAIN:SEND_ROWS], recv_two[SEND_MAIN:SEND_ROWS]
    tail = jnp.concatenate(
        [
            jnp.concatenate([one[:, 0:TAIL], two[:, 0:TAIL]], axis=1),
            jnp.concatenate([one[:, TAIL:2 * TAIL], two[:, TAIL:2 * TAIL]], axis=1),
        ],
        axis=0,
    )
    return jnp.concatenate([high, low], axis=0), tail


def local_faces(traces, keys, hots, lanes, own_sign):
    width = traces.shape[1]
    blocks = width // CHUNK
    out = []
    for f in range(6):
        key = keys[f:f + 1]
        other = 48 * (f ^ 1)
        lhs = jnp.concatenate(
            [traces[p + other:p + other + 48, s] for p in (0, 288) for s in chunks(width)], axis=0
        )
        got = mm(lhs, hots[f, :, lanes])
        which = key >> 8
        own = traces[48 * f:48 * f + 48, lanes].astype(f32)
        own = own + traces[288 + 48 * f:288 + 48 * f + 48, lanes].astype(f32)
        total = jnp.where(which < 0, own_sign * own, 0.0)
        for a in range(blocks):
            both = got[48 * a:48 * a + 48] + got[48 * (blocks + a):48 * (blocks + a) + 48]
            total = jnp.where(which == a, both, total)
        out.append(total)
    return out


def put_traces(traces, lanes, comp, face, value):
    at = 48 * face + 16 * comp
    traces[at:at + 16, lanes], traces[288 + at:288 + at + 16, lanes] = split(value)


def vel_traces(traces, lanes, velocity, stage):
    for i in range(3):
        faces = (*xy_faces(velocity[i]), *z_faces(velocity[i], stage.at[i], lanes))
        for f, value in enumerate(faces):
            put_traces(traces, lanes, i, f, value)


def str_traces(traces, lanes, stress, stage):
    faces = [xy_faces(stress[m]) for m in range(6)]
    for i in range(3):
        for f in range(4):
            put_traces(traces, lanes, i, f, faces[symmetric_index[i][f // 2]][f])
        for f, value in enumerate(z_faces(stress[symmetric_index[i][2]], stage.at[i], lanes)):
            put_traces(traces, lanes, i, 4 + f, value)


def pack(traces, values, picks, faces, late, send_one, send_two):
    width = traces.shape[1]
    pieces = []
    for s in chunks(2 * MAIN):
        face = faces[:, s]
        got = mm(traces[...], picks[:, s])
        total = jnp.zeros((48, CHUNK), f32)
        for f in range(6):
            both = got[48 * f:48 * f + 48] + got[288 + 48 * f:288 + 48 * f + 48]
            total = jnp.where(face == f, both, total)
        pieces.append(total)
    whole = jnp.concatenate(pieces, axis=1)
    for t in range(MAIN // 128):
        for first, send in ((0, send_one), (MAIN, send_two)):
            send[48 * t:48 * t + 48] = whole[:, first + 128 * t:first + 128 * t + 128]
    for at in range(0, 288, 16):
        values[at:at + 16] = (
            traces[at:at + 16].astype(f32) + traces[288 + at:288 + at + 16].astype(f32)
        )
    key = late[...]
    lane = key & 127
    which = jnp.broadcast_to(key >> 7, (48, 128))
    total = jnp.zeros((48, 128), f32)
    for f in range(6):
        for a in range(width // 128):
            got = gather_tile(values[48 * f:48 * f + 48, 128 * a:128 * a + 128], lane)
            total = jnp.where(which == f * (width // 128) + a, got, total)
    one, two = total[:, 0:TAIL], total[:, TAIL:2 * TAIL]
    send_one[SEND_MAIN:SEND_ROWS] = jnp.concatenate([one[0:24], one[24:48]], axis=1)
    send_two[SEND_MAIN:SEND_ROWS] = jnp.concatenate([two[0:24], two[24:48]], axis=1)


def rate_of(grad, lame, shear):
    trace = lame * (grad[0][0] + grad[1][1] + grad[2][2])
    return [
        trace + 2.0 * shear * grad[0][0],
        trace + 2.0 * shear * grad[1][1],
        trace + 2.0 * shear * grad[2][2],
        shear * (grad[0][1] + grad[1][0]),
        shear * (grad[0][2] + grad[2][0]),
        shear * (grad[1][2] + grad[2][1]),
    ]


def lift_velocity(plus, scratch, lanes):
    grad, jump = [], []
    for i in range(3):
        fields = spread(plus, i, scratch, lanes)
        grad.append(signed(fields))
        jump.append(lift_half * (fields[0] + fields[1] + fields[2]))
    return grad, jump


def lift_stress(plus, scratch, lanes):
    out = []
    for i in range(3):
        along_x, along_y, along_z = signed(spread(plus, i, scratch, lanes))
        out.append(along_x + along_y + along_z)
    return out


def start_kernel(
    even, state_hbm, neighbour_hbm, send_list_hbm,
    velocity, keys, picks, faces, late, traces, send_one, send_two,
    state, neighbour, send_list, values, stage, sems,
):
    copies = [
        pltpu.make_async_copy(source, target, sems.at[k])
        for k, (source, target) in enumerate((
            (neighbour_hbm, neighbour), (send_list_hbm, send_list),
            (state_hbm.at[0:3], state),
        ))
    ]
    for copy in copies:
        copy.start()
    for copy in copies[0:2]:
        copy.wait()
    width = neighbour.shape[1]
    cap = send_list.shape[1]
    is_even = even[0] == 1
    code = neighbour[...]
    low = code < width + cap
    at = code - width - jnp.where(low, 0, cap)
    second = jnp.where(low == is_even, 0, 1)
    place = jnp.where(
        at < MAIN, at + MAIN * second, at - MAIN + 2 * MAIN + TAIL * second
    )
    keys[...] = jnp.where(code < width, code, width + place)
    valid = jnp.where(jnp.max(code, axis=0, keepdims=True) >= 0, 1.0, 0.0)
    entries = send_list[...]
    entries = jnp.concatenate(
        [entries, jnp.full((2, MAIN + TAIL - cap), -1, jnp.int32)], axis=1
    )
    one, two = entries[0:1], entries[1:2]
    one, two = jnp.where(is_even, one, two), jnp.where(is_even, two, one)
    late[...] = jnp.concatenate([one[:, MAIN:], two[:, MAIN:]], axis=1)
    main = jnp.concatenate([one[:, 0:MAIN], two[:, 0:MAIN]], axis=1)
    face = jnp.zeros_like(main)
    for f in range(1, 6):
        face = face + jnp.where(main >= f * width, 1, 0)
    faces[...] = face
    slots = main - face * width
    for s in chunks(2 * MAIN):
        picks[:, s] = onehot(slots[:, s], width)
    copies[2].wait()
    for lanes in chunks(width):
        mask = valid[:, lanes]
        now = [state[i, :, lanes] * mask for i in range(3)]
        for i in range(3):
            velocity[i, :, lanes] = now[i]
        vel_traces(traces, lanes, now, stage)
    pack(traces, values, picks, faces, late, send_one, send_two)


def vel_local_kernel(
    step, velocity, stress, traces, keys, lame, shear, vel, *rest,
):
    total = None
    *rest, scratch = rest
    scratch[...] = jnp.zeros(scratch.shape, f32)
    if step < 0:
        stress_out, jump_out, hots = rest
    elif step == 0:
        hots, forward, stress_out, jump_out, total_out = rest
    else:
        hots, forward, total, stress_out, jump_out, total_out = rest
    width = velocity.shape[2]
    for lanes in chunks(width):
        if step < 0:
            for f in range(6):
                hots[f, :, lanes] = onehot(keys[f:f + 1, lanes] & (CHUNK - 1), CHUNK)
            valid = jnp.where(jnp.max(keys[:, lanes], axis=0, keepdims=True) >= 0, 1.0, 0.0)
        plus = local_faces(traces, keys[:, lanes], hots, lanes, 1.0)
        grad, jump = lift_velocity(plus, scratch, lanes)
        own = -lift_half * holders(CHUNK)
        whole = []
        for i in range(3):
            now = velocity[i, :, lanes]
            high, low = split(now)
            got = mm(vel[...], jnp.concatenate([high, low, high], axis=0))
            whole.append([got[64 * j:64 * j + 64] + grad[i][j] for j in range(3)])
            jump_out[i, :, lanes] = own * now + jump[i]
        rate = rate_of(whole, lame[:, lanes], shear[:, lanes])
        for m in range(6):
            if step < 0:
                old = stress[3 + m, :, lanes] * valid
            else:
                old = stress[m, :, lanes]
            stress_out[m, :, lanes] = old + time_step * rate[m]
        if step >= 0:
            term = rho_term(forward, step, velocity, lanes)
            total_out[:, lanes] = term if total is None else total[:, lanes] + term


def rho_term(forward, step, velocity, lanes):
    acc = forward[step, 0, :, lanes] * velocity[0, :, lanes]
    acc = acc + forward[step, 1, :, lanes] * velocity[1, :, lanes]
    acc = acc + forward[step, 2, :, lanes] * velocity[2, :, lanes]
    return -time_step * acc


def vel_halo_kernel(
    stress, jump, recv_one, recv_two, keys, hots, picks, faces, late, lame, shear,
    stress_out, jump_out, traces, send_one, send_two, values, scratch, stage,
):
    width = stress.shape[2]
    scratch[...] = jnp.zeros(scratch.shape, f32)
    lhs, tail = halo_lhs(recv_one, recv_two)
    for lanes in chunks(width):
        plus = halo_faces(lhs, tail, keys[:, lanes], hots, lanes, width)
        grad, more = lift_velocity(plus, scratch, lanes)
        rate = rate_of(grad, lame[:, lanes], shear[:, lanes])
        now = [stress[m, :, lanes] + time_step * rate[m] for m in range(6)]
        for m in range(6):
            stress_out[m, :, lanes] = now[m]
        for i in range(3):
            jump_out[i, :, lanes] = jump[i, :, lanes] + more[i]
        str_traces(traces, lanes, now, stage)
    pack(traces, values, picks, faces, late, send_one, send_two)


def str_local_kernel(
    step, velocity, stress, jump, traces, keys, hots, density, lame, shear, div, *rest,
):
    *rest, scratch = rest
    scratch[...] = jnp.zeros(scratch.shape, f32)
    forward = fwd = total = total_out = None
    if len(rest) == 1:
        velocity_out, = rest
    elif len(rest) == 4:
        forward, fwd, velocity_out, total_out = rest
    else:
        forward, fwd, total, velocity_out, total_out = rest
    width = velocity.shape[2]
    for lanes in chunks(width):
        plus = local_faces(traces, keys[:, lanes], hots, lanes, -1.0)
        lifted = lift_stress(plus, scratch, lanes)
        now = [stress[m, :, lanes] for m in range(6)]
        pieces = [split(s) for s in now]
        rho = density[:, lanes]
        impedance = jnp.sqrt(rho * (lame[:, lanes] + 2.0 * shear[:, lanes]))
        scale = time_step / rho
        for i in range(3):
            rows = []
            for m in symmetric_index[i]:
                rows += [pieces[m][0], pieces[m][1], pieces[m][0]]
            got = mm(div[...], jnp.concatenate(rows, axis=0))
            velocity_out[i, :, lanes] = velocity[i, :, lanes] + scale * (
                got + lifted[i] + impedance * jump[i, :, lanes]
            )
        if total_out is not None:
            event_terms(step, now, forward, fwd, total, total_out, lanes)


def event_terms(step, now, forward, fwd, total, total_out, lanes):
    grad = []
    for i in range(3):
        high, low = split(forward[step, i, :, lanes])
        got = mm(fwd[...], jnp.concatenate([high, low, high], axis=0))
        grad.append([got[64 * j:64 * j + 64] for j in range(3)])
    diag = (grad[0][0], grad[1][1], grad[2][2])
    lame_term = -time_step * (diag[0] + diag[1] + diag[2]) * (now[0] + now[1] + now[2])
    shear_term = (-2.0 * time_step) * (
        diag[0] * now[0]
        + diag[1] * now[1]
        + diag[2] * now[2]
        + (grad[0][1] + grad[1][0]) * now[3]
        + (grad[0][2] + grad[2][0]) * now[4]
        + (grad[1][2] + grad[2][1]) * now[5]
    )
    for m, term in enumerate((lame_term, shear_term)):
        rows = total_out.shape[2]
        for e in range(total_out.shape[0]):
            share = term[rows * e:rows * e + rows]
            if total is not None:
                share = total[e, m, :, lanes] + share
            total_out[e, m, :, lanes] = share


def terms_kernel(step, stress, forward, fwd, *rest):
    *total, total_out = rest
    total = total[0] if total else None
    for lanes in chunks(stress.shape[2]):
        now = [stress[m, :, lanes] for m in range(6)]
        event_terms(step, now, forward, fwd, total, total_out, lanes)


def str_halo_kernel(
    velocity, recv_one, recv_two, keys, hots, picks, faces, late, density,
    velocity_out, traces, send_one, send_two, values, scratch, stage,
):
    halo_velocity(velocity, recv_one, recv_two, keys, hots, density, velocity_out, traces, scratch, stage)
    pack(traces, values, picks, faces, late, send_one, send_two)


def last_kernel(
    step, velocity, recv_one, recv_two, keys, hots, density, forward, *rest
):
    *total, velocity_out, total_out, scratch = rest
    total = total[0] if total else None
    halo_velocity(velocity, recv_one, recv_two, keys, hots, density, velocity_out, None, scratch, None)
    for lanes in chunks(velocity.shape[2]):
        term = rho_term(forward, step, velocity_out, lanes)
        if total is not None:
            term = total[:, lanes] + term
        rows = total_out.shape[2]
        for e in range(total_out.shape[0]):
            total_out[e, 0, :, lanes] = term[rows * e:rows * e + rows]


def event_sum_kernel(rho, other, out):
    width = rho.shape[3]
    for m, (parts, at) in enumerate(((rho, 0), (other, 0), (other, 1))):
        total = parts[0, at]
        for e in range(1, parts.shape[0]):
            total = total + parts[e, at]
        for k in range(total.shape[0]):
            out[m, :, k * width:(k + 1) * width] = total[k:k + 1]


def halo_velocity(
    velocity, recv_one, recv_two, keys, hots, density, velocity_out, traces, scratch, stage
):
    width = velocity.shape[2]
    scratch[...] = jnp.zeros(scratch.shape, f32)
    lhs, tail = halo_lhs(recv_one, recv_two)
    for lanes in chunks(width):
        plus = halo_faces(lhs, tail, keys[:, lanes], hots, lanes, width)
        lifted = lift_stress(plus, scratch, lanes)
        scale = time_step / density[:, lanes]
        now = [velocity[i, :, lanes] + scale * lifted[i] for i in range(3)]
        for i in range(3):
            velocity_out[i, :, lanes] = now[i]
        if traces is not None:
            vel_traces(traces, lanes, now, stage)


def call(name, kernel, args, outs, specs=None, cost=0, scratch=()):
    whole = pl.BlockSpec(memory_space=pltpu.VMEM)
    specs = specs or {}
    return pl.pallas_call(
        kernel,
        name=name,
        in_specs=[specs.get(k, whole) for k in range(len(args))],
        out_specs=[whole] * len(outs),
        out_shape=[jax.ShapeDtypeStruct(s, d) for s, d in outs],
        scratch_shapes=list(scratch),
        compiler_params=pltpu.CompilerParams(vmem_limit_bytes=VMEM_LIMIT),
        cost_estimate=pl.CostEstimate(flops=cost, bytes_accessed=6_000_000, transcendentals=0),
    )(*args)


def swap(sent, axis):
    count = lax.axis_size(axis)
    got = []
    for first, value in enumerate(sent):
        pairs = []
        for low in range(1 - first, count - 1, 2):
            pairs += [(low, low + 1), (low + 1, low)]
        got.append(lax.ppermute(value, axis, pairs))
    return got


def local(
    adjoint_state, forward_velocity, density, lame_lambda, shear_modulus, neighbour, send_list
):
    width = density.shape[1]
    steps = forward_velocity.shape[1]
    table = {k: jnp.asarray(v) for k, v in tables().items()}
    state = adjoint_state[0]
    forward = forward_velocity[0]
    even = (1 - lax.axis_index("dom") % 2).astype(jnp.int32).reshape(1)

    nodal = pltpu.VMEM((3, width // 128, 64, 128), f32)
    values = pltpu.VMEM((288, width), f32)
    field = ((64, width), f32)
    vector = ((3, 64, width), f32)
    tensor = ((6, 64, width), f32)
    count = lax.axis_size("event")
    shares = count if 64 % (8 * count) == 0 else 1
    two = ((shares, 2, 64 // shares, width), f32)
    one = ((shares, 1, 64 // shares, width), f32)
    trace = ((576, width), bf16)
    hot = ((6, CHUNK, width), bf16)
    sends = [((SEND_ROWS, 128), f32)] * 2
    lists = [((6, width), jnp.int32), ((width, 2 * MAIN), bf16),
             ((1, 2 * MAIN), jnp.int32), ((1, 2 * TAIL), jnp.int32)]

    velocity, keys, picks, faces, late, traces, *sent = call(
        "start", start_kernel,
        (even, *(pltpu.with_memory_space_constraint(x, pltpu.HBM)
                for x in (state, neighbour, send_list))),
        [vector] + lists + [trace] + sends,
        specs={0: pl.BlockSpec(memory_space=pltpu.SMEM)}
        | {k: pl.BlockSpec(memory_space=pltpu.HBM) for k in range(1, 4)},
        scratch=[
            pltpu.VMEM((3, 64, width), f32), pltpu.VMEM(neighbour.shape, jnp.int32),
            pltpu.VMEM(send_list.shape, jnp.int32), values, nodal, pltpu.SemaphoreType.DMA((3,)),
        ],
    )
    rho_total = other_total = hots = None
    stress = state
    for n in range(steps):
        recv = swap(sent, "dom")
        args = [velocity, stress, traces, keys, lame_lambda, shear_modulus,
                table["vel"]]
        outs = [tensor, vector]
        if n:
            args += [hots, forward] + ([rho_total] if n > 1 else [])
            outs += [field]
        else:
            outs += [hot]
        stress, jump, more = call(
            "vel_local", functools.partial(vel_local_kernel, n - 1), args, outs, cost=4_000_000_000,
            scratch=[nodal],
        )
        if n:
            rho_total = more
        else:
            hots = more
        stress, jump, traces, *sent = call(
            "vel_halo", vel_halo_kernel,
            (stress, jump, *recv, keys, hots, picks, faces, late, lame_lambda, shear_modulus),
            [tensor, vector, trace] + sends, scratch=[values, nodal, nodal],
        )
        recv = swap(sent, "dom")
        args = [velocity, stress, jump, traces, keys, hots, density, lame_lambda, shear_modulus,
                table["div"]]
        before = [other_total] if n else []
        if n < steps - 1:
            velocity, other_total = call(
                "str_local", functools.partial(str_local_kernel, n),
                args + [forward, table["fwd"]] + before, [vector, two],
                cost=4_000_000_000, scratch=[nodal],
            )
        else:
            other_total, = call(
                "terms", functools.partial(terms_kernel, n),
                [stress, forward, table["fwd"]] + before, [two], cost=1_000_000_000,
            )
            if shares == count:
                other_total = lax.all_to_all(other_total, "event", 0, 0, tiled=True)
            velocity, = call(
                "str_local", functools.partial(str_local_kernel, n), args, [vector],
                cost=4_000_000_000, scratch=[nodal],
            )
        if n < steps - 1:
            velocity, traces, *sent = call(
                "str_halo", str_halo_kernel,
                (velocity, *recv, keys, hots, picks, faces, late, density),
                [vector, trace] + sends, scratch=[values, nodal, nodal],
            )
        else:
            velocity, rho_total = call(
                "last", functools.partial(last_kernel, n),
                (velocity, *recv, keys, hots, density, forward)
                + ((rho_total,) if n else ()),
                [vector, one], scratch=[nodal], cost=4_000_000_000,
            )

    if shares == count:
        parts = (lax.all_to_all(rho_total, "event", 0, 0, tiled=True), other_total)
        kernels, = call(
            "event_sum", event_sum_kernel, parts, [((3, 1, 64 // count * width), f32)]
        )
    else:
        flat = jnp.concatenate([rho_total, other_total], axis=1).reshape(3, -1)
        part = lax.psum_scatter(flat, "event", scatter_dimension=1, tiled=True)
        kernels = part.reshape(3, 1, -1)
    return velocity[None], kernels


def solution(mesh):
    placed = (
        P("event", None, None, "dom"),
        P("event", None, None, None, "dom"),
        P(None, "dom"),
        P(None, "dom"),
        P(None, "dom"),
        P(None, "dom"),
        P(None, "dom"),
    )
    return jax.shard_map(
        local,
        mesh=mesh,
        in_specs=placed,
        out_specs=(P("event", None, None, "dom"), P(None, "dom", "event")),
        check_vma=False,
    )
```

```python
import functools
import math

import jax
import jax.numpy as jnp
import numpy as np
from jax import lax
from jax.experimental import pallas as pl
from jax.experimental.pallas import tpu as pltpu
from jax.sharding import PartitionSpec as P

time_step = 0.02
lift_half = 3.0
symmetric_index = ((0, 3, 4), (3, 1, 5), (4, 5, 2))
f32 = jnp.float32
bf16 = jnp.bfloat16
CHUNK = 256
MAIN = 384
TAIL = 64
SEND_MAIN = 48 * MAIN // 128
SEND_ROWS = SEND_MAIN + 48 * TAIL // 128
VMEM_LIMIT = 40 * 2**20


def lobatto_diff():
    points = [-1.0, -1.0 / math.sqrt(5.0), 1.0 / math.sqrt(5.0), 1.0]
    weights = [
        1.0 / math.prod([points[t] - points[o] for o in range(4) if o != t]) for t in range(4)
    ]
    offdiag = [
        [
            0.0 if t == s else weights[s] / weights[t] / (points[t] - points[s])
            for s in range(4)
        ]
        for t in range(4)
    ]
    return np.array(
        [[-sum(offdiag[t]) if t == s else offdiag[t][s] for s in range(4)] for t in range(4)],
        dtype=np.float64,
    )


def kron3(first, second, third):
    return np.kron(np.kron(first, second), third)


def deriv_parts(inner):
    matrix = lobatto_diff()
    if inner:
        matrix = matrix + np.diag([lift_half, 0.0, 0.0, -lift_half])
    matrix = matrix.astype(np.float32)
    eye = np.eye(4, dtype=np.float32)
    stack = [kron3(matrix, eye, eye), kron3(eye, matrix, eye), kron3(eye, eye, matrix)]
    high = [np.asarray(m.astype(bf16)) for m in stack]
    low = [np.asarray((m - h.astype(np.float32)).astype(bf16)) for m, h in zip(stack, high)]
    return [h.astype(np.float32) for h in high], [l.astype(np.float32) for l in low]


def tables():
    high, low = deriv_parts(True)
    plain_high, plain_low = deriv_parts(False)

    def rows(upper, lower):
        return np.concatenate(
            [np.concatenate([upper[j], upper[j], lower[j]], axis=1) for j in range(3)], axis=0
        )

    vel = rows(high, low)
    fwd = rows(plain_high, plain_low)
    div = np.concatenate([m for j in range(3) for m in (high[j], high[j], low[j])], axis=1)
    return {
        name: np.asarray(value).astype(bf16) for name, value in dict(vel=vel, fwd=fwd, div=div).items()
    }


def split(value):
    high = value.astype(bf16)
    return high, (value - high.astype(f32)).astype(bf16)


def mm(left, right):
    return jnp.dot(left, right, preferred_element_type=f32)


def onehot(row, depth):
    ids = lax.broadcasted_iota(jnp.int32, (depth, row.shape[-1]), 0)
    return jnp.where(ids == row, 1.0, 0.0).astype(bf16)


def chunks(width):
    return [slice(c, c + CHUNK) for c in range(0, width, CHUNK)]


def top_half(shape):
    return lax.broadcasted_iota(jnp.int32, shape, 0) < 4


def tiles_of(lanes):
    return [(lanes.start // 128 + t, slice(128 * t, 128 * t + 128)) for t in range(CHUNK // 128)]


def z_faces(value, stage, lanes):
    low, high = [], []
    for tile, at in tiles_of(lanes):
        stage[tile] = value[:, at]
        low.append(stage[tile, pl.ds(0, 16, stride=4)])
        high.append(stage[tile, pl.ds(3, 16, stride=4)])
    return jnp.concatenate(low, axis=1), jnp.concatenate(high, axis=1)


def xy_faces(value):
    top = top_half((8, value.shape[1]))

    def rows(at):
        return value[at:at + 8]

    def turned(at):
        return pltpu.roll(value[at:at + 8], 4, 0)

    low_y = [jnp.where(top, rows(at), turned(at + 16)) for at in (0, 32)]
    high_y = [jnp.where(top, turned(at), rows(at + 16)) for at in (8, 40)]
    return [
        value[0:16],
        value[48:64],
        jnp.concatenate(low_y, axis=0),
        jnp.concatenate(high_y, axis=0),
    ]


def spread(faces, comp, scratch, lanes):
    low_x, high_x, low_y, high_y, low_z, high_z = (
        p[16 * comp:16 * comp + 16] for p in faces
    )
    width = low_x.shape[1]
    top = top_half((8, width))
    none = jnp.zeros((8, width), f32)
    along_y = []
    for a in range(4):
        first = low_y[8 * (a // 2):8 * (a // 2) + 8]
        second = high_y[8 * (a // 2):8 * (a // 2) + 8]
        first, second = (
            (pltpu.roll(first, 4, 0), second) if a % 2 else (first, pltpu.roll(second, 4, 0))
        )
        along_y += [jnp.where(top, first, none), jnp.where(top, none, second)]
    along_z = []
    for tile, at in tiles_of(lanes):
        scratch[comp, tile, pl.ds(0, 16, stride=4)] = low_z[:, at]
        scratch[comp, tile, pl.ds(3, 16, stride=4)] = high_z[:, at]
        along_z.append(scratch[comp, tile])
    return (
        jnp.concatenate([low_x, none, none, none, none, high_x], axis=0),
        jnp.concatenate(along_y, axis=0),
        jnp.concatenate(along_z, axis=1),
    )


def signed(fields):
    along_x, along_y, along_z = fields
    width = along_x.shape[1]
    node = lax.broadcasted_iota(jnp.int32, (8, width), 0) & 3
    sign = jnp.where(node == 0, -1.0, 1.0)
    return (
        jnp.concatenate([-along_x[0:16], along_x[16:64]], axis=0),
        jnp.concatenate(
            [along_y[8 * b:8 * b + 8] if b % 2 else -along_y[8 * b:8 * b + 8] for b in range(8)],
            axis=0,
        ),
        jnp.concatenate([sign * along_z[8 * b:8 * b + 8] for b in range(8)], axis=0),
    )


def holders(width):
    node = lax.broadcasted_iota(jnp.int32, (64, width), 0)
    total = jnp.zeros((64, width), f32)
    for index in (node >> 4, (node >> 2) & 3, node & 3):
        total = total + jnp.where((index == 0) | (index == 3), 1.0, 0.0)
    return total


def gather_tile(source, lane):
    lane = jnp.broadcast_to(lane, (8, 128))
    return jnp.concatenate(
        [jnp.take_along_axis(source[r:r + 8], lane, axis=1) for r in range(0, 48, 8)], axis=0
    )


def halo_faces(lhs, tail, keys, hots, lanes, width):
    blocks = 2 * MAIN // CHUNK
    first = width // CHUNK
    out = []
    for f in range(6):
        key = keys[f:f + 1]
        got = mm(lhs, hots[f, :, lanes])
        which = key >> 8
        late = jnp.concatenate(
            [gather_tile(tail, key[:, t:t + 128] & 127) for t in range(0, CHUNK, 128)], axis=1
        )
        total = jnp.where(which == first + blocks, late, 0.0)
        for a in range(blocks):
            both = got[48 * a:48 * a + 48] + got[48 * (blocks + a):48 * (blocks + a) + 48]
            total = jnp.where(which == first + a, both, total)
        out.append(total)
    return out


def halo_lhs(recv_one, recv_two):
    tiles = [
        recv[48 * t:48 * t + 48] for recv in (recv_one, recv_two) for t in range(MAIN // 128)
    ]
    blocks = [jnp.concatenate(tiles[t:t + 2], axis=1) for t in range(0, len(tiles), 2)]
    high, low = split(jnp.concatenate(blocks, axis=0))
    one, two = recv_one[SEND_MAIN:SEND_ROWS], recv_two[SEND_MAIN:SEND_ROWS]
    tail = jnp.concatenate(
        [
            jnp.concatenate([one[:, 0:TAIL], two[:, 0:TAIL]], axis=1),
            jnp.concatenate([one[:, TAIL:2 * TAIL], two[:, TAIL:2 * TAIL]], axis=1),
        ],
        axis=0,
    )
    return jnp.concatenate([high, low], axis=0), tail


def local_faces(traces, keys, hots, lanes, own_sign):
    width = traces.shape[1]
    blocks = width // CHUNK
    out = []
    for f in range(6):
        key = keys[f:f + 1]
        other = 48 * (f ^ 1)
        lhs = jnp.concatenate(
            [traces[p + other:p + other + 48, s] for p in (0, 288) for s in chunks(width)], axis=0
        )
        got = mm(lhs, hots[f, :, lanes])
        which = key >> 8
        own = traces[48 * f:48 * f + 48, lanes].astype(f32)
        own = own + traces[288 + 48 * f:288 + 48 * f + 48, lanes].astype(f32)
        total = jnp.where(which < 0, own_sign * own, 0.0)
        for a in range(blocks):
            both = got[48 * a:48 * a + 48] + got[48 * (blocks + a):48 * (blocks + a) + 48]
            total = jnp.where(which == a, both, total)
        out.append(total)
    return out


def put_traces(traces, values, lanes, comp, face, value):
    at = 48 * face + 16 * comp
    values[at:at + 16, lanes] = value
    traces[at:at + 16, lanes], traces[288 + at:288 + at + 16, lanes] = split(value)


def vel_traces(traces, values, lanes, velocity, stage):
    for i in range(3):
        faces = (*xy_faces(velocity[i]), *z_faces(velocity[i], stage.at[i], lanes))
        for f, value in enumerate(faces):
            put_traces(traces, values, lanes, i, f, value)


def str_traces(traces, values, lanes, stress, stage):
    faces = [xy_faces(stress[m]) for m in range(6)]
    for i in range(3):
        for f in range(4):
            put_traces(traces, values, lanes, i, f, faces[symmetric_index[i][f // 2]][f])
        for f, value in enumerate(z_faces(stress[symmetric_index[i][2]], stage.at[i], lanes)):
            put_traces(traces, values, lanes, i, 4 + f, value)


def pack(traces, values, picks, faces, late, send_one, send_two):
    width = traces.shape[1]
    pieces = []
    for s in chunks(2 * MAIN):
        face = faces[:, s]
        got = mm(traces[...], picks[:, s])
        total = jnp.zeros((48, CHUNK), f32)
        for f in range(6):
            both = got[48 * f:48 * f + 48] + got[288 + 48 * f:288 + 48 * f + 48]
            total = jnp.where(face == f, both, total)
        pieces.append(total)
    whole = jnp.concatenate(pieces, axis=1)
    for t in range(MAIN // 128):
        for first, send in ((0, send_one), (MAIN, send_two)):
            send[48 * t:48 * t + 48] = whole[:, first + 128 * t:first + 128 * t + 128]
    key = late[...]
    lane = key & 127
    which = jnp.broadcast_to(key >> 7, (48, 128))
    total = jnp.zeros((48, 128), f32)
    for f in range(6):
        for a in range(width // 128):
            got = gather_tile(values[48 * f:48 * f + 48, 128 * a:128 * a + 128], lane)
            total = jnp.where(which == f * (width // 128) + a, got, total)
    one, two = total[:, 0:TAIL], total[:, TAIL:2 * TAIL]
    send_one[SEND_MAIN:SEND_ROWS] = jnp.concatenate([one[0:24], one[24:48]], axis=1)
    send_two[SEND_MAIN:SEND_ROWS] = jnp.concatenate([two[0:24], two[24:48]], axis=1)


def rate_of(grad, lame, shear):
    trace = lame * (grad[0][0] + grad[1][1] + grad[2][2])
    return [
        trace + 2.0 * shear * grad[0][0],
        trace + 2.0 * shear * grad[1][1],
        trace + 2.0 * shear * grad[2][2],
        shear * (grad[0][1] + grad[1][0]),
        shear * (grad[0][2] + grad[2][0]),
        shear * (grad[1][2] + grad[2][1]),
    ]


def lift_velocity(plus, scratch, lanes):
    grad, jump = [], []
    for i in range(3):
        fields = spread(plus, i, scratch, lanes)
        grad.append(signed(fields))
        jump.append(fields[0] + fields[1] + fields[2])
    return grad, jump


def lift_stress(plus, scratch, lanes):
    out = []
    for i in range(3):
        along_x, along_y, along_z = signed(spread(plus, i, scratch, lanes))
        out.append(along_x + along_y + along_z)
    return out


def start_kernel(
    even, state_hbm, neighbour_hbm, send_list_hbm,
    velocity, stress, keys, picks, faces, late, traces, send_one, send_two,
    state, neighbour, send_list, values, stage, sems,
):
    copies = [
        pltpu.make_async_copy(source, target, sems.at[k])
        for k, (source, target) in enumerate((
            (neighbour_hbm, neighbour), (send_list_hbm, send_list),
            (state_hbm.at[0:3], state.at[0:3]), (state_hbm.at[3:9], state.at[3:9]),
        ))
    ]
    for copy in copies:
        copy.start()
    for copy in copies[0:2]:
        copy.wait()
    width = neighbour.shape[1]
    cap = send_list.shape[1]
    is_even = even[0] == 1
    code = neighbour[...]
    low = code < width + cap
    at = code - width - jnp.where(low, 0, cap)
    second = jnp.where(low == is_even, 0, 1)
    place = jnp.where(
        at < MAIN, at + MAIN * second, at - MAIN + 2 * MAIN + TAIL * second
    )
    keys[...] = jnp.where(code < width, code, width + place)
    valid = jnp.where(jnp.max(code, axis=0, keepdims=True) >= 0, 1.0, 0.0)
    entries = send_list[...]
    entries = jnp.concatenate(
        [entries, jnp.full((2, MAIN + TAIL - cap), -1, jnp.int32)], axis=1
    )
    one, two = entries[0:1], entries[1:2]
    one, two = jnp.where(is_even, one, two), jnp.where(is_even, two, one)
    late[...] = jnp.concatenate([one[:, MAIN:], two[:, MAIN:]], axis=1)
    main = jnp.concatenate([one[:, 0:MAIN], two[:, 0:MAIN]], axis=1)
    face = jnp.zeros_like(main)
    for f in range(1, 6):
        face = face + jnp.where(main >= f * width, 1, 0)
    faces[...] = face
    slots = main - face * width
    for s in chunks(2 * MAIN):
        picks[:, s] = onehot(slots[:, s], width)
    copies[2].wait()
    for lanes in chunks(width):
        mask = valid[:, lanes]
        now = [state[i, :, lanes] * mask for i in range(3)]
        for i in range(3):
            velocity[i, :, lanes] = now[i]
        vel_traces(traces, values, lanes, now, stage)
    pack(traces, values, picks, faces, late, send_one, send_two)
    copies[3].wait()
    for lanes in chunks(width):
        for i in range(6):
            stress[i, :, lanes] = state[3 + i, :, lanes] * valid[:, lanes]


def vel_local_kernel(
    step, velocity, stress, traces, keys, lame, shear, vel, *rest,
):
    total = None
    *rest, scratch = rest
    scratch[...] = jnp.zeros(scratch.shape, f32)
    if step < 0:
        stress_out, jump_out, hots, lame_scaled, shear_scaled = rest
    elif step == 0:
        hots, forward, stress_out, jump_out, total_out = rest
    else:
        hots, forward, total, stress_out, jump_out, total_out = rest
    width = velocity.shape[2]
    for lanes in chunks(width):
        if step < 0:
            for f in range(6):
                hots[f, :, lanes] = onehot(keys[f:f + 1, lanes] & (CHUNK - 1), CHUNK)
            lame_scaled[:, lanes] = (lift_half * time_step) * lame[:, lanes]
            shear_scaled[:, lanes] = (lift_half * time_step) * shear[:, lanes]
        plus = local_faces(traces, keys[:, lanes], hots, lanes, 1.0)
        grad, jump = lift_velocity(plus, scratch, lanes)
        count = holders(CHUNK)
        whole = []
        for i in range(3):
            now = velocity[i, :, lanes]
            high, low = split(now)
            got = mm(vel[...], jnp.concatenate([high, low, high], axis=0))
            whole.append([got[64 * j:64 * j + 64] + lift_half * grad[i][j] for j in range(3)])
            jump_out[i, :, lanes] = jump[i] - count * now
        rate = rate_of(whole, lame[:, lanes], shear[:, lanes])
        for m in range(6):
            stress_out[m, :, lanes] = stress[m, :, lanes] + time_step * rate[m]
        if step >= 0:
            term = rho_term(forward, step, velocity, lanes)
            total_out[:, lanes] = term if total is None else total[:, lanes] + term


def rho_term(forward, step, velocity, lanes):
    acc = forward[step, 0, :, lanes] * velocity[0, :, lanes]
    acc = acc + forward[step, 1, :, lanes] * velocity[1, :, lanes]
    acc = acc + forward[step, 2, :, lanes] * velocity[2, :, lanes]
    return -time_step * acc


def vel_halo_kernel(
    stress, jump, recv_one, recv_two, keys, hots, picks, faces, late, lame_scaled, shear_scaled,
    stress_out, jump_out, traces, send_one, send_two, values, scratch, stage,
):
    width = stress.shape[2]
    scratch[...] = jnp.zeros(scratch.shape, f32)
    lhs, tail = halo_lhs(recv_one, recv_two)
    for lanes in chunks(width):
        plus = halo_faces(lhs, tail, keys[:, lanes], hots, lanes, width)
        grad, more = lift_velocity(plus, scratch, lanes)
        rate = rate_of(grad, lame_scaled[:, lanes], shear_scaled[:, lanes])
        now = [stress[m, :, lanes] + rate[m] for m in range(6)]
        for m in range(6):
            stress_out[m, :, lanes] = now[m]
        for i in range(3):
            jump_out[i, :, lanes] = jump[i, :, lanes] + more[i]
        str_traces(traces, values, lanes, now, stage)
    pack(traces, values, picks, faces, late, send_one, send_two)


def str_local_kernel(
    step, velocity, stress, jump, traces, keys, hots, density, lame, shear, forward, div, fwd, *rest,
):
    *rest, scratch = rest
    scratch[...] = jnp.zeros(scratch.shape, f32)
    if step == 0:
        total = None
        velocity_out, total_out, scale_out = rest
    else:
        total, velocity_out, total_out = rest
    width = velocity.shape[2]
    for lanes in chunks(width):
        plus = local_faces(traces, keys[:, lanes], hots, lanes, -1.0)
        lifted = lift_stress(plus, scratch, lanes)
        now = [stress[m, :, lanes] for m in range(6)]
        pieces = [split(s) for s in now]
        rho = density[:, lanes]
        impedance = jnp.sqrt(rho * (lame[:, lanes] + 2.0 * shear[:, lanes]))
        scale = time_step / rho
        if step == 0:
            scale_out[:, lanes] = lift_half * scale
        for i in range(3):
            rows = []
            for m in symmetric_index[i]:
                rows += [pieces[m][0], pieces[m][1], pieces[m][0]]
            got = mm(div[...], jnp.concatenate(rows, axis=0))
            velocity_out[i, :, lanes] = velocity[i, :, lanes] + scale * (
                got + lift_half * (lifted[i] + impedance * jump[i, :, lanes])
            )
        grad = []
        for i in range(3):
            high, low = split(forward[step, i, :, lanes])
            got = mm(fwd[...], jnp.concatenate([high, low, high], axis=0))
            grad.append([got[64 * j:64 * j + 64] for j in range(3)])
        diag = (grad[0][0], grad[1][1], grad[2][2])
        lame_term = -time_step * (diag[0] + diag[1] + diag[2]) * (now[0] + now[1] + now[2])
        shear_term = (-2.0 * time_step) * (
            diag[0] * now[0]
            + diag[1] * now[1]
            + diag[2] * now[2]
            + (grad[0][1] + grad[1][0]) * now[3]
            + (grad[0][2] + grad[2][0]) * now[4]
            + (grad[1][2] + grad[2][1]) * now[5]
        )
        for m, term in enumerate((lame_term, shear_term)):
            rows = total_out.shape[2]
            for e in range(total_out.shape[0]):
                share = term[rows * e:rows * e + rows]
                if total is not None:
                    share = total[e, m, :, lanes] + share
                total_out[e, m, :, lanes] = share


def str_halo_kernel(
    velocity, recv_one, recv_two, keys, hots, picks, faces, late, scale,
    velocity_out, traces, send_one, send_two, values, scratch, stage,
):
    halo_velocity(
        velocity, recv_one, recv_two, keys, hots, scale, velocity_out, traces, values, scratch, stage
    )
    pack(traces, values, picks, faces, late, send_one, send_two)


def last_kernel(
    step, velocity, recv_one, recv_two, keys, hots, scale, forward, other, *rest
):
    *total, velocity_out, total_out, scratch, buffer, sems = rest
    total = total[0] if total else None
    rows = total_out.shape[2]
    copies = []

    def finish(lanes):
        copy = pltpu.make_async_copy(
            buffer.at[:, :, lanes], velocity_out.at[:, :, lanes], sems.at[len(copies)]
        )
        copy.start()
        copies.append(copy)
        term = rho_term(forward, step, buffer, lanes)
        if total is not None:
            term = total[:, lanes] + term
        for e in range(total_out.shape[0]):
            total_out[e, 0, :, lanes] = term[rows * e:rows * e + rows]
            for m in range(2):
                total_out[e, m + 1, :, lanes] = other[e, m, :, lanes]

    halo_velocity(
        velocity, recv_one, recv_two, keys, hots, scale, buffer, None, None, scratch, None, finish
    )
    for copy in copies:
        copy.wait()


def event_sum_kernel(parts, out):
    width = parts.shape[3]
    for m in range(3):
        total = parts[0, m]
        for e in range(1, parts.shape[0]):
            total = total + parts[e, m]
        for k in range(total.shape[0]):
            out[m, :, k * width:(k + 1) * width] = total[k:k + 1]


def halo_velocity(
    velocity, recv_one, recv_two, keys, hots, scale, velocity_out, traces, values, scratch, stage,
    finish=None,
):
    width = velocity.shape[2]
    scratch[...] = jnp.zeros(scratch.shape, f32)
    lhs, tail = halo_lhs(recv_one, recv_two)
    for lanes in chunks(width):
        plus = halo_faces(lhs, tail, keys[:, lanes], hots, lanes, width)
        lifted = lift_stress(plus, scratch, lanes)
        now = [velocity[i, :, lanes] + scale[:, lanes] * lifted[i] for i in range(3)]
        for i in range(3):
            velocity_out[i, :, lanes] = now[i]
        if traces is not None:
            vel_traces(traces, values, lanes, now, stage)
        if finish is not None:
            finish(lanes)


def call(name, kernel, args, outs, specs=None, cost=0, scratch=(), out_specs=None):
    whole = pl.BlockSpec(memory_space=pltpu.VMEM)
    specs = specs or {}
    return pl.pallas_call(
        kernel,
        name=name,
        in_specs=[specs.get(k, whole) for k in range(len(args))],
        out_specs=out_specs or [whole] * len(outs),
        out_shape=[jax.ShapeDtypeStruct(s, d) for s, d in outs],
        scratch_shapes=list(scratch),
        compiler_params=pltpu.CompilerParams(vmem_limit_bytes=VMEM_LIMIT),
        cost_estimate=pl.CostEstimate(flops=cost, bytes_accessed=6_000_000, transcendentals=0),
    )(*args)


def swap(sent, axis):
    count = lax.axis_size(axis)
    got = []
    for first, value in enumerate(sent):
        pairs = []
        for low in range(1 - first, count - 1, 2):
            pairs += [(low, low + 1), (low + 1, low)]
        got.append(lax.ppermute(value, axis, pairs))
    return got


def local(
    adjoint_state, forward_velocity, density, lame_lambda, shear_modulus, neighbour, send_list
):
    width = density.shape[1]
    steps = forward_velocity.shape[1]
    table = {k: jnp.asarray(v) for k, v in tables().items()}
    state = adjoint_state[0]
    forward = forward_velocity[0]
    even = (1 - lax.axis_index("dom") % 2).astype(jnp.int32).reshape(1)

    nodal = pltpu.VMEM((3, width // 128, 64, 128), f32)
    values = pltpu.VMEM((288, width), f32)
    field = ((64, width), f32)
    vector = ((3, 64, width), f32)
    tensor = ((6, 64, width), f32)
    count = lax.axis_size("event")
    shares = count if 64 % (8 * count) == 0 else 1
    two = ((shares, 2, 64 // shares, width), f32)
    three = ((shares, 3, 64 // shares, width), f32)
    trace = ((576, width), bf16)
    hot = ((6, CHUNK, width), bf16)
    sends = [((SEND_ROWS, 128), f32)] * 2
    lists = [((6, width), jnp.int32), ((width, 2 * MAIN), bf16),
             ((1, 2 * MAIN), jnp.int32), ((1, 2 * TAIL), jnp.int32)]

    velocity, stress, keys, picks, faces, late, traces, *sent = call(
        "start", start_kernel,
        (even, *(pltpu.with_memory_space_constraint(x, pltpu.HBM)
                for x in (state, neighbour, send_list))),
        [vector, tensor] + lists + [trace] + sends,
        specs={0: pl.BlockSpec(memory_space=pltpu.SMEM)}
        | {k: pl.BlockSpec(memory_space=pltpu.HBM) for k in range(1, 4)},
        scratch=[
            pltpu.VMEM(state.shape, f32), pltpu.VMEM(neighbour.shape, jnp.int32),
            pltpu.VMEM(send_list.shape, jnp.int32), values, nodal, pltpu.SemaphoreType.DMA((4,)),
        ],
    )
    rho_total = other_total = hots = None
    for n in range(steps):
        recv = swap(sent, "dom")
        args = [velocity, stress, traces, keys, lame_lambda, shear_modulus,
                table["vel"]]
        outs = [tensor, vector]
        if n:
            args += [hots, forward] + ([rho_total] if n > 1 else [])
            outs += [field]
        else:
            outs += [hot, field, field]
        stress, jump, *more = call(
            "vel_local", functools.partial(vel_local_kernel, n - 1), args, outs, cost=4_000_000_000,
            scratch=[nodal],
        )
        if n:
            rho_total, = more
        else:
            hots, lame_scaled, shear_scaled = more
        stress, jump, traces, *sent = call(
            "vel_halo", vel_halo_kernel,
            (stress, jump, *recv, keys, hots, picks, faces, late, lame_scaled, shear_scaled),
            [tensor, vector, trace] + sends, scratch=[values, nodal, nodal],
        )
        recv = swap(sent, "dom")
        args = [velocity, stress, jump, traces, keys, hots, density, lame_lambda, shear_modulus,
                forward, table["div"], table["fwd"]]
        if n:
            args += [other_total]
        velocity, other_total, *more = call(
            "str_local", functools.partial(str_local_kernel, n), args,
            [vector, two] + ([] if n else [field]), cost=4_000_000_000, scratch=[nodal],
        )
        if not n:
            scale, = more
        if n < steps - 1:
            velocity, traces, *sent = call(
                "str_halo", str_halo_kernel,
                (velocity, *recv, keys, hots, picks, faces, late, scale),
                [vector, trace] + sends, scratch=[values, nodal, nodal],
            )
        else:
            velocity, kernel_total = call(
                "last", functools.partial(last_kernel, n),
                (velocity, *recv, keys, hots, scale, forward, other_total)
                + ((rho_total,) if n else ()),
                [vector, three],
                scratch=[
                    nodal, pltpu.VMEM((3, 64, width), f32),
                    pltpu.SemaphoreType.DMA((width // CHUNK,)),
                ],
                out_specs=[
                    pl.BlockSpec(memory_space=pl.ANY), pl.BlockSpec(memory_space=pltpu.VMEM)
                ],
            )

    if shares == count:
        parts = lax.all_to_all(kernel_total, "event", 0, 0, tiled=True)
        kernels, = call(
            "event_sum", event_sum_kernel, (parts,), [((3, 1, 64 // count * width), f32)]
        )
    else:
        flat = kernel_total.reshape(3, -1)
        part = lax.psum_scatter(flat, "event", scatter_dimension=1, tiled=True)
        kernels = part.reshape(3, 1, -1)
    return velocity[None], kernels


def solution(mesh):
    placed = (
        P("event", None, None, "dom"),
        P("event", None, None, None, "dom"),
        P(None, "dom"),
        P(None, "dom"),
        P(None, "dom"),
        P(None, "dom"),
        P(None, "dom"),
    )
    return jax.shard_map(
        local,
        mesh=mesh,
        in_specs=placed,
        out_specs=(P("event", None, None, "dom"), P(None, "dom", "event")),
        check_vma=False,
    )
```

```python
import functools
import math

import jax
import jax.numpy as jnp
import numpy as np
from jax import lax
from jax.experimental import pallas as pl
from jax.experimental.pallas import tpu as pltpu
from jax.sharding import PartitionSpec as P

time_step = 0.02
lift_half = 3.0
symmetric_index = ((0, 3, 4), (3, 1, 5), (4, 5, 2))
f32 = jnp.float32
bf16 = jnp.bfloat16
CHUNK = 256
MAIN = 256
MID = 128
TAIL = 64
SEND_MAIN = 48 * (MAIN + MID) // 128
SEND_ROWS = SEND_MAIN + 48 * TAIL // 128
VMEM_LIMIT = 40 * 2**20


def lobatto_diff():
    points = [-1.0, -1.0 / math.sqrt(5.0), 1.0 / math.sqrt(5.0), 1.0]
    weights = [
        1.0 / math.prod([points[t] - points[o] for o in range(4) if o != t]) for t in range(4)
    ]
    offdiag = [
        [
            0.0 if t == s else weights[s] / weights[t] / (points[t] - points[s])
            for s in range(4)
        ]
        for t in range(4)
    ]
    return np.array(
        [[-sum(offdiag[t]) if t == s else offdiag[t][s] for s in range(4)] for t in range(4)],
        dtype=np.float64,
    )


def kron3(first, second, third):
    return np.kron(np.kron(first, second), third)


def deriv_parts(inner):
    matrix = lobatto_diff()
    if inner:
        matrix = matrix + np.diag([lift_half, 0.0, 0.0, -lift_half])
    matrix = matrix.astype(np.float32)
    eye = np.eye(4, dtype=np.float32)
    stack = [kron3(matrix, eye, eye), kron3(eye, matrix, eye), kron3(eye, eye, matrix)]
    high = [np.asarray(m.astype(bf16)) for m in stack]
    low = [np.asarray((m - h.astype(np.float32)).astype(bf16)) for m, h in zip(stack, high)]
    return [h.astype(np.float32) for h in high], [l.astype(np.float32) for l in low]


def tables():
    high, low = deriv_parts(True)
    plain_high, plain_low = deriv_parts(False)

    def rows(upper, lower):
        return np.concatenate(
            [np.concatenate([upper[j], upper[j], lower[j]], axis=1) for j in range(3)], axis=0
        )

    vel = rows(high, low)
    fwd = rows(plain_high, plain_low)
    div = np.concatenate([m for j in range(3) for m in (high[j], high[j], low[j])], axis=1)
    return {
        name: np.asarray(value).astype(bf16) for name, value in dict(vel=vel, fwd=fwd, div=div).items()
    }


def split(value):
    high = value.astype(bf16)
    return high, (value - high.astype(f32)).astype(bf16)


def mm(left, right):
    return jnp.dot(left, right, preferred_element_type=f32)


def onehot(row, depth):
    ids = lax.broadcasted_iota(jnp.int32, (depth, row.shape[-1]), 0)
    return jnp.where(ids == row, 1.0, 0.0).astype(bf16)


def chunks(width):
    return [slice(c, c + CHUNK) for c in range(0, width, CHUNK)]


def top_half(shape):
    return lax.broadcasted_iota(jnp.int32, shape, 0) < 4


def tiles_of(lanes):
    return [(lanes.start // 128 + t, slice(128 * t, 128 * t + 128)) for t in range(CHUNK // 128)]


def z_faces(value, stage, lanes):
    low, high = [], []
    for tile, at in tiles_of(lanes):
        stage[tile] = value[:, at]
        low.append(stage[tile, pl.ds(0, 16, stride=4)])
        high.append(stage[tile, pl.ds(3, 16, stride=4)])
    return jnp.concatenate(low, axis=1), jnp.concatenate(high, axis=1)


def xy_faces(value):
    top = top_half((8, value.shape[1]))

    def rows(at):
        return value[at:at + 8]

    def turned(at):
        return pltpu.roll(value[at:at + 8], 4, 0)

    low_y = [jnp.where(top, rows(at), turned(at + 16)) for at in (0, 32)]
    high_y = [jnp.where(top, turned(at), rows(at + 16)) for at in (8, 40)]
    return [
        value[0:16],
        value[48:64],
        jnp.concatenate(low_y, axis=0),
        jnp.concatenate(high_y, axis=0),
    ]


def spread(faces, comp, scratch, lanes):
    low_x, high_x, low_y, high_y, low_z, high_z = (
        p[16 * comp:16 * comp + 16] for p in faces
    )
    width = low_x.shape[1]
    top = top_half((8, width))
    none = jnp.zeros((8, width), f32)
    along_y = []
    for a in range(4):
        first = low_y[8 * (a // 2):8 * (a // 2) + 8]
        second = high_y[8 * (a // 2):8 * (a // 2) + 8]
        first, second = (
            (pltpu.roll(first, 4, 0), second) if a % 2 else (first, pltpu.roll(second, 4, 0))
        )
        along_y += [jnp.where(top, first, none), jnp.where(top, none, second)]
    along_z = []
    for tile, at in tiles_of(lanes):
        scratch[comp, tile, pl.ds(0, 16, stride=4)] = low_z[:, at]
        scratch[comp, tile, pl.ds(3, 16, stride=4)] = high_z[:, at]
        along_z.append(scratch[comp, tile])
    return (
        jnp.concatenate([low_x, none, none, none, none, high_x], axis=0),
        jnp.concatenate(along_y, axis=0),
        jnp.concatenate(along_z, axis=1),
    )


def signed(fields):
    along_x, along_y, along_z = fields
    width = along_x.shape[1]
    node = lax.broadcasted_iota(jnp.int32, (8, width), 0) & 3
    sign = jnp.where(node == 0, -1.0, 1.0)
    return (
        jnp.concatenate([-along_x[0:16], along_x[16:64]], axis=0),
        jnp.concatenate(
            [along_y[8 * b:8 * b + 8] if b % 2 else -along_y[8 * b:8 * b + 8] for b in range(8)],
            axis=0,
        ),
        jnp.concatenate([sign * along_z[8 * b:8 * b + 8] for b in range(8)], axis=0),
    )


def holders(width):
    node = lax.broadcasted_iota(jnp.int32, (64, width), 0)
    total = jnp.zeros((64, width), f32)
    for index in (node >> 4, (node >> 2) & 3, node & 3):
        total = total + jnp.where((index == 0) | (index == 3), 1.0, 0.0)
    return total


def gather_tile(source, lane):
    lane = jnp.broadcast_to(lane, (8, 128))
    return jnp.concatenate(
        [jnp.take_along_axis(source[r:r + 8], lane, axis=1) for r in range(0, 48, 8)], axis=0
    )


def halo_faces(lhs, late, keys, hots, lanes, width):
    blocks = 2 * MAIN // CHUNK
    first = width // CHUNK
    late_first = (width + 2 * MAIN) // 128
    out = []
    for f in range(6):
        key = keys[f:f + 1]
        got = mm(lhs, hots[f, :, lanes])
        parts = []
        for at in range(0, CHUNK, 128):
            lane = key[:, at:at + 128] & 127
            tile = key[:, at:at + 128] >> 7
            part = jnp.zeros((48, 128), f32)
            for t, source in enumerate(late):
                part = jnp.where(tile == late_first + t, gather_tile(source, lane), part)
            parts.append(part)
        total = jnp.concatenate(parts, axis=1)
        which = key >> 8
        for a in range(blocks):
            both = got[48 * a:48 * a + 48] + got[48 * (blocks + a):48 * (blocks + a) + 48]
            total = jnp.where(which == first + a, both, total)
        out.append(total)
    return out


def halo_lhs(recv_one, recv_two):
    tiles = [
        recv[48 * t:48 * t + 48] for recv in (recv_one, recv_two) for t in range(MAIN // 128)
    ]
    blocks = [jnp.concatenate(tiles[t:t + 2], axis=1) for t in range(0, len(tiles), 2)]
    high, low = split(jnp.concatenate(blocks, axis=0))
    one, two = recv_one[SEND_MAIN:SEND_ROWS], recv_two[SEND_MAIN:SEND_ROWS]
    tail = jnp.concatenate(
        [
            jnp.concatenate([one[:, 0:TAIL], two[:, 0:TAIL]], axis=1),
            jnp.concatenate([one[:, TAIL:2 * TAIL], two[:, TAIL:2 * TAIL]], axis=1),
        ],
        axis=0,
    )
    mid = [recv[SEND_MAIN - 48:SEND_MAIN] for recv in (recv_one, recv_two)]
    return jnp.concatenate([high, low], axis=0), [*mid, tail]


def local_faces(traces, keys, hots, lanes, own_sign):
    width = traces.shape[1]
    blocks = width // CHUNK
    out = []
    for f in range(6):
        key = keys[f:f + 1]
        other = 48 * (f ^ 1)
        lhs = jnp.concatenate(
            [traces[p + other:p + other + 48, s] for p in (0, 288) for s in chunks(width)], axis=0
        )
        got = mm(lhs, hots[f, :, lanes])
        which = key >> 8
        own = traces[48 * f:48 * f + 48, lanes].astype(f32)
        own = own + traces[288 + 48 * f:288 + 48 * f + 48, lanes].astype(f32)
        total = jnp.where(which < 0, own_sign * own, 0.0)
        for a in range(blocks):
            both = got[48 * a:48 * a + 48] + got[48 * (blocks + a):48 * (blocks + a) + 48]
            total = jnp.where(which == a, both, total)
        out.append(total)
    return out


def put_traces(traces, values, lanes, comp, face, value):
    at = 48 * face + 16 * comp
    values[at:at + 16, lanes] = value
    traces[at:at + 16, lanes], traces[288 + at:288 + at + 16, lanes] = split(value)


def vel_traces(traces, values, lanes, velocity, stage):
    for i in range(3):
        faces = (*xy_faces(velocity[i]), *z_faces(velocity[i], stage.at[i], lanes))
        for f, value in enumerate(faces):
            put_traces(traces, values, lanes, i, f, value)


def str_traces(traces, values, lanes, stress, stage):
    faces = [xy_faces(stress[m]) for m in range(6)]
    for i in range(3):
        for f in range(4):
            put_traces(traces, values, lanes, i, f, faces[symmetric_index[i][f // 2]][f])
        for f, value in enumerate(z_faces(stress[symmetric_index[i][2]], stage.at[i], lanes)):
            put_traces(traces, values, lanes, i, 4 + f, value)


def pack(traces, values, picks, faces, late, send_one, send_two):
    width = traces.shape[1]
    pieces = []
    for s in chunks(2 * MAIN):
        face = faces[:, s]
        got = mm(traces[...], picks[:, s])
        total = jnp.zeros((48, CHUNK), f32)
        for f in range(6):
            both = got[48 * f:48 * f + 48] + got[288 + 48 * f:288 + 48 * f + 48]
            total = jnp.where(face == f, both, total)
        pieces.append(total)
    whole = jnp.concatenate(pieces, axis=1)
    for t in range(MAIN // 128):
        for first, send in ((0, send_one), (MAIN, send_two)):
            send[48 * t:48 * t + 48] = whole[:, first + 128 * t:first + 128 * t + 128]
    tiles = width // 128
    rest = []
    for s in (slice(t, t + 128) for t in range(0, late.shape[1], 128)):
        key = late[:, s]
        lane = key & 127
        which = jnp.broadcast_to(key >> 7, (48, 128))
        total = jnp.zeros((48, 128), f32)
        for f in range(6):
            for a in range(tiles):
                got = gather_tile(values[48 * f:48 * f + 48, 128 * a:128 * a + 128], lane)
                total = jnp.where(which == f * tiles + a, got, total)
        rest.append(total)
    send_one[SEND_MAIN - 48:SEND_MAIN] = rest[0]
    send_two[SEND_MAIN - 48:SEND_MAIN] = rest[1]
    one, two = rest[2][:, 0:TAIL], rest[2][:, TAIL:2 * TAIL]
    send_one[SEND_MAIN:SEND_ROWS] = jnp.concatenate([one[0:24], one[24:48]], axis=1)
    send_two[SEND_MAIN:SEND_ROWS] = jnp.concatenate([two[0:24], two[24:48]], axis=1)


def rate_of(grad, lame, shear):
    trace = lame * (grad[0][0] + grad[1][1] + grad[2][2])
    return [
        trace + 2.0 * shear * grad[0][0],
        trace + 2.0 * shear * grad[1][1],
        trace + 2.0 * shear * grad[2][2],
        shear * (grad[0][1] + grad[1][0]),
        shear * (grad[0][2] + grad[2][0]),
        shear * (grad[1][2] + grad[2][1]),
    ]


def lift_velocity(plus, scratch, lanes):
    grad, jump = [], []
    for i in range(3):
        fields = spread(plus, i, scratch, lanes)
        grad.append(signed(fields))
        jump.append(fields[0] + fields[1] + fields[2])
    return grad, jump


def lift_stress(plus, scratch, lanes):
    out = []
    for i in range(3):
        along_x, along_y, along_z = signed(spread(plus, i, scratch, lanes))
        out.append(along_x + along_y + along_z)
    return out


def start_kernel(
    even, state_hbm, neighbour_hbm, send_list_hbm,
    velocity, stress, keys, picks, faces, late, traces, send_one, send_two,
    state, neighbour, send_list, values, stage, sems,
):
    copies = [
        pltpu.make_async_copy(source, target, sems.at[k])
        for k, (source, target) in enumerate((
            (neighbour_hbm, neighbour), (send_list_hbm, send_list),
            (state_hbm.at[0:3], state.at[0:3]), (state_hbm.at[3:9], state.at[3:9]),
        ))
    ]
    for copy in copies:
        copy.start()
    for copy in copies[0:2]:
        copy.wait()
    width = neighbour.shape[1]
    cap = send_list.shape[1]
    is_even = even[0] == 1
    code = neighbour[...]
    low = code < width + cap
    at = code - width - jnp.where(low, 0, cap)
    second = jnp.where(low == is_even, 0, 1)
    place = jnp.where(
        at < MAIN,
        at + MAIN * second,
        jnp.where(
            at < MAIN + MID,
            at + MAIN + MID * second,
            at + MAIN + MID + TAIL * second,
        ),
    )
    keys[...] = jnp.where(code < width, code, width + place)
    valid = jnp.where(jnp.max(code, axis=0, keepdims=True) >= 0, 1.0, 0.0)
    entries = send_list[...]
    entries = jnp.concatenate(
        [entries, jnp.full((2, MAIN + MID + TAIL - cap), -1, jnp.int32)], axis=1
    )
    one, two = entries[0:1], entries[1:2]
    one, two = jnp.where(is_even, one, two), jnp.where(is_even, two, one)
    late[...] = jnp.concatenate(
        [x[:, c] for c in (slice(MAIN, MAIN + MID), slice(MAIN + MID, None)) for x in (one, two)],
        axis=1,
    )
    main = jnp.concatenate([one[:, 0:MAIN], two[:, 0:MAIN]], axis=1)
    face = jnp.zeros_like(main)
    for f in range(1, 6):
        face = face + jnp.where(main >= f * width, 1, 0)
    faces[...] = face
    slots = main - face * width
    for s in chunks(2 * MAIN):
        picks[:, s] = onehot(slots[:, s], width)
    copies[2].wait()
    for lanes in chunks(width):
        mask = valid[:, lanes]
        now = [state[i, :, lanes] * mask for i in range(3)]
        for i in range(3):
            velocity[i, :, lanes] = now[i]
        vel_traces(traces, values, lanes, now, stage)
    copies[3].wait()
    for lanes in chunks(width):
        for i in range(6):
            stress[i, :, lanes] = state[3 + i, :, lanes] * valid[:, lanes]
    pack(traces, values, picks, faces, late, send_one, send_two)


def vel_local_kernel(
    step, velocity, stress, traces, keys, lame, shear, vel, *rest,
):
    total = None
    *rest, scratch = rest
    scratch[...] = jnp.zeros(scratch.shape, f32)
    if step < 0:
        stress_out, jump_out, hots, lame_scaled, shear_scaled = rest
    elif step == 0:
        hots, forward, stress_out, jump_out, total_out = rest
    else:
        hots, forward, total, stress_out, jump_out, total_out = rest
    width = velocity.shape[2]
    for lanes in chunks(width):
        if step < 0:
            for f in range(6):
                hots[f, :, lanes] = onehot(keys[f:f + 1, lanes] & (CHUNK - 1), CHUNK)
            lame_scaled[:, lanes] = (lift_half * time_step) * lame[:, lanes]
            shear_scaled[:, lanes] = (lift_half * time_step) * shear[:, lanes]
        plus = local_faces(traces, keys[:, lanes], hots, lanes, 1.0)
        grad, jump = lift_velocity(plus, scratch, lanes)
        count = holders(CHUNK)
        whole = []
        for i in range(3):
            now = velocity[i, :, lanes]
            high, low = split(now)
            got = mm(vel[...], jnp.concatenate([high, low, high], axis=0))
            whole.append([got[64 * j:64 * j + 64] + lift_half * grad[i][j] for j in range(3)])
            jump_out[i, :, lanes] = jump[i] - count * now
        rate = rate_of(whole, lame[:, lanes], shear[:, lanes])
        for m in range(6):
            stress_out[m, :, lanes] = stress[m, :, lanes] + time_step * rate[m]
        if step >= 0:
            term = rho_term(forward, step, velocity, lanes)
            total_out[:, lanes] = term if total is None else total[:, lanes] + term


def rho_term(forward, step, velocity, lanes):
    acc = forward[step, 0, :, lanes] * velocity[0, :, lanes]
    acc = acc + forward[step, 1, :, lanes] * velocity[1, :, lanes]
    acc = acc + forward[step, 2, :, lanes] * velocity[2, :, lanes]
    return -time_step * acc


def vel_halo_kernel(
    stress, jump, recv_one, recv_two, keys, hots, picks, faces, late, lame_scaled, shear_scaled,
    stress_out, jump_out, traces, send_one, send_two, values, scratch, stage,
):
    width = stress.shape[2]
    scratch[...] = jnp.zeros(scratch.shape, f32)
    lhs, tail = halo_lhs(recv_one, recv_two)
    for lanes in chunks(width):
        plus = halo_faces(lhs, tail, keys[:, lanes], hots, lanes, width)
        grad, more = lift_velocity(plus, scratch, lanes)
        rate = rate_of(grad, lame_scaled[:, lanes], shear_scaled[:, lanes])
        now = [stress[m, :, lanes] + rate[m] for m in range(6)]
        for m in range(6):
            stress_out[m, :, lanes] = now[m]
        for i in range(3):
            jump_out[i, :, lanes] = jump[i, :, lanes] + more[i]
        str_traces(traces, values, lanes, now, stage)
    pack(traces, values, picks, faces, late, send_one, send_two)


def str_local_kernel(
    step, velocity, stress, jump, traces, keys, hots, density, lame, shear, forward, div, fwd, *rest,
):
    *rest, scratch = rest
    scratch[...] = jnp.zeros(scratch.shape, f32)
    if step == 0:
        total = None
        velocity_out, total_out, scale_out = rest
    else:
        total, velocity_out, total_out = rest
    width = velocity.shape[2]
    for lanes in chunks(width):
        plus = local_faces(traces, keys[:, lanes], hots, lanes, -1.0)
        lifted = lift_stress(plus, scratch, lanes)
        now = [stress[m, :, lanes] for m in range(6)]
        pieces = [split(s) for s in now]
        rho = density[:, lanes]
        impedance = jnp.sqrt(rho * (lame[:, lanes] + 2.0 * shear[:, lanes]))
        scale = time_step / rho
        if step == 0:
            scale_out[:, lanes] = lift_half * scale
        for i in range(3):
            rows = []
            for m in symmetric_index[i]:
                rows += [pieces[m][0], pieces[m][1], pieces[m][0]]
            got = mm(div[...], jnp.concatenate(rows, axis=0))
            velocity_out[i, :, lanes] = velocity[i, :, lanes] + scale * (
                got + lift_half * (lifted[i] + impedance * jump[i, :, lanes])
            )
        grad = []
        for i in range(3):
            high, low = split(forward[step, i, :, lanes])
            got = mm(fwd[...], jnp.concatenate([high, low, high], axis=0))
            grad.append([got[64 * j:64 * j + 64] for j in range(3)])
        diag = (grad[0][0], grad[1][1], grad[2][2])
        lame_term = -time_step * (diag[0] + diag[1] + diag[2]) * (now[0] + now[1] + now[2])
        shear_term = (-2.0 * time_step) * (
            diag[0] * now[0]
            + diag[1] * now[1]
            + diag[2] * now[2]
            + (grad[0][1] + grad[1][0]) * now[3]
            + (grad[0][2] + grad[2][0]) * now[4]
            + (grad[1][2] + grad[2][1]) * now[5]
        )
        for m, term in enumerate((lame_term, shear_term)):
            rows = total_out.shape[2]
            for e in range(total_out.shape[0]):
                share = term[rows * e:rows * e + rows]
                if total is not None:
                    share = total[e, m, :, lanes] + share
                total_out[e, m, :, lanes] = share


def str_halo_kernel(
    velocity, recv_one, recv_two, keys, hots, picks, faces, late, scale,
    velocity_out, traces, send_one, send_two, values, scratch, stage,
):
    halo_velocity(
        velocity, recv_one, recv_two, keys, hots, scale, velocity_out, traces, values, scratch, stage
    )
    pack(traces, values, picks, faces, late, send_one, send_two)


def last_kernel(
    step, velocity, recv_one, recv_two, keys, hots, scale, forward, other, *rest
):
    *total, velocity_out, total_out, scratch, buffer, sems = rest
    total = total[0] if total else None
    rows = total_out.shape[2]
    copies = []

    def finish(lanes):
        copy = pltpu.make_async_copy(
            buffer.at[:, :, lanes], velocity_out.at[:, :, lanes], sems.at[len(copies)]
        )
        copy.start()
        copies.append(copy)
        term = rho_term(forward, step, buffer, lanes)
        if total is not None:
            term = total[:, lanes] + term
        for e in range(total_out.shape[0]):
            total_out[e, 0, :, lanes] = term[rows * e:rows * e + rows]
            for m in range(2):
                total_out[e, m + 1, :, lanes] = other[e, m, :, lanes]

    halo_velocity(
        velocity, recv_one, recv_two, keys, hots, scale, buffer, None, None, scratch, None, finish
    )
    for copy in copies:
        copy.wait()


def event_sum_kernel(parts, out):
    width = parts.shape[3]
    for m in range(3):
        total = parts[0, m]
        for e in range(1, parts.shape[0]):
            total = total + parts[e, m]
        for k in range(total.shape[0]):
            out[m, :, k * width:(k + 1) * width] = total[k:k + 1]


def halo_velocity(
    velocity, recv_one, recv_two, keys, hots, scale, velocity_out, traces, values, scratch, stage,
    finish=None,
):
    width = velocity.shape[2]
    scratch[...] = jnp.zeros(scratch.shape, f32)
    lhs, tail = halo_lhs(recv_one, recv_two)
    for lanes in chunks(width):
        plus = halo_faces(lhs, tail, keys[:, lanes], hots, lanes, width)
        lifted = lift_stress(plus, scratch, lanes)
        now = [velocity[i, :, lanes] + scale[:, lanes] * lifted[i] for i in range(3)]
        for i in range(3):
            velocity_out[i, :, lanes] = now[i]
        if traces is not None:
            vel_traces(traces, values, lanes, now, stage)
        if finish is not None:
            finish(lanes)


def call(name, kernel, args, outs, specs=None, cost=0, scratch=(), out_specs=None):
    whole = pl.BlockSpec(memory_space=pltpu.VMEM)
    specs = specs or {}
    return pl.pallas_call(
        kernel,
        name=name,
        in_specs=[specs.get(k, whole) for k in range(len(args))],
        out_specs=out_specs or [whole] * len(outs),
        out_shape=[jax.ShapeDtypeStruct(s, d) for s, d in outs],
        scratch_shapes=list(scratch),
        compiler_params=pltpu.CompilerParams(vmem_limit_bytes=VMEM_LIMIT),
        cost_estimate=pl.CostEstimate(flops=cost, bytes_accessed=6_000_000, transcendentals=0),
    )(*args)


def swap(sent, axis):
    count = lax.axis_size(axis)
    got = []
    for first, value in enumerate(sent):
        pairs = []
        for low in range(1 - first, count - 1, 2):
            pairs += [(low, low + 1), (low + 1, low)]
        got.append(lax.ppermute(value, axis, pairs))
    return got


def local(
    adjoint_state, forward_velocity, density, lame_lambda, shear_modulus, neighbour, send_list
):
    width = density.shape[1]
    steps = forward_velocity.shape[1]
    table = {k: jnp.asarray(v) for k, v in tables().items()}
    state = adjoint_state[0]
    forward = forward_velocity[0]
    even = (1 - lax.axis_index("dom") % 2).astype(jnp.int32).reshape(1)

    nodal = pltpu.VMEM((3, width // 128, 64, 128), f32)
    values = pltpu.VMEM((288, width), f32)
    field = ((64, width), f32)
    vector = ((3, 64, width), f32)
    tensor = ((6, 64, width), f32)
    count = lax.axis_size("event")
    shares = count if 64 % (8 * count) == 0 else 1
    two = ((shares, 2, 64 // shares, width), f32)
    three = ((shares, 3, 64 // shares, width), f32)
    trace = ((576, width), bf16)
    hot = ((6, CHUNK, width), bf16)
    sends = [((SEND_ROWS, 128), f32)] * 2
    lists = [((6, width), jnp.int32), ((width, 2 * MAIN), bf16),
             ((1, 2 * MAIN), jnp.int32), ((1, 2 * MID + 2 * TAIL), jnp.int32)]

    velocity, stress, keys, picks, faces, late, traces, *sent = call(
        "start", start_kernel,
        (even, *(pltpu.with_memory_space_constraint(x, pltpu.HBM)
                for x in (state, neighbour, send_list))),
        [vector, tensor] + lists + [trace] + sends,
        specs={0: pl.BlockSpec(memory_space=pltpu.SMEM)}
        | {k: pl.BlockSpec(memory_space=pltpu.HBM) for k in range(1, 4)},
        scratch=[
            pltpu.VMEM(state.shape, f32), pltpu.VMEM(neighbour.shape, jnp.int32),
            pltpu.VMEM(send_list.shape, jnp.int32), values, nodal, pltpu.SemaphoreType.DMA((4,)),
        ],
    )
    rho_total = other_total = hots = None
    for n in range(steps):
        recv = swap(sent, "dom")
        args = [velocity, stress, traces, keys, lame_lambda, shear_modulus,
                table["vel"]]
        outs = [tensor, vector]
        if n:
            args += [hots, forward] + ([rho_total] if n > 1 else [])
            outs += [field]
        else:
            outs += [hot, field, field]
        stress, jump, *more = call(
            "vel_local", functools.partial(vel_local_kernel, n - 1), args, outs, cost=4_000_000_000,
            scratch=[nodal],
        )
        if n:
            rho_total, = more
        else:
            hots, lame_scaled, shear_scaled = more
        stress, jump, traces, *sent = call(
            "vel_halo", vel_halo_kernel,
            (stress, jump, *recv, keys, hots, picks, faces, late, lame_scaled, shear_scaled),
            [tensor, vector, trace] + sends, scratch=[values, nodal, nodal],
        )
        recv = swap(sent, "dom")
        args = [velocity, stress, jump, traces, keys, hots, density, lame_lambda, shear_modulus,
                forward, table["div"], table["fwd"]]
        if n:
            args += [other_total]
        velocity, other_total, *more = call(
            "str_local", functools.partial(str_local_kernel, n), args,
            [vector, two] + ([] if n else [field]), cost=4_000_000_000, scratch=[nodal],
        )
        if not n:
            scale, = more
        if n < steps - 1:
            velocity, traces, *sent = call(
                "str_halo", str_halo_kernel,
                (velocity, *recv, keys, hots, picks, faces, late, scale),
                [vector, trace] + sends, scratch=[values, nodal, nodal],
            )
        else:
            velocity, kernel_total = call(
                "last", functools.partial(last_kernel, n),
                (velocity, *recv, keys, hots, scale, forward, other_total)
                + ((rho_total,) if n else ()),
                [vector, three],
                scratch=[
                    nodal, pltpu.VMEM((3, 64, width), f32),
                    pltpu.SemaphoreType.DMA((width // CHUNK,)),
                ],
                out_specs=[
                    pl.BlockSpec(memory_space=pl.ANY), pl.BlockSpec(memory_space=pltpu.VMEM)
                ],
            )

    if shares == count:
        parts = lax.all_to_all(kernel_total, "event", 0, 0, tiled=True)
        kernels, = call(
            "event_sum", event_sum_kernel, (parts,), [((3, 1, 64 // count * width), f32)]
        )
    else:
        flat = kernel_total.reshape(3, -1)
        part = lax.psum_scatter(flat, "event", scatter_dimension=1, tiled=True)
        kernels = part.reshape(3, 1, -1)
    return velocity[None], kernels


def solution(mesh):
    placed = (
        P("event", None, None, "dom"),
        P("event", None, None, None, "dom"),
        P(None, "dom"),
        P(None, "dom"),
        P(None, "dom"),
        P(None, "dom"),
        P(None, "dom"),
    )
    return jax.shard_map(
        local,
        mesh=mesh,
        in_specs=placed,
        out_specs=(P("event", None, None, "dom"), P(None, "dom", "event")),
        check_vma=False,
    )
```

```python
import functools
import math

import jax
import jax.numpy as jnp
import numpy as np
from jax import lax
from jax.experimental import pallas as pl
from jax.experimental.pallas import tpu as pltpu
from jax.sharding import PartitionSpec as P

time_step = 0.02
lift_half = 3.0
symmetric_index = ((0, 3, 4), (3, 1, 5), (4, 5, 2))
f32 = jnp.float32
bf16 = jnp.bfloat16
CHUNK = 256
MAIN = 384
TAIL = 64
HALO = 512
SEND_MAIN = 48 * MAIN // 128
SEND_ROWS = SEND_MAIN + 48 * TAIL // 128
VMEM_LIMIT = 40 * 2**20


def lobatto_diff():
    points = [-1.0, -1.0 / math.sqrt(5.0), 1.0 / math.sqrt(5.0), 1.0]
    weights = [
        1.0 / math.prod([points[t] - points[o] for o in range(4) if o != t]) for t in range(4)
    ]
    offdiag = [
        [
            0.0 if t == s else weights[s] / weights[t] / (points[t] - points[s])
            for s in range(4)
        ]
        for t in range(4)
    ]
    return np.array(
        [[-sum(offdiag[t]) if t == s else offdiag[t][s] for s in range(4)] for t in range(4)],
        dtype=np.float64,
    )


def kron3(first, second, third):
    return np.kron(np.kron(first, second), third)


def deriv_parts(inner):
    matrix = lobatto_diff()
    if inner:
        matrix = matrix + np.diag([lift_half, 0.0, 0.0, -lift_half])
    matrix = matrix.astype(np.float32)
    eye = np.eye(4, dtype=np.float32)
    stack = [kron3(matrix, eye, eye), kron3(eye, matrix, eye), kron3(eye, eye, matrix)]
    high = [np.asarray(m.astype(bf16)) for m in stack]
    low = [np.asarray((m - h.astype(np.float32)).astype(bf16)) for m, h in zip(stack, high)]
    return [h.astype(np.float32) for h in high], [l.astype(np.float32) for l in low]


def tables():
    high, low = deriv_parts(True)
    plain_high, plain_low = deriv_parts(False)

    def rows(upper, lower):
        return np.concatenate(
            [np.concatenate([upper[j], upper[j], lower[j]], axis=1) for j in range(3)], axis=0
        )

    vel = rows(high, low)
    fwd = rows(plain_high, plain_low)
    div = np.concatenate([m for j in range(3) for m in (high[j], high[j], low[j])], axis=1)
    return {
        name: np.asarray(value).astype(bf16) for name, value in dict(vel=vel, fwd=fwd, div=div).items()
    }


def split(value):
    high = value.astype(bf16)
    return high, (value - high.astype(f32)).astype(bf16)


def mm(left, right):
    return jnp.dot(left, right, preferred_element_type=f32)


def onehot(row, depth):
    ids = lax.broadcasted_iota(jnp.int32, (depth, row.shape[-1]), 0)
    return jnp.where(ids == row, 1.0, 0.0).astype(bf16)


def chunks(width):
    return [slice(c, c + CHUNK) for c in range(0, width, CHUNK)]


def top_half(shape):
    return lax.broadcasted_iota(jnp.int32, shape, 0) < 4


def tiles_of(lanes):
    return [(lanes.start // 128 + t, slice(128 * t, 128 * t + 128)) for t in range(CHUNK // 128)]


def z_faces(value, stage, lanes):
    low, high = [], []
    for tile, at in tiles_of(lanes):
        stage[tile] = value[:, at]
        low.append(stage[tile, pl.ds(0, 16, stride=4)])
        high.append(stage[tile, pl.ds(3, 16, stride=4)])
    return jnp.concatenate(low, axis=1), jnp.concatenate(high, axis=1)


def xy_faces(value):
    top = top_half((8, value.shape[1]))

    def rows(at):
        return value[at:at + 8]

    def turned(at):
        return pltpu.roll(value[at:at + 8], 4, 0)

    low_y = [jnp.where(top, rows(at), turned(at + 16)) for at in (0, 32)]
    high_y = [jnp.where(top, turned(at), rows(at + 16)) for at in (8, 40)]
    return [
        value[0:16],
        value[48:64],
        jnp.concatenate(low_y, axis=0),
        jnp.concatenate(high_y, axis=0),
    ]


def spread(faces, comp, scratch, lanes):
    low_x, high_x, low_y, high_y, low_z, high_z = (
        p[16 * comp:16 * comp + 16] for p in faces
    )
    width = low_x.shape[1]
    top = top_half((8, width))
    none = jnp.zeros((8, width), f32)
    along_y = []
    for a in range(4):
        first = low_y[8 * (a // 2):8 * (a // 2) + 8]
        second = high_y[8 * (a // 2):8 * (a // 2) + 8]
        first, second = (
            (pltpu.roll(first, 4, 0), second) if a % 2 else (first, pltpu.roll(second, 4, 0))
        )
        along_y += [jnp.where(top, first, none), jnp.where(top, none, second)]
    along_z = []
    for tile, at in tiles_of(lanes):
        scratch[comp, tile, pl.ds(0, 16, stride=4)] = low_z[:, at]
        scratch[comp, tile, pl.ds(3, 16, stride=4)] = high_z[:, at]
        along_z.append(scratch[comp, tile])
    return (
        jnp.concatenate([low_x, none, none, none, none, high_x], axis=0),
        jnp.concatenate(along_y, axis=0),
        jnp.concatenate(along_z, axis=1),
    )


def signed(fields):
    along_x, along_y, along_z = fields
    width = along_x.shape[1]
    node = lax.broadcasted_iota(jnp.int32, (8, width), 0) & 3
    sign = jnp.where(node == 0, -1.0, 1.0)
    return (
        jnp.concatenate([-along_x[0:16], along_x[16:64]], axis=0),
        jnp.concatenate(
            [along_y[8 * b:8 * b + 8] if b % 2 else -along_y[8 * b:8 * b + 8] for b in range(8)],
            axis=0,
        ),
        jnp.concatenate([sign * along_z[8 * b:8 * b + 8] for b in range(8)], axis=0),
    )


def holders(width):
    node = lax.broadcasted_iota(jnp.int32, (64, width), 0)
    total = jnp.zeros((64, width), f32)
    for index in (node >> 4, (node >> 2) & 3, node & 3):
        total = total + jnp.where((index == 0) | (index == 3), 1.0, 0.0)
    return total


def gather_tile(source, lane):
    lane = jnp.broadcast_to(lane, (8, 128))
    return jnp.concatenate(
        [jnp.take_along_axis(source[r:r + 8], lane, axis=1) for r in range(0, 48, 8)], axis=0
    )


def halo_faces(lhs, keys, hots, lanes, width):
    blocks = HALO // CHUNK
    first = width // CHUNK + blocks
    out = []
    for f in range(6):
        key = keys[f:f + 1]
        got = mm(lhs, hots[f, :, lanes])
        which = key >> 8
        total = jnp.zeros((48, CHUNK), f32)
        for a in range(blocks):
            both = got[48 * a:48 * a + 48] + got[48 * (blocks + a):48 * (blocks + a) + 48]
            total = jnp.where(which == first + a, both, total)
        out.append(total)
    return out


def halo_lhs(recv):
    late = recv[SEND_MAIN:SEND_ROWS]
    late = jnp.concatenate([late[:, 0:TAIL], late[:, TAIL:2 * TAIL]], axis=0)
    late = jnp.concatenate([late, jnp.zeros((48, 128 - TAIL), f32)], axis=1)
    tiles = [recv[48 * t:48 * t + 48] for t in range(MAIN // 128)] + [late]
    blocks = [jnp.concatenate(tiles[t:t + 2], axis=1) for t in range(0, len(tiles), 2)]
    high, low = split(jnp.concatenate(blocks, axis=0))
    return jnp.concatenate([high, low], axis=0)


def local_faces(traces, near, keys, hots, lanes, own_sign):
    width = traces.shape[1]
    blocks = width // CHUNK
    out = []
    for f in range(6):
        key = keys[f:f + 1]
        other = 48 * (f ^ 1)
        lhs = jnp.concatenate(
            [traces[p + other:p + other + 48, s] for p in (0, 288) for s in chunks(width)]
            + [near],
            axis=0,
        )
        got = mm(lhs, hots[f, :, lanes])
        which = key >> 8
        own = traces[48 * f:48 * f + 48, lanes].astype(f32)
        own = own + traces[288 + 48 * f:288 + 48 * f + 48, lanes].astype(f32)
        total = jnp.where(which < 0, own_sign * own, 0.0)
        for a in range(blocks):
            both = got[48 * a:48 * a + 48] + got[48 * (blocks + a):48 * (blocks + a) + 48]
            total = jnp.where(which == a, both, total)
        for a in range(HALO // CHUNK):
            at = 96 * blocks + 48 * a
            low = at + 48 * (HALO // CHUNK)
            both = got[at:at + 48] + got[low:low + 48]
            total = jnp.where(which == blocks + a, both, total)
        out.append(total)
    return out


def put_traces(traces, values, lanes, comp, face, value):
    at = 48 * face + 16 * comp
    values[at:at + 16, lanes] = value
    traces[at:at + 16, lanes], traces[288 + at:288 + at + 16, lanes] = split(value)


def vel_traces(traces, values, lanes, velocity, stage):
    for i in range(3):
        faces = (*xy_faces(velocity[i]), *z_faces(velocity[i], stage.at[i], lanes))
        for f, value in enumerate(faces):
            put_traces(traces, values, lanes, i, f, value)


def str_traces(traces, values, lanes, stress, stage):
    faces = [xy_faces(stress[m]) for m in range(6)]
    for i in range(3):
        for f in range(4):
            put_traces(traces, values, lanes, i, f, faces[symmetric_index[i][f // 2]][f])
        for f, value in enumerate(z_faces(stress[symmetric_index[i][2]], stage.at[i], lanes)):
            put_traces(traces, values, lanes, i, 4 + f, value)


def pack(traces, values, picks, faces, late, send_one, send_two):
    width = traces.shape[1]
    pieces = []
    for s in chunks(2 * MAIN):
        face = faces[:, s]
        got = mm(traces[...], picks[:, s])
        total = jnp.zeros((48, CHUNK), f32)
        for f in range(6):
            both = got[48 * f:48 * f + 48] + got[288 + 48 * f:288 + 48 * f + 48]
            total = jnp.where(face == f, both, total)
        pieces.append(total)
    whole = jnp.concatenate(pieces, axis=1)
    for t in range(MAIN // 128):
        for first, send in ((0, send_one), (MAIN, send_two)):
            send[48 * t:48 * t + 48] = whole[:, first + 128 * t:first + 128 * t + 128]
    key = late[...]
    lane = key & 127
    which = jnp.broadcast_to(key >> 7, (48, 128))
    total = jnp.zeros((48, 128), f32)
    for f in range(6):
        for a in range(width // 128):
            got = gather_tile(values[48 * f:48 * f + 48, 128 * a:128 * a + 128], lane)
            total = jnp.where(which == f * (width // 128) + a, got, total)
    one, two = total[:, 0:TAIL], total[:, TAIL:2 * TAIL]
    send_one[SEND_MAIN:SEND_ROWS] = jnp.concatenate([one[0:24], one[24:48]], axis=1)
    send_two[SEND_MAIN:SEND_ROWS] = jnp.concatenate([two[0:24], two[24:48]], axis=1)


def rate_of(grad, lame, shear):
    trace = lame * (grad[0][0] + grad[1][1] + grad[2][2])
    return [
        trace + 2.0 * shear * grad[0][0],
        trace + 2.0 * shear * grad[1][1],
        trace + 2.0 * shear * grad[2][2],
        shear * (grad[0][1] + grad[1][0]),
        shear * (grad[0][2] + grad[2][0]),
        shear * (grad[1][2] + grad[2][1]),
    ]


def lift_velocity(plus, scratch, lanes):
    grad, jump = [], []
    for i in range(3):
        fields = spread(plus, i, scratch, lanes)
        grad.append(signed(fields))
        jump.append(fields[0] + fields[1] + fields[2])
    return grad, jump


def lift_stress(plus, scratch, lanes):
    out = []
    for i in range(3):
        along_x, along_y, along_z = signed(spread(plus, i, scratch, lanes))
        out.append(along_x + along_y + along_z)
    return out


def start_kernel(
    down, state_hbm, neighbour_hbm, send_list_hbm,
    velocity, stress, keys, picks, faces, late, traces, send_one, send_two,
    state, neighbour, send_list, values, stage, sems,
):
    copies = [
        pltpu.make_async_copy(source, target, sems.at[k])
        for k, (source, target) in enumerate((
            (neighbour_hbm, neighbour), (send_list_hbm, send_list),
            (state_hbm.at[0:3], state.at[0:3]), (state_hbm.at[3:9], state.at[3:9]),
        ))
    ]
    for copy in copies:
        copy.start()
    for copy in copies[0:2]:
        copy.wait()
    width = neighbour.shape[1]
    cap = send_list.shape[1]
    is_down = down[0] == 1
    code = neighbour[...]
    low = code < width + cap
    at = code - width - jnp.where(low, 0, cap)
    second = jnp.where(low == is_down, 0, 1)
    place = at + HALO * second
    keys[...] = jnp.where(code < width, code, width + place)
    valid = jnp.where(jnp.max(code, axis=0, keepdims=True) >= 0, 1.0, 0.0)
    entries = send_list[...]
    entries = jnp.concatenate(
        [entries, jnp.full((2, MAIN + TAIL - cap), -1, jnp.int32)], axis=1
    )
    one, two = entries[0:1], entries[1:2]
    one, two = jnp.where(is_down, one, two), jnp.where(is_down, two, one)
    late[...] = jnp.concatenate([one[:, MAIN:], two[:, MAIN:]], axis=1)
    main = jnp.concatenate([one[:, 0:MAIN], two[:, 0:MAIN]], axis=1)
    face = jnp.zeros_like(main)
    for f in range(1, 6):
        face = face + jnp.where(main >= f * width, 1, 0)
    faces[...] = face
    slots = main - face * width
    for s in chunks(2 * MAIN):
        picks[:, s] = onehot(slots[:, s], width)
    copies[2].wait()
    for lanes in chunks(width):
        mask = valid[:, lanes]
        now = [state[i, :, lanes] * mask for i in range(3)]
        for i in range(3):
            velocity[i, :, lanes] = now[i]
        vel_traces(traces, values, lanes, now, stage)
    pack(traces, values, picks, faces, late, send_one, send_two)
    copies[3].wait()
    for lanes in chunks(width):
        for i in range(6):
            stress[i, :, lanes] = state[3 + i, :, lanes] * valid[:, lanes]


def vel_local_kernel(
    step, velocity, stress, traces, recv, keys, lame, shear, vel, *rest,
):
    total = None
    *rest, scratch = rest
    scratch[...] = jnp.zeros(scratch.shape, f32)
    near = halo_lhs(recv)
    if step < 0:
        stress_out, jump_out, hots, lame_scaled, shear_scaled = rest
    elif step == 0:
        hots, forward, stress_out, jump_out, total_out = rest
    else:
        hots, forward, total, stress_out, jump_out, total_out = rest
    width = velocity.shape[2]
    for lanes in chunks(width):
        if step < 0:
            for f in range(6):
                hots[f, :, lanes] = onehot(keys[f:f + 1, lanes] & (CHUNK - 1), CHUNK)
            lame_scaled[:, lanes] = (lift_half * time_step) * lame[:, lanes]
            shear_scaled[:, lanes] = (lift_half * time_step) * shear[:, lanes]
        plus = local_faces(traces, near, keys[:, lanes], hots, lanes, 1.0)
        grad, jump = lift_velocity(plus, scratch, lanes)
        count = holders(CHUNK)
        whole = []
        for i in range(3):
            now = velocity[i, :, lanes]
            high, low = split(now)
            got = mm(vel[...], jnp.concatenate([high, low, high], axis=0))
            whole.append([got[64 * j:64 * j + 64] + lift_half * grad[i][j] for j in range(3)])
            jump_out[i, :, lanes] = jump[i] - count * now
        rate = rate_of(whole, lame[:, lanes], shear[:, lanes])
        for m in range(6):
            stress_out[m, :, lanes] = stress[m, :, lanes] + time_step * rate[m]
        if step >= 0:
            term = rho_term(forward, step, velocity, lanes)
            total_out[:, lanes] = term if total is None else total[:, lanes] + term


def rho_term(forward, step, velocity, lanes):
    acc = forward[step, 0, :, lanes] * velocity[0, :, lanes]
    acc = acc + forward[step, 1, :, lanes] * velocity[1, :, lanes]
    acc = acc + forward[step, 2, :, lanes] * velocity[2, :, lanes]
    return -time_step * acc


def vel_halo_kernel(
    stress, jump, recv, keys, hots, picks, faces, late, lame_scaled, shear_scaled,
    stress_out, jump_out, traces, send_one, send_two, values, scratch, stage,
):
    width = stress.shape[2]
    scratch[...] = jnp.zeros(scratch.shape, f32)
    lhs = halo_lhs(recv)
    for lanes in chunks(width):
        plus = halo_faces(lhs, keys[:, lanes], hots, lanes, width)
        grad, more = lift_velocity(plus, scratch, lanes)
        rate = rate_of(grad, lame_scaled[:, lanes], shear_scaled[:, lanes])
        now = [stress[m, :, lanes] + rate[m] for m in range(6)]
        for m in range(6):
            stress_out[m, :, lanes] = now[m]
        for i in range(3):
            jump_out[i, :, lanes] = jump[i, :, lanes] + more[i]
        str_traces(traces, values, lanes, now, stage)
    pack(traces, values, picks, faces, late, send_one, send_two)


def str_local_kernel(
    step, velocity, stress, jump, traces, recv, keys, hots, density, lame, shear, forward, div, fwd, *rest,
):
    *rest, scratch = rest
    scratch[...] = jnp.zeros(scratch.shape, f32)
    near = halo_lhs(recv)
    if step == 0:
        total = None
        velocity_out, total_out, scale_out = rest
    else:
        total, velocity_out, total_out = rest
    width = velocity.shape[2]
    for lanes in chunks(width):
        plus = local_faces(traces, near, keys[:, lanes], hots, lanes, -1.0)
        lifted = lift_stress(plus, scratch, lanes)
        now = [stress[m, :, lanes] for m in range(6)]
        pieces = [split(s) for s in now]
        rho = density[:, lanes]
        impedance = jnp.sqrt(rho * (lame[:, lanes] + 2.0 * shear[:, lanes]))
        scale = time_step / rho
        if step == 0:
            scale_out[:, lanes] = lift_half * scale
        for i in range(3):
            rows = []
            for m in symmetric_index[i]:
                rows += [pieces[m][0], pieces[m][1], pieces[m][0]]
            got = mm(div[...], jnp.concatenate(rows, axis=0))
            velocity_out[i, :, lanes] = velocity[i, :, lanes] + scale * (
                got + lift_half * (lifted[i] + impedance * jump[i, :, lanes])
            )
        grad = []
        for i in range(3):
            high, low = split(forward[step, i, :, lanes])
            got = mm(fwd[...], jnp.concatenate([high, low, high], axis=0))
            grad.append([got[64 * j:64 * j + 64] for j in range(3)])
        diag = (grad[0][0], grad[1][1], grad[2][2])
        lame_term = -time_step * (diag[0] + diag[1] + diag[2]) * (now[0] + now[1] + now[2])
        shear_term = (-2.0 * time_step) * (
            diag[0] * now[0]
            + diag[1] * now[1]
            + diag[2] * now[2]
            + (grad[0][1] + grad[1][0]) * now[3]
            + (grad[0][2] + grad[2][0]) * now[4]
            + (grad[1][2] + grad[2][1]) * now[5]
        )
        for m, term in enumerate((lame_term, shear_term)):
            rows = total_out.shape[2]
            for e in range(total_out.shape[0]):
                share = term[rows * e:rows * e + rows]
                if total is not None:
                    share = total[e, m, :, lanes] + share
                total_out[e, m, :, lanes] = share


def str_halo_kernel(
    velocity, recv, keys, hots, picks, faces, late, scale,
    velocity_out, traces, send_one, send_two, values, scratch, stage,
):
    halo_velocity(
        velocity, recv, keys, hots, scale, velocity_out, traces, values, scratch, stage
    )
    pack(traces, values, picks, faces, late, send_one, send_two)


def last_kernel(
    step, velocity, recv, keys, hots, scale, forward, other, *rest
):
    *total, velocity_out, total_out, scratch, buffer, sems = rest
    total = total[0] if total else None
    rows = total_out.shape[2]
    copies = []

    def finish(lanes):
        copy = pltpu.make_async_copy(
            buffer.at[:, :, lanes], velocity_out.at[:, :, lanes], sems.at[len(copies)]
        )
        copy.start()
        copies.append(copy)
        term = rho_term(forward, step, buffer, lanes)
        if total is not None:
            term = total[:, lanes] + term
        for e in range(total_out.shape[0]):
            total_out[e, 0, :, lanes] = term[rows * e:rows * e + rows]
            for m in range(2):
                total_out[e, m + 1, :, lanes] = other[e, m, :, lanes]

    halo_velocity(
        velocity, recv, keys, hots, scale, buffer, None, None, scratch, None, finish
    )
    for copy in copies:
        copy.wait()


def event_sum_kernel(parts, out):
    width = parts.shape[3]
    for m in range(3):
        total = parts[0, m]
        for e in range(1, parts.shape[0]):
            total = total + parts[e, m]
        for k in range(total.shape[0]):
            out[m, :, k * width:(k + 1) * width] = total[k:k + 1]


def halo_velocity(
    velocity, recv, keys, hots, scale, velocity_out, traces, values, scratch, stage,
    finish=None,
):
    width = velocity.shape[2]
    scratch[...] = jnp.zeros(scratch.shape, f32)
    lhs = halo_lhs(recv)
    for lanes in chunks(width):
        plus = halo_faces(lhs, keys[:, lanes], hots, lanes, width)
        lifted = lift_stress(plus, scratch, lanes)
        now = [velocity[i, :, lanes] + scale[:, lanes] * lifted[i] for i in range(3)]
        for i in range(3):
            velocity_out[i, :, lanes] = now[i]
        if traces is not None:
            vel_traces(traces, values, lanes, now, stage)
        if finish is not None:
            finish(lanes)


def call(name, kernel, args, outs, specs=None, cost=0, scratch=(), out_specs=None):
    whole = pl.BlockSpec(memory_space=pltpu.VMEM)
    specs = specs or {}
    return pl.pallas_call(
        kernel,
        name=name,
        in_specs=[specs.get(k, whole) for k in range(len(args))],
        out_specs=out_specs or [whole] * len(outs),
        out_shape=[jax.ShapeDtypeStruct(s, d) for s, d in outs],
        scratch_shapes=list(scratch),
        compiler_params=pltpu.CompilerParams(vmem_limit_bytes=VMEM_LIMIT),
        cost_estimate=pl.CostEstimate(flops=cost, bytes_accessed=6_000_000, transcendentals=0),
    )(*args)


def swap(sent, axis):
    count = lax.axis_size(axis)
    got = []
    for first, value in enumerate(sent):
        pairs = []
        for low in range(first, count - 1, 2):
            pairs += [(low, low + 1), (low + 1, low)]
        got.append(lax.ppermute(value, axis, pairs))
    return got


def local(
    adjoint_state, forward_velocity, density, lame_lambda, shear_modulus, neighbour, send_list
):
    width = density.shape[1]
    steps = forward_velocity.shape[1]
    table = {k: jnp.asarray(v) for k, v in tables().items()}
    state = adjoint_state[0]
    forward = forward_velocity[0]
    down = (lax.axis_index("dom") % 2).astype(jnp.int32).reshape(1)

    nodal = pltpu.VMEM((3, width // 128, 64, 128), f32)
    values = pltpu.VMEM((288, width), f32)
    field = ((64, width), f32)
    vector = ((3, 64, width), f32)
    tensor = ((6, 64, width), f32)
    count = lax.axis_size("event")
    shares = count if 64 % (8 * count) == 0 else 1
    two = ((shares, 2, 64 // shares, width), f32)
    three = ((shares, 3, 64 // shares, width), f32)
    trace = ((576, width), bf16)
    hot = ((6, CHUNK, width), bf16)
    sends = [((SEND_ROWS, 128), f32)] * 2
    lists = [((6, width), jnp.int32), ((width, 2 * MAIN), bf16),
             ((1, 2 * MAIN), jnp.int32), ((1, 2 * TAIL), jnp.int32)]

    velocity, stress, keys, picks, faces, late, traces, *sent = call(
        "start", start_kernel,
        (down, *(pltpu.with_memory_space_constraint(x, pltpu.HBM)
                for x in (state, neighbour, send_list))),
        [vector, tensor] + lists + [trace] + sends,
        specs={0: pl.BlockSpec(memory_space=pltpu.SMEM)}
        | {k: pl.BlockSpec(memory_space=pltpu.HBM) for k in range(1, 4)},
        scratch=[
            pltpu.VMEM(state.shape, f32), pltpu.VMEM(neighbour.shape, jnp.int32),
            pltpu.VMEM(send_list.shape, jnp.int32), values, nodal, pltpu.SemaphoreType.DMA((4,)),
        ],
    )
    rho_total = other_total = hots = None
    for n in range(steps):
        first, recv = swap(sent, "dom")
        args = [velocity, stress, traces, first, keys, lame_lambda, shear_modulus,
                table["vel"]]
        outs = [tensor, vector]
        if n:
            args += [hots, forward] + ([rho_total] if n > 1 else [])
            outs += [field]
        else:
            outs += [hot, field, field]
        stress, jump, *more = call(
            "vel_local", functools.partial(vel_local_kernel, n - 1), args, outs, cost=4_000_000_000,
            scratch=[nodal],
        )
        if n:
            rho_total, = more
        else:
            hots, lame_scaled, shear_scaled = more
        stress, jump, traces, *sent = call(
            "vel_halo", vel_halo_kernel,
            (stress, jump, recv, keys, hots, picks, faces, late, lame_scaled, shear_scaled),
            [tensor, vector, trace] + sends, scratch=[values, nodal, nodal],
        )
        first, recv = swap(sent, "dom")
        args = [velocity, stress, jump, traces, first, keys, hots, density, lame_lambda, shear_modulus,
                forward, table["div"], table["fwd"]]
        if n:
            args += [other_total]
        velocity, other_total, *more = call(
            "str_local", functools.partial(str_local_kernel, n), args,
            [vector, two] + ([] if n else [field]), cost=4_000_000_000, scratch=[nodal],
        )
        if not n:
            scale, = more
        if n < steps - 1:
            velocity, traces, *sent = call(
                "str_halo", str_halo_kernel,
                (velocity, recv, keys, hots, picks, faces, late, scale),
                [vector, trace] + sends, scratch=[values, nodal, nodal],
            )
        else:
            velocity, kernel_total = call(
                "last", functools.partial(last_kernel, n),
                (velocity, recv, keys, hots, scale, forward, other_total)
                + ((rho_total,) if n else ()),
                [vector, three],
                scratch=[
                    nodal, pltpu.VMEM((3, 64, width), f32),
                    pltpu.SemaphoreType.DMA((width // CHUNK,)),
                ],
                out_specs=[
                    pl.BlockSpec(memory_space=pl.ANY), pl.BlockSpec(memory_space=pltpu.VMEM)
                ],
            )

    if shares == count:
        parts = lax.all_to_all(kernel_total, "event", 0, 0, tiled=True)
        kernels, = call(
            "event_sum", event_sum_kernel, (parts,), [((3, 1, 64 // count * width), f32)]
        )
    else:
        flat = kernel_total.reshape(3, -1)
        part = lax.psum_scatter(flat, "event", scatter_dimension=1, tiled=True)
        kernels = part.reshape(3, 1, -1)
    return velocity[None], kernels


def solution(mesh):
    placed = (
        P("event", None, None, "dom"),
        P("event", None, None, None, "dom"),
        P(None, "dom"),
        P(None, "dom"),
        P(None, "dom"),
        P(None, "dom"),
        P(None, "dom"),
    )
    return jax.shard_map(
        local,
        mesh=mesh,
        in_specs=placed,
        out_specs=(P("event", None, None, "dom"), P(None, "dom", "event")),
        check_vma=False,
    )
```

```python
import functools
import math

import jax
import jax.numpy as jnp
import numpy as np
from jax import lax
from jax.experimental import pallas as pl
from jax.experimental.pallas import tpu as pltpu
from jax.sharding import PartitionSpec as P

time_step = 0.02
lift_half = 3.0
symmetric_index = ((0, 3, 4), (3, 1, 5), (4, 5, 2))
f32 = jnp.float32
bf16 = jnp.bfloat16
CHUNK = 256
MAIN = 384
TAIL = 64
HALO = 512
SEND_MAIN = 48 * MAIN // 128
SEND_ROWS = SEND_MAIN + 48 * TAIL // 128
VMEM_LIMIT = 40 * 2**20


def lobatto_diff():
    points = [-1.0, -1.0 / math.sqrt(5.0), 1.0 / math.sqrt(5.0), 1.0]
    weights = [
        1.0 / math.prod([points[t] - points[o] for o in range(4) if o != t]) for t in range(4)
    ]
    offdiag = [
        [
            0.0 if t == s else weights[s] / weights[t] / (points[t] - points[s])
            for s in range(4)
        ]
        for t in range(4)
    ]
    return np.array(
        [[-sum(offdiag[t]) if t == s else offdiag[t][s] for s in range(4)] for t in range(4)],
        dtype=np.float64,
    )


def kron3(first, second, third):
    return np.kron(np.kron(first, second), third)


def deriv_parts(inner):
    matrix = lobatto_diff()
    if inner:
        matrix = matrix + np.diag([lift_half, 0.0, 0.0, -lift_half])
    matrix = matrix.astype(np.float32)
    eye = np.eye(4, dtype=np.float32)
    stack = [kron3(matrix, eye, eye), kron3(eye, matrix, eye), kron3(eye, eye, matrix)]
    high = [np.asarray(m.astype(bf16)) for m in stack]
    low = [np.asarray((m - h.astype(np.float32)).astype(bf16)) for m, h in zip(stack, high)]
    return [h.astype(np.float32) for h in high], [l.astype(np.float32) for l in low]


def tables():
    high, low = deriv_parts(True)
    plain_high, plain_low = deriv_parts(False)

    def rows(upper, lower):
        return np.concatenate(
            [np.concatenate([upper[j], upper[j], lower[j]], axis=1) for j in range(3)], axis=0
        )

    vel = rows(high, low)
    fwd = rows(plain_high, plain_low)
    div = np.concatenate([m for j in range(3) for m in (high[j], high[j], low[j])], axis=1)
    return {
        name: np.asarray(value).astype(bf16) for name, value in dict(vel=vel, fwd=fwd, div=div).items()
    }


def split(value):
    high = value.astype(bf16)
    return high, (value - high.astype(f32)).astype(bf16)


def mm(left, right):
    return jnp.dot(left, right, preferred_element_type=f32)


def onehot(row, depth):
    ids = lax.broadcasted_iota(jnp.int32, (depth, row.shape[-1]), 0)
    return jnp.where(ids == row, 1.0, 0.0).astype(bf16)


def chunks(width):
    return [slice(c, c + CHUNK) for c in range(0, width, CHUNK)]


def top_half(shape):
    return lax.broadcasted_iota(jnp.int32, shape, 0) < 4


def tiles_of(lanes):
    return [(lanes.start // 128 + t, slice(128 * t, 128 * t + 128)) for t in range(CHUNK // 128)]


def z_faces(value, stage, lanes):
    low, high = [], []
    for tile, at in tiles_of(lanes):
        stage[tile] = value[:, at]
        low.append(stage[tile, pl.ds(0, 16, stride=4)])
        high.append(stage[tile, pl.ds(3, 16, stride=4)])
    return jnp.concatenate(low, axis=1), jnp.concatenate(high, axis=1)


def xy_faces(value):
    top = top_half((8, value.shape[1]))

    def rows(at):
        return value[at:at + 8]

    def turned(at):
        return pltpu.roll(value[at:at + 8], 4, 0)

    low_y = [jnp.where(top, rows(at), turned(at + 16)) for at in (0, 32)]
    high_y = [jnp.where(top, turned(at), rows(at + 16)) for at in (8, 40)]
    return [
        value[0:16],
        value[48:64],
        jnp.concatenate(low_y, axis=0),
        jnp.concatenate(high_y, axis=0),
    ]


def clear_inner(scratch):
    for comp in range(scratch.shape[0]):
        for tile in range(scratch.shape[1]):
            for first in (1, 2):
                scratch[comp, tile, pl.ds(first, 16, stride=4)] = jnp.zeros((16, 128), f32)


def spread(faces, comp, scratch, lanes):
    low_x, high_x, low_y, high_y, low_z, high_z = (
        p[16 * comp:16 * comp + 16] for p in faces
    )
    width = low_x.shape[1]
    top = top_half((8, width))
    none = jnp.zeros((8, width), f32)
    along_y = []
    for a in range(4):
        first = low_y[8 * (a // 2):8 * (a // 2) + 8]
        second = high_y[8 * (a // 2):8 * (a // 2) + 8]
        first, second = (
            (pltpu.roll(first, 4, 0), second) if a % 2 else (first, pltpu.roll(second, 4, 0))
        )
        along_y += [jnp.where(top, first, none), jnp.where(top, none, second)]
    along_z = []
    for tile, at in tiles_of(lanes):
        scratch[comp, tile, pl.ds(0, 16, stride=4)] = low_z[:, at]
        scratch[comp, tile, pl.ds(3, 16, stride=4)] = high_z[:, at]
        along_z.append(scratch[comp, tile])
    return (
        jnp.concatenate([low_x, none, none, none, none, high_x], axis=0),
        jnp.concatenate(along_y, axis=0),
        jnp.concatenate(along_z, axis=1),
    )


def signed(fields):
    along_x, along_y, along_z = fields
    width = along_x.shape[1]
    node = lax.broadcasted_iota(jnp.int32, (8, width), 0) & 3
    sign = jnp.where(node == 0, -1.0, 1.0)
    return (
        jnp.concatenate([-along_x[0:16], along_x[16:64]], axis=0),
        jnp.concatenate(
            [along_y[8 * b:8 * b + 8] if b % 2 else -along_y[8 * b:8 * b + 8] for b in range(8)],
            axis=0,
        ),
        jnp.concatenate([sign * along_z[8 * b:8 * b + 8] for b in range(8)], axis=0),
    )


def holders(width):
    node = lax.broadcasted_iota(jnp.int32, (64, width), 0)
    total = jnp.zeros((64, width), f32)
    for index in (node >> 4, (node >> 2) & 3, node & 3):
        total = total + jnp.where((index == 0) | (index == 3), 1.0, 0.0)
    return total


def gather_tile(source, lane):
    lane = jnp.broadcast_to(lane, (8, 128))
    return jnp.concatenate(
        [jnp.take_along_axis(source[r:r + 8], lane, axis=1) for r in range(0, 48, 8)], axis=0
    )


def halo_faces(lhs, keys, hots, lanes, width):
    blocks = HALO // CHUNK
    first = width // CHUNK + blocks
    out = []
    for f in range(6):
        key = keys[f:f + 1]
        got = mm(lhs, hots[f, :, lanes])
        which = key >> 8
        total = jnp.zeros((48, CHUNK), f32)
        for a in range(blocks):
            both = got[48 * a:48 * a + 48] + got[48 * (blocks + a):48 * (blocks + a) + 48]
            total = jnp.where(which == first + a, both, total)
        out.append(total)
    return out


def halo_lhs(recv):
    late = recv[SEND_MAIN:SEND_ROWS]
    late = jnp.concatenate([late[:, 0:TAIL], late[:, TAIL:2 * TAIL]], axis=0)
    late = jnp.concatenate([late, jnp.zeros((48, 128 - TAIL), f32)], axis=1)
    tiles = [recv[48 * t:48 * t + 48] for t in range(MAIN // 128)] + [late]
    blocks = [jnp.concatenate(tiles[t:t + 2], axis=1) for t in range(0, len(tiles), 2)]
    high, low = split(jnp.concatenate(blocks, axis=0))
    return jnp.concatenate([high, low], axis=0)


def local_faces(traces, near, keys, hots, lanes, own_sign):
    width = traces.shape[1]
    blocks = width // CHUNK
    out = []
    for f in range(6):
        key = keys[f:f + 1]
        other = 48 * (f ^ 1)
        lhs = jnp.concatenate(
            [traces[p + other:p + other + 48, s] for p in (0, 288) for s in chunks(width)]
            + [near],
            axis=0,
        )
        got = mm(lhs, hots[f, :, lanes])
        which = key >> 8
        own = traces[48 * f:48 * f + 48, lanes].astype(f32)
        own = own + traces[288 + 48 * f:288 + 48 * f + 48, lanes].astype(f32)
        total = jnp.where(which < 0, own_sign * own, 0.0)
        for a in range(blocks):
            both = got[48 * a:48 * a + 48] + got[48 * (blocks + a):48 * (blocks + a) + 48]
            total = jnp.where(which == a, both, total)
        for a in range(HALO // CHUNK):
            at = 96 * blocks + 48 * a
            low = at + 48 * (HALO // CHUNK)
            both = got[at:at + 48] + got[low:low + 48]
            total = jnp.where(which == blocks + a, both, total)
        out.append(total)
    return out


def put_traces(traces, values, lanes, comp, face, value):
    at = 48 * face + 16 * comp
    values[at:at + 16, lanes] = value
    traces[at:at + 16, lanes], traces[288 + at:288 + at + 16, lanes] = split(value)


def vel_traces(traces, values, lanes, velocity, stage):
    for i in range(3):
        faces = (*xy_faces(velocity[i]), *z_faces(velocity[i], stage.at[i], lanes))
        for f, value in enumerate(faces):
            put_traces(traces, values, lanes, i, f, value)


def str_traces(traces, values, lanes, stress, stage):
    faces = [xy_faces(stress[m]) for m in range(6)]
    for i in range(3):
        for f in range(4):
            put_traces(traces, values, lanes, i, f, faces[symmetric_index[i][f // 2]][f])
        for f, value in enumerate(z_faces(stress[symmetric_index[i][2]], stage.at[i], lanes)):
            put_traces(traces, values, lanes, i, 4 + f, value)


def pack(traces, values, picks, faces, late, send_one, send_two):
    width = traces.shape[1]
    pieces = []
    for s in chunks(2 * MAIN):
        face = faces[:, s]
        got = mm(traces[...], picks[:, s])
        total = jnp.zeros((48, CHUNK), f32)
        for f in range(6):
            both = got[48 * f:48 * f + 48] + got[288 + 48 * f:288 + 48 * f + 48]
            total = jnp.where(face == f, both, total)
        pieces.append(total)
    whole = jnp.concatenate(pieces, axis=1)
    for t in range(MAIN // 128):
        for first, send in ((0, send_one), (MAIN, send_two)):
            send[48 * t:48 * t + 48] = whole[:, first + 128 * t:first + 128 * t + 128]
    key = late[...]
    lane = key & 127
    which = jnp.broadcast_to(key >> 7, (48, 128))
    total = jnp.zeros((48, 128), f32)
    for f in range(6):
        for a in range(width // 128):
            got = gather_tile(values[48 * f:48 * f + 48, 128 * a:128 * a + 128], lane)
            total = jnp.where(which == f * (width // 128) + a, got, total)
    one, two = total[:, 0:TAIL], total[:, TAIL:2 * TAIL]
    send_one[SEND_MAIN:SEND_ROWS] = jnp.concatenate([one[0:24], one[24:48]], axis=1)
    send_two[SEND_MAIN:SEND_ROWS] = jnp.concatenate([two[0:24], two[24:48]], axis=1)


def rate_of(grad, lame, shear):
    trace = lame * (grad[0][0] + grad[1][1] + grad[2][2])
    return [
        trace + 2.0 * shear * grad[0][0],
        trace + 2.0 * shear * grad[1][1],
        trace + 2.0 * shear * grad[2][2],
        shear * (grad[0][1] + grad[1][0]),
        shear * (grad[0][2] + grad[2][0]),
        shear * (grad[1][2] + grad[2][1]),
    ]


def lift_velocity(plus, scratch, lanes):
    grad, jump = [], []
    for i in range(3):
        fields = spread(plus, i, scratch, lanes)
        grad.append(signed(fields))
        jump.append(fields[0] + fields[1] + fields[2])
    return grad, jump


def lift_stress(plus, scratch, lanes):
    out = []
    for i in range(3):
        along_x, along_y, along_z = signed(spread(plus, i, scratch, lanes))
        out.append(along_x + along_y + along_z)
    return out


def start_kernel(
    down, state_hbm, neighbour_hbm, send_list_hbm,
    velocity, stress, keys, picks, faces, late, traces, send_one, send_two,
    state, neighbour, send_list, values, stage, sems,
):
    copies = [
        pltpu.make_async_copy(source, target, sems.at[k])
        for k, (source, target) in enumerate((
            (neighbour_hbm, neighbour), (send_list_hbm, send_list),
            (state_hbm.at[0:3], state.at[0:3]), (state_hbm.at[3:9], state.at[3:9]),
        ))
    ]
    for copy in copies:
        copy.start()
    for copy in copies[0:2]:
        copy.wait()
    width = neighbour.shape[1]
    cap = send_list.shape[1]
    is_down = down[0] == 1
    code = neighbour[...]
    low = code < width + cap
    at = code - width - jnp.where(low, 0, cap)
    second = jnp.where(low == is_down, 0, 1)
    place = at + HALO * second
    keys[...] = jnp.where(code < width, code, width + place)
    valid = jnp.where(jnp.max(code, axis=0, keepdims=True) >= 0, 1.0, 0.0)
    entries = send_list[...]
    entries = jnp.concatenate(
        [entries, jnp.full((2, MAIN + TAIL - cap), -1, jnp.int32)], axis=1
    )
    one, two = entries[0:1], entries[1:2]
    one, two = jnp.where(is_down, one, two), jnp.where(is_down, two, one)
    late[...] = jnp.concatenate([one[:, MAIN:], two[:, MAIN:]], axis=1)
    main = jnp.concatenate([one[:, 0:MAIN], two[:, 0:MAIN]], axis=1)
    face = jnp.zeros_like(main)
    for f in range(1, 6):
        face = face + jnp.where(main >= f * width, 1, 0)
    faces[...] = face
    slots = main - face * width
    for s in chunks(2 * MAIN):
        picks[:, s] = onehot(slots[:, s], width)
    copies[2].wait()
    for lanes in chunks(width):
        mask = valid[:, lanes]
        now = [state[i, :, lanes] * mask for i in range(3)]
        for i in range(3):
            velocity[i, :, lanes] = now[i]
        vel_traces(traces, values, lanes, now, stage)
    pack(traces, values, picks, faces, late, send_one, send_two)
    copies[3].wait()
    for lanes in chunks(width):
        for i in range(6):
            stress[i, :, lanes] = state[3 + i, :, lanes] * valid[:, lanes]


def vel_local_kernel(
    step, velocity, stress, traces, recv, keys, lame, shear, vel, *rest,
):
    total = None
    *rest, scratch = rest
    clear_inner(scratch)
    near = halo_lhs(recv)
    if step < 0:
        stress_out, jump_out, hots, lame_scaled, shear_scaled = rest
    elif step == 0:
        hots, forward, stress_out, jump_out, total_out = rest
    else:
        hots, forward, total, stress_out, jump_out, total_out = rest
    width = velocity.shape[2]
    for lanes in chunks(width):
        if step < 0:
            for f in range(6):
                hots[f, :, lanes] = onehot(keys[f:f + 1, lanes] & (CHUNK - 1), CHUNK)
            lame_scaled[:, lanes] = (lift_half * time_step) * lame[:, lanes]
            shear_scaled[:, lanes] = (lift_half * time_step) * shear[:, lanes]
        plus = local_faces(traces, near, keys[:, lanes], hots, lanes, 1.0)
        grad, jump = lift_velocity(plus, scratch, lanes)
        count = holders(CHUNK)
        whole = []
        for i in range(3):
            now = velocity[i, :, lanes]
            high, low = split(now)
            got = mm(vel[...], jnp.concatenate([high, low, high], axis=0))
            whole.append([got[64 * j:64 * j + 64] + lift_half * grad[i][j] for j in range(3)])
            jump_out[i, :, lanes] = jump[i] - count * now
        rate = rate_of(whole, lame[:, lanes], shear[:, lanes])
        for m in range(6):
            stress_out[m, :, lanes] = stress[m, :, lanes] + time_step * rate[m]
        if step >= 0:
            term = rho_term(forward, step, velocity, lanes)
            total_out[:, lanes] = term if total is None else total[:, lanes] + term


def rho_term(forward, step, velocity, lanes):
    acc = forward[step, 0, :, lanes] * velocity[0, :, lanes]
    acc = acc + forward[step, 1, :, lanes] * velocity[1, :, lanes]
    acc = acc + forward[step, 2, :, lanes] * velocity[2, :, lanes]
    return -time_step * acc


def vel_halo_kernel(
    stress, jump, recv, keys, hots, picks, faces, late, lame_scaled, shear_scaled,
    stress_out, jump_out, traces, send_one, send_two, values, scratch, stage,
):
    width = stress.shape[2]
    clear_inner(scratch)
    lhs = halo_lhs(recv)
    for lanes in chunks(width):
        plus = halo_faces(lhs, keys[:, lanes], hots, lanes, width)
        grad, more = lift_velocity(plus, scratch, lanes)
        rate = rate_of(grad, lame_scaled[:, lanes], shear_scaled[:, lanes])
        now = [stress[m, :, lanes] + rate[m] for m in range(6)]
        for m in range(6):
            stress_out[m, :, lanes] = now[m]
        for i in range(3):
            jump_out[i, :, lanes] = jump[i, :, lanes] + more[i]
        str_traces(traces, values, lanes, now, stage)
    pack(traces, values, picks, faces, late, send_one, send_two)


def str_local_kernel(
    step, velocity, stress, jump, traces, recv, keys, hots, density, lame, shear, forward, div, fwd, *rest,
):
    *rest, scratch = rest
    clear_inner(scratch)
    near = halo_lhs(recv)
    if step == 0:
        total = None
        velocity_out, total_out, scale_out = rest
    else:
        total, velocity_out, total_out = rest
    width = velocity.shape[2]
    for lanes in chunks(width):
        plus = local_faces(traces, near, keys[:, lanes], hots, lanes, -1.0)
        lifted = lift_stress(plus, scratch, lanes)
        now = [stress[m, :, lanes] for m in range(6)]
        pieces = [split(s) for s in now]
        rho = density[:, lanes]
        impedance = jnp.sqrt(rho * (lame[:, lanes] + 2.0 * shear[:, lanes]))
        scale = time_step / rho
        if step == 0:
            scale_out[:, lanes] = lift_half * scale
        for i in range(3):
            rows = []
            for m in symmetric_index[i]:
                rows += [pieces[m][0], pieces[m][1], pieces[m][0]]
            got = mm(div[...], jnp.concatenate(rows, axis=0))
            velocity_out[i, :, lanes] = velocity[i, :, lanes] + scale * (
                got + lift_half * (lifted[i] + impedance * jump[i, :, lanes])
            )
        grad = []
        for i in range(3):
            high, low = split(forward[step, i, :, lanes])
            got = mm(fwd[...], jnp.concatenate([high, low, high], axis=0))
            grad.append([got[64 * j:64 * j + 64] for j in range(3)])
        diag = (grad[0][0], grad[1][1], grad[2][2])
        lame_term = -time_step * (diag[0] + diag[1] + diag[2]) * (now[0] + now[1] + now[2])
        shear_term = (-2.0 * time_step) * (
            diag[0] * now[0]
            + diag[1] * now[1]
            + diag[2] * now[2]
            + (grad[0][1] + grad[1][0]) * now[3]
            + (grad[0][2] + grad[2][0]) * now[4]
            + (grad[1][2] + grad[2][1]) * now[5]
        )
        for m, term in enumerate((lame_term, shear_term)):
            rows = total_out.shape[2]
            for e in range(total_out.shape[0]):
                share = term[rows * e:rows * e + rows]
                if total is not None:
                    share = total[e, m, :, lanes] + share
                total_out[e, m, :, lanes] = share


def str_halo_kernel(
    velocity, recv, keys, hots, picks, faces, late, scale,
    velocity_out, traces, send_one, send_two, values, scratch, stage,
):
    halo_velocity(
        velocity, recv, keys, hots, scale, velocity_out, traces, values, scratch, stage
    )
    pack(traces, values, picks, faces, late, send_one, send_two)


def last_kernel(
    step, velocity, recv, keys, hots, scale, forward, other, *rest
):
    *total, velocity_out, total_out, scratch, buffer, sems = rest
    total = total[0] if total else None
    rows = total_out.shape[2]
    copies = []

    def finish(lanes):
        copy = pltpu.make_async_copy(
            buffer.at[:, :, lanes], velocity_out.at[:, :, lanes], sems.at[len(copies)]
        )
        copy.start()
        copies.append(copy)
        term = rho_term(forward, step, buffer, lanes)
        if total is not None:
            term = total[:, lanes] + term
        for e in range(total_out.shape[0]):
            total_out[e, 0, :, lanes] = term[rows * e:rows * e + rows]
            for m in range(2):
                total_out[e, m + 1, :, lanes] = other[e, m, :, lanes]

    halo_velocity(
        velocity, recv, keys, hots, scale, buffer, None, None, scratch, None, finish
    )
    for copy in copies:
        copy.wait()


def event_sum_kernel(parts, out):
    width = parts.shape[3]
    for m in range(3):
        total = parts[0, m]
        for e in range(1, parts.shape[0]):
            total = total + parts[e, m]
        for k in range(total.shape[0]):
            out[m, :, k * width:(k + 1) * width] = total[k:k + 1]


def halo_velocity(
    velocity, recv, keys, hots, scale, velocity_out, traces, values, scratch, stage,
    finish=None,
):
    width = velocity.shape[2]
    clear_inner(scratch)
    lhs = halo_lhs(recv)
    for lanes in chunks(width):
        plus = halo_faces(lhs, keys[:, lanes], hots, lanes, width)
        lifted = lift_stress(plus, scratch, lanes)
        now = [velocity[i, :, lanes] + scale[:, lanes] * lifted[i] for i in range(3)]
        for i in range(3):
            velocity_out[i, :, lanes] = now[i]
        if traces is not None:
            vel_traces(traces, values, lanes, now, stage)
        if finish is not None:
            finish(lanes)


def call(name, kernel, args, outs, specs=None, cost=0, scratch=(), out_specs=None):
    whole = pl.BlockSpec(memory_space=pltpu.VMEM)
    specs = specs or {}
    return pl.pallas_call(
        kernel,
        name=name,
        in_specs=[specs.get(k, whole) for k in range(len(args))],
        out_specs=out_specs or [whole] * len(outs),
        out_shape=[jax.ShapeDtypeStruct(s, d) for s, d in outs],
        scratch_shapes=list(scratch),
        compiler_params=pltpu.CompilerParams(vmem_limit_bytes=VMEM_LIMIT),
        cost_estimate=pl.CostEstimate(flops=cost, bytes_accessed=6_000_000, transcendentals=0),
    )(*args)


def swap(sent, axis):
    count = lax.axis_size(axis)
    got = []
    for first, value in enumerate(sent):
        pairs = []
        for low in range(first, count - 1, 2):
            pairs += [(low, low + 1), (low + 1, low)]
        got.append(lax.ppermute(value, axis, pairs))
    return got


def local(
    adjoint_state, forward_velocity, density, lame_lambda, shear_modulus, neighbour, send_list
):
    width = density.shape[1]
    steps = forward_velocity.shape[1]
    table = {k: jnp.asarray(v) for k, v in tables().items()}
    state = adjoint_state[0]
    forward = forward_velocity[0]
    down = (lax.axis_index("dom") % 2).astype(jnp.int32).reshape(1)

    nodal = pltpu.VMEM((3, width // 128, 64, 128), f32)
    values = pltpu.VMEM((288, width), f32)
    field = ((64, width), f32)
    vector = ((3, 64, width), f32)
    tensor = ((6, 64, width), f32)
    count = lax.axis_size("event")
    shares = count if 64 % (8 * count) == 0 else 1
    two = ((shares, 2, 64 // shares, width), f32)
    three = ((shares, 3, 64 // shares, width), f32)
    trace = ((576, width), bf16)
    hot = ((6, CHUNK, width), bf16)
    sends = [((SEND_ROWS, 128), f32)] * 2
    lists = [((6, width), jnp.int32), ((width, 2 * MAIN), bf16),
             ((1, 2 * MAIN), jnp.int32), ((1, 2 * TAIL), jnp.int32)]

    velocity, stress, keys, picks, faces, late, traces, *sent = call(
        "start", start_kernel,
        (down, *(pltpu.with_memory_space_constraint(x, pltpu.HBM)
                for x in (state, neighbour, send_list))),
        [vector, tensor] + lists + [trace] + sends,
        specs={0: pl.BlockSpec(memory_space=pltpu.SMEM)}
        | {k: pl.BlockSpec(memory_space=pltpu.HBM) for k in range(1, 4)},
        scratch=[
            pltpu.VMEM(state.shape, f32), pltpu.VMEM(neighbour.shape, jnp.int32),
            pltpu.VMEM(send_list.shape, jnp.int32), values, nodal, pltpu.SemaphoreType.DMA((4,)),
        ],
    )
    rho_total = other_total = hots = None
    for n in range(steps):
        first, recv = swap(sent, "dom")
        args = [velocity, stress, traces, first, keys, lame_lambda, shear_modulus,
                table["vel"]]
        outs = [tensor, vector]
        if n:
            args += [hots, forward] + ([rho_total] if n > 1 else [])
            outs += [field]
        else:
            outs += [hot, field, field]
        stress, jump, *more = call(
            "vel_local", functools.partial(vel_local_kernel, n - 1), args, outs, cost=4_000_000_000,
            scratch=[nodal],
        )
        if n:
            rho_total, = more
        else:
            hots, lame_scaled, shear_scaled = more
        stress, jump, traces, *sent = call(
            "vel_halo", vel_halo_kernel,
            (stress, jump, recv, keys, hots, picks, faces, late, lame_scaled, shear_scaled),
            [tensor, vector, trace] + sends, scratch=[values, nodal, nodal],
        )
        first, recv = swap(sent, "dom")
        args = [velocity, stress, jump, traces, first, keys, hots, density, lame_lambda, shear_modulus,
                forward, table["div"], table["fwd"]]
        if n:
            args += [other_total]
        velocity, other_total, *more = call(
            "str_local", functools.partial(str_local_kernel, n), args,
            [vector, two] + ([] if n else [field]), cost=4_000_000_000, scratch=[nodal],
        )
        if not n:
            scale, = more
        if n < steps - 1:
            velocity, traces, *sent = call(
                "str_halo", str_halo_kernel,
                (velocity, recv, keys, hots, picks, faces, late, scale),
                [vector, trace] + sends, scratch=[values, nodal, nodal],
            )
        else:
            velocity, kernel_total = call(
                "last", functools.partial(last_kernel, n),
                (velocity, recv, keys, hots, scale, forward, other_total)
                + ((rho_total,) if n else ()),
                [vector, three],
                scratch=[
                    nodal, pltpu.VMEM((3, 64, width), f32),
                    pltpu.SemaphoreType.DMA((width // CHUNK,)),
                ],
                out_specs=[
                    pl.BlockSpec(memory_space=pl.ANY), pl.BlockSpec(memory_space=pltpu.VMEM)
                ],
            )

    if shares == count:
        parts = lax.all_to_all(kernel_total, "event", 0, 0, tiled=True)
        kernels, = call(
            "event_sum", event_sum_kernel, (parts,), [((3, 1, 64 // count * width), f32)]
        )
    else:
        flat = kernel_total.reshape(3, -1)
        part = lax.psum_scatter(flat, "event", scatter_dimension=1, tiled=True)
        kernels = part.reshape(3, 1, -1)
    return velocity[None], kernels


def solution(mesh):
    placed = (
        P("event", None, None, "dom"),
        P("event", None, None, None, "dom"),
        P(None, "dom"),
        P(None, "dom"),
        P(None, "dom"),
        P(None, "dom"),
        P(None, "dom"),
    )
    return jax.shard_map(
        local,
        mesh=mesh,
        in_specs=placed,
        out_specs=(P("event", None, None, "dom"), P(None, "dom", "event")),
        check_vma=False,
    )
```
